128 devices in a mesh: row: 8 (over z, core), col: 16 (over y, x).
Axes of the slice: x: 4, y: 4, z: 4, core: 2. Of those that a mesh axis runs over, the one named last changes fastest.
Arguments:
- trail_cov: float32 [16384, 16384], P('row', 'col')
- panel_two_rows: float32 [16384, 512], P('row'), may hold values from -0.046875 to 0.046875
- diag_inv_two: float32 [512, 512], replicated
- panel_one_top: float32 [512, 512], replicated, may hold values from -0.25 to 0.25
- panel_one_rows: float32 [16384, 512], P('row'), may hold values from -0.046875 to 0.046875
- diag_inv_one: float32 [512, 512], replicated
- pattern_two: int32 [128], replicated, may hold values 0 or 1
- pattern_one: int32 [132], replicated, may hold values from 0 to 1, as said below
- loadings: bfloat16 [262144, 256], P(('row', 'col')), may hold values from -0.5 to 0.5
- unit_block: int32 [262144, 1], P(('row', 'col')), may hold values from 0 to 127; in each aligned block of 2048 rows (0 to 2047, 2048 to 4095, ...) at most 32 rows name the same one
- block_panel: int32 [128], replicated, may hold values from 0 to 3
- counts: int32 [262144], P(('row', 'col')), may hold values from 0 to 31
- shape_par: float32 [262144], P(('row', 'col')), may hold values from 0.5 to 5
- exposure: float32 [262144], P(('row', 'col')), may hold values from 0.2 to 5
Outputs:
- cov_two: float32 [16384, 512], P(('row', 'col'))
- top_cov: float32 [512, 512], replicated
- cov_one: float32 [16384, 512], P(('row', 'col'))
- diag_two: float32 [512, 512], replicated
- diag_one: float32 [512, 512], replicated
- shape_grad: float32 [262144], P(('row', 'col'))
The draws below stay inside these ranges and needn't reach their ends.
Inputs may be any that keep to these rules, and one draw needn't show every extreme that they name: `unit_block`: among the histories of one device, no trailing block is named by more than 32 of them, and some block by exactly 32. `pattern_one`: at least one of the first 4 entries is 1.
All inputs are finite; a program needn't handle non-finite values.
Results may differ from the reference program's by a relative error of at most 0.0003.
Values may be sent and summed in bfloat16 or wider, within the bound.
No kernel may reach another device: no remote copies, remote signals or barrier semaphores. Data moves between devices by JAX's collectives and lax.ppermute only.
A program may use at most 192 MiB of HBM per device.

```python
import math
import jax
import jax.numpy as jnp
import numpy as np
from jax import lax

BLK = 128
PANEL = 512
U_DEV = 2048
NBLK = 128
TRAIL = 16384
PB = 4
UNITS = 262144
CAP = 32
N_ROW = 8
N_COL = 16


def triangle(raw, key):
    lower = jnp.arange(PANEL)[:, None] > jnp.arange(PANEL)[None, :]
    same = jnp.arange(PANEL)[:, None] == jnp.arange(PANEL)[None, :]
    diag = jnp.exp(jax.random.uniform(key, (PANEL,), jnp.float32, 0.0, 0.5))
    below = jnp.where(lower, raw * (0.5 / math.sqrt(PANEL)), jnp.zeros_like(raw))
    return jnp.where(same, diag[:, None] * jnp.ones((1, PANEL), jnp.float32), below)


def draw_trail_cov(key, part):
    key = jax.random.fold_in(key, 11)
    key_off = jax.random.fold_in(key, 0)
    key_diag = jax.random.fold_in(key, 1)
    key_decay = jax.random.fold_in(key, 3)
    key_bump = jax.random.fold_in(key, 4)
    raw = jax.random.normal(key_off, (TRAIL, TRAIL), jnp.float32)
    off = (raw + raw.T) * (0.15 / math.sqrt(TRAIL))
    diag = jnp.exp(jax.random.uniform(key_diag, (TRAIL,), jnp.float32, 0.0, 0.7))
    position = jnp.arange(TRAIL, dtype=jnp.int32)
    same = position[:, None] == position[None, :]
    base = jnp.where(same, diag[:, None] * jnp.ones((1, TRAIL), jnp.float32), off)
    owner = position // BLK
    same_block = owner[:, None] == owner[None, :]
    log_decay = jnp.log(jax.random.uniform(key_decay, (NBLK,), jnp.float32, 0.75, 0.92))
    row_decay = log_decay[owner]
    bump = jnp.exp(jax.random.uniform(key_bump, (TRAIL,), jnp.float32, -0.35, 0.35))
    distance = jnp.abs(position[:, None] - position[None, :]).astype(jnp.float32)
    kernel = jnp.exp(row_decay[:, None] * distance) * bump[:, None] * bump[None, :]
    return base + jnp.where(same_block, kernel, jnp.zeros_like(kernel))


def draw_diag_inv_two(key, part):
    key = jax.random.fold_in(key, 21)
    key_raw, key_diag = jax.random.split(key)
    raw = jax.random.normal(key_raw, (PANEL, PANEL), jnp.float32)
    return triangle(raw, key_diag)


def draw_diag_inv_one(key, part):
    key = jax.random.fold_in(key, 31)
    key_raw, key_diag = jax.random.split(key)
    raw = jax.random.normal(key_raw, (PANEL, PANEL), jnp.float32)
    return triangle(raw, key_diag)


def draw_pattern_one(key, part):
    key = jax.random.fold_in(key, 41)
    key_bits, key_pick = jax.random.split(key)
    bits = jax.random.randint(key_bits, (PB + NBLK,), 0, 2, jnp.int32)
    pick = jax.random.randint(key_pick, (), 0, PB, jnp.int32)
    position = jnp.arange(PB + NBLK, dtype=jnp.int32)
    return jnp.where(position == pick, jnp.ones_like(bits), bits).astype(jnp.int32)


def with_ends(result, own_key, low, top_value):
    longest = result.shape.index(max(result.shape))
    spots = []
    for shift in (0, 1):
        where = [jax.random.randint(jax.random.fold_in(own_key, axis), (), 0, length) for axis, length in enumerate(result.shape)]
        where[longest] = (where[longest] + shift) % result.shape[longest]
        spots.append(tuple(where))
    return result.at[spots[0]].set(low).at[spots[1]].set(top_value)


def block_levels(own_key, extent, shards, least, largest):
    def one(axis_at, blocks):
        steps = jax.random.uniform(jax.random.fold_in(jax.random.fold_in(own_key, 6), axis_at), (blocks,), jnp.float32, least / len(shards), largest / len(shards))
        return jnp.repeat(jnp.exp(steps), extent[axis_at] // blocks).reshape((-1,) + (1,) * (len(extent) - axis_at - 1))

    gain = one(*shards[0])
    for cut in shards[1:]:
        gain = gain * one(*cut)
    return gain


def deal_out(key, own, number, rows, amount, top, limit, skew):
    ranking = jax.random.permutation(key, amount)
    packed, common = load_shares(amount, rows * top, limit, skew, True), load_shares(amount, rows * top, limit, skew, False)
    places = jnp.arange(amount)

    def named(lengths, offset_by):
        used = int((lengths > 0).sum())
        fixed = max(1, used // 4)
        passed = fixed + (places - fixed + offset_by * (used - fixed)) % max(1, amount - fixed)
        return jnp.zeros((amount,), jnp.int32).at[ranking[jnp.where(places < fixed, places, passed)]].set(jnp.asarray(lengths, jnp.int32))

    lengths = jnp.where(number % 4 == 0, named(packed, number // 4), named(common, number - number // 4 - 1))
    mixed = jax.random.permutation(jax.random.fold_in(own, 3), amount)
    giver, receiver = mixed[0:amount // 2 * 2:2], mixed[1:amount // 2 * 2:2]
    slack = jnp.minimum(lengths[giver] - 1, limit - lengths[receiver]) // 2
    slack = jnp.where((giver == ranking[0]) | (receiver == ranking[0]) | (lengths[receiver] == 0), 0, jnp.maximum(slack, 0))
    passed = jax.random.randint(jax.random.fold_in(own, 4), (amount // 2,), 0, 1 << 20) % (slack + 1)
    lengths = lengths.at[giver].add(-passed).at[receiver].add(passed)
    labels = jnp.searchsorted(jnp.cumsum(lengths), jnp.arange(rows * top), side="right").astype(jnp.int32)
    listing = labels.reshape(top, rows).T
    listing = listing[jax.random.permutation(jax.random.fold_in(own, 1), rows)]
    offset_by = jax.random.randint(jax.random.fold_in(own, 2), (rows, 1), 0, top)
    return jnp.take_along_axis(listing, (jnp.arange(top)[None, :] + offset_by) % top, axis=1)


def load_shares(count, total, limit, slope, full):
    portions = [(1 << 20) // math.isqrt(standing ** slope) + 1 for standing in range(1, count + 1)]
    largest = limit if full else min(limit, max(-(-total // count), total * portions[0] // sum(portions)))
    least = 1 if total - largest >= count - 1 else 0
    given, spare = [largest] + [least] * (count - 1), total - largest - least * (count - 1)
    while spare > 0:
        free = [i for i in range(1, count) if given[i] < largest] or [i for i in range(1, count) if given[i] < limit]
        mass, budget = sum([portions[i] for i in free]), spare
        for i in free:
            more = min(limit - given[i], max(1, budget * portions[i] // mass), spare)
            given[i] = given[i] + more
            spare = spare - more
    return np.array(given)


def centred(own_key, shape, scale, limit, pieces=(), held_as=jnp.bfloat16):
    entries = scale * jax.random.normal(own_key, shape, jnp.float32)
    if pieces:
        entries = entries * block_levels(own_key, shape, pieces, -0.22, 0.18)
    return jnp.clip(entries, -limit, limit).astype(held_as)


def setup_inputs(seed: int = 0) -> dict:
    arg_keys = jax.random.split(jax.random.key(seed), 15)
    trail_cov = draw_trail_cov(jax.random.fold_in(arg_keys[14], 71), 0)
    panel_two_rows = centred(arg_keys[1], (TRAIL, PANEL), TRAIL ** -0.5, 0.046875, ((0, 8),), jnp.float32)
    diag_inv_two = draw_diag_inv_two(jax.random.fold_in(arg_keys[14], 71), 0)
    panel_one_top = centred(arg_keys[3], (PANEL, PANEL), PANEL ** -0.5, 0.25, (), jnp.float32)
    panel_one_rows = centred(arg_keys[4], (TRAIL, PANEL), TRAIL ** -0.5, 0.046875, ((0, 8),), jnp.float32)
    diag_inv_one = draw_diag_inv_one(jax.random.fold_in(arg_keys[14], 71), 0)
    pattern_two = with_ends((jax.random.randint(arg_keys[6], (NBLK,), 0, 2) < 1).astype(jnp.int32), jax.random.fold_in(arg_keys[6], 1), 0, 1)
    pattern_one = draw_pattern_one(jax.random.fold_in(arg_keys[14], 71), 0)
    loadings = centred(arg_keys[8], (UNITS, 2 * BLK), 0.09, 0.5, ((0, 128),))
    unit_block_keys = jax.random.split(jax.random.fold_in(arg_keys[9], 1), UNITS // U_DEV)
    unit_block_turns = jax.random.permutation(jax.random.fold_in(arg_keys[9], 3), UNITS // U_DEV)
    unit_block = jax.vmap(lambda own, number: deal_out(jax.random.fold_in(arg_keys[9], 2), own, number, U_DEV, NBLK, 1, CAP, 1))(unit_block_keys, unit_block_turns).reshape((UNITS, 1))
    block_panel = with_ends(jax.random.randint(arg_keys[10], (NBLK,), 0, PB), jax.random.fold_in(arg_keys[10], 1), 0, PB - 1).astype(jnp.int32)
    counts = with_ends(jax.random.randint(arg_keys[11], (UNITS,), 0, 32), jax.random.fold_in(arg_keys[11], 1), 0, 31).astype(jnp.int32)
    shape_par = jnp.clip(jnp.exp(math.log(5.0) - 2.3025851 * jax.random.uniform(arg_keys[12], (UNITS,), jnp.float32) ** block_levels(arg_keys[12], (UNITS,), ((0, 128),), -0.2, 0.2)), 0.5, 5.0)
    exposure = jnp.clip(jnp.exp(math.log(5.0) - 3.218876 * jax.random.uniform(arg_keys[13], (UNITS,), jnp.float32) ** block_levels(arg_keys[13], (UNITS,), ((0, 128),), -0.2, 0.2)), 0.2, 5.0)
    return {"trail_cov": trail_cov, "panel_two_rows": panel_two_rows, "diag_inv_two": diag_inv_two, "panel_one_top": panel_one_top, "panel_one_rows": panel_one_rows, "diag_inv_one": diag_inv_one, "pattern_two": pattern_two, "pattern_one": pattern_one, "loadings": loadings, "unit_block": unit_block, "block_panel": block_panel, "counts": counts, "shape_par": shape_par, "exposure": exposure}


def product(left, right):
    return jnp.dot(left, right, precision=lax.Precision.HIGHEST, preferred_element_type=jnp.float32)


def expand(bits):
    return jnp.repeat(bits.astype(jnp.float32), BLK)[:, None]


def unit_variances(trail_cov, cov_one, diag_one, loadings, unit_block, block_panel):
    blocks = unit_block[:, 0].astype(jnp.int32)
    order = jnp.argsort(blocks, stable=True).astype(jnp.int32)
    tally = jnp.bincount(blocks, length=NBLK).astype(jnp.int32)
    starts = (jnp.cumsum(tally) - tally).astype(jnp.int32)
    most = CAP * N_ROW * N_COL
    padded = jnp.concatenate([order, jnp.zeros((most,), jnp.int32)])

    def one_block(block):
        index = lax.dynamic_slice(padded, (starts[block],), (most,))
        valid = jnp.arange(most, dtype=jnp.int32) < tally[block]
        rows = loadings[index].astype(jnp.float32)
        front = rows[:, :BLK]
        back = rows[:, BLK:]
        panel = block_panel[block].astype(jnp.int32)
        tile = lax.dynamic_slice(trail_cov, (block * BLK, block * BLK), (BLK, BLK))
        cross = lax.dynamic_slice(cov_one, (block * BLK, panel * BLK), (BLK, BLK))
        inner = lax.dynamic_slice(diag_one, (panel * BLK, panel * BLK), (BLK, BLK))
        value = jnp.sum(product(front, tile) * front, axis=1)
        value = value + 2.0 * jnp.sum(product(front, cross) * back, axis=1)
        value = value + jnp.sum(product(back, inner) * back, axis=1)
        return index, jnp.where(valid, value, jnp.zeros_like(value))

    indices, values = lax.map(one_block, jnp.arange(NBLK, dtype=jnp.int32))
    return jnp.zeros((UNITS,), jnp.float32).at[indices.reshape(-1)].add(values.reshape(-1))


def shape_terms(variance, counts, shape_par, exposure):
    mean = exposure * jnp.exp(0.5 * variance)
    seen = counts.astype(jnp.float32)
    total = shape_par + mean
    return lax.digamma(shape_par + seen) - lax.digamma(shape_par) + jnp.log(shape_par / total) + (mean - seen) / total


def reference(trail_cov, panel_two_rows, diag_inv_two, panel_one_top, panel_one_rows, diag_inv_one, pattern_two, pattern_one, loadings, unit_block, block_panel, counts, shape_par, exposure):
    mask_two = expand(pattern_two)
    mask_top = expand(pattern_one[:PB])
    mask_one = expand(pattern_one[PB:])
    norm_two = product(mask_two * panel_two_rows, diag_inv_two)
    norm_top = product(mask_top * panel_one_top, diag_inv_one)
    norm_one = product(mask_one * panel_one_rows, diag_inv_one)
    cov_two = -mask_two * product(trail_cov, norm_two)
    diag_two = product(diag_inv_two.T, diag_inv_two) - product(norm_two.T, cov_two)
    top_cov = -mask_top * (product(diag_two, norm_top) + product(cov_two.T, norm_one))
    cov_one = -mask_one * (product(cov_two, norm_top) + product(trail_cov, norm_one))
    diag_one = product(diag_inv_one.T, diag_inv_one) - product(norm_top.T, top_cov) - product(norm_one.T, cov_one)
    variance = unit_variances(trail_cov, cov_one, diag_one, loadings, unit_block, block_panel)
    shape_grad = shape_terms(variance, counts, shape_par, exposure)
    return cov_two, top_cov, cov_one, diag_two, diag_one, shape_grad
```

```python
import functools
import jax
import jax.numpy as jnp
from jax import lax
from jax.experimental import pallas as pl
from jax.experimental.pallas import tpu as pltpu
from jax.sharding import PartitionSpec as P

BOTH = ("row", "col")

LEVELS = 32700.0
STEPS = 64.0
TINY = 1e-33
ROOM = 56 * 1024 * 1024


def split(value):
    head = value.astype(jnp.bfloat16)
    return head, (value - head.astype(jnp.float32)).astype(jnp.bfloat16)


def dot(left, right):
    return jnp.dot(left, right, preferred_element_type=jnp.float32)


def tdot(left, right):
    return lax.dot_general(
        left, right, (((0,), (0,)), ((), ())), preferred_element_type=jnp.float32
    )


def product(left, right, form=dot):
    left_head, left_tail = split(left)
    right_head, right_tail = split(right)
    return form(left_head, right_head) + (form(left_head, right_tail) + form(left_tail, right_head))


def pack(code):
    half = code.shape[-1] // 2
    return code[..., :half] * 65536 + code[..., half:]


def unpack(word):
    low = lax.shift_right_arithmetic(lax.shift_left(word, 16), 16)
    high = lax.shift_right_arithmetic(word - low, 16)
    return jnp.concatenate([high, low], axis=-1).astype(jnp.float32)


def encode(value, out_ref, *at):
    rows = value.shape[0]
    largest = jnp.max(jnp.abs(value), axis=0, keepdims=True)
    step = jnp.ceil(jnp.log2(jnp.maximum(largest, TINY)) * STEPS)
    code = jnp.round(value * (jnp.exp2(step * (-1.0 / STEPS)) * LEVELS))
    code = jnp.clip(code, -32767.0, 32767.0).astype(jnp.int32)
    out_ref[(*at, pl.ds(0, rows), slice(None))] = pack(code)
    head = pack(step.astype(jnp.int32))
    out_ref[(*at, pl.ds(rows, 8), slice(None))] = jnp.broadcast_to(head, (8, head.shape[1]))


def decode(word):
    rows = word.shape[0] - 8
    scale = jnp.exp2(unpack(word[rows : rows + 1]) * (1.0 / STEPS)) * (1.0 / LEVELS)
    return unpack(word[:rows]) * scale


def share_kernel(at_ref, two_ref, one_ref, inv_two_ref, inv_one_ref, out_ref):
    for i, (rows, inv) in enumerate(((two_ref, inv_two_ref), (one_ref, inv_one_ref))):
        keep = at_ref[1 + i].astype(jnp.float32)
        encode(product(keep * rows[...], inv[...]), out_ref, i)


def share(at, panel_two, panel_one, inv_two, inv_one, bw):
    width = inv_two.shape[0]
    rows = pl.BlockSpec((bw, width), lambda i, at: (at[0], 0))
    whole = pl.BlockSpec((width, width), lambda i, at: (0, 0))
    return pl.pallas_call(
        share_kernel,
        out_shape=jax.ShapeDtypeStruct((2, bw + 8, width // 2), jnp.int32),
        grid_spec=pltpu.PrefetchScalarGridSpec(
            num_scalar_prefetch=1,
            grid=(1,),
            in_specs=[rows, rows, whole, whole],
            out_specs=pl.BlockSpec((2, bw + 8, width // 2), lambda i, at: (0, 0, 0)),
        ),
        compiler_params=pltpu.CompilerParams(vmem_limit_bytes=ROOM),
    )(at, panel_two, panel_one, inv_two, inv_one)


def image_kernel(panel, bw, pieces, at_ref, cov_ref, *refs):
    held, (image_ref, code_ref, head_ref, tail_ref) = refs[:pieces], refs[pieces:]

    @pl.when(pl.program_id(0) == 0)
    def _():
        for i, ref in enumerate(held):
            head, tail = split(decode(ref[panel]))
            rows = pl.ds(pl.multiple_of(at_ref[i] * bw, bw), bw)
            head_ref[rows, :] = head
            tail_ref[rows, :] = tail

    cov_head, cov_tail = split(cov_ref[...])
    image = dot(cov_head, head_ref[...]) + (
        dot(cov_head, tail_ref[...]) + dot(cov_tail, head_ref[...])
    )
    image_ref[...] = image
    for i in range(image.shape[0] // bw):
        encode(image[i * bw : (i + 1) * bw], code_ref, i)


def image(at, trail_cov, held, panel, bw, tile=256):
    rows, span = trail_cov.shape
    width = 2 * held[0].shape[-1]
    every = pl.BlockSpec(held[0].shape, lambda i, at: (0, 0, 0))
    return pl.pallas_call(
        functools.partial(image_kernel, panel, bw, len(held)),
        out_shape=[
            jax.ShapeDtypeStruct((rows, width), jnp.float32),
            jax.ShapeDtypeStruct((rows // bw, bw + 8, width // 2), jnp.int32),
        ],
        grid_spec=pltpu.PrefetchScalarGridSpec(
            num_scalar_prefetch=1,
            grid=(rows // tile,),
            in_specs=[pl.BlockSpec((tile, span), lambda i, at: (i, 0))] + [every] * len(held),
            out_specs=[
                pl.BlockSpec((tile, width), lambda i, at: (i, 0)),
                pl.BlockSpec((tile // bw, bw + 8, width // 2), lambda i, at: (i, 0, 0)),
            ],
            scratch_shapes=[pltpu.VMEM((span, width), jnp.bfloat16)] * 2,
        ),
        compiler_params=pltpu.CompilerParams(vmem_limit_bytes=ROOM),
        cost_estimate=pl.CostEstimate(
            flops=6 * rows * span * width, bytes_accessed=4 * rows * (span + width), transcendentals=0
        ),
    )(at, trail_cov, *held)


def sums_kernel(
    bw, bits_two_ref, bits_one_ref, two_ref, one_ref, image_two_ref, image_one_ref,
    inv_two_ref, inv_one_ref, out_ref,
):
    step = pl.program_id(0)

    @pl.when(step == 0)
    def _():
        out_ref[...] = jnp.zeros_like(out_ref)

    count = two_ref.shape[0] // bw

    def masked(ref, bits_ref):
        keep = [
            jnp.full((bw, 1), bits_ref[step * count + i].astype(jnp.float32)) for i in range(count)
        ]
        keep = jnp.concatenate(keep, axis=0)
        return ref[...] * keep, keep

    two, keep_two = masked(two_ref, bits_two_ref)
    one, _ = masked(one_ref, bits_one_ref)
    image_two = split(image_two_ref[...] * keep_two)
    image_one = split(image_one_ref[...])
    two, one = split(two), split(one)
    for i, (left, right) in enumerate(((two, image_two), (one, image_two), (one, image_one))):
        out_ref[i] += tdot(left[0], right[0]) + (tdot(left[0], right[1]) + tdot(left[1], right[0]))

    @pl.when(step == pl.num_programs(0) - 1)
    def _():
        for i, inv in enumerate((inv_two_ref, inv_one_ref, inv_one_ref)):
            out_ref[i] = product(inv[...], out_ref[i], tdot)


def sums(bits_two, bits_one, panel_two, panel_one, image_two, image_one, inv_two, inv_one, bw, tile=256):
    rows, width = panel_two.shape
    part = pl.BlockSpec((tile, width), lambda i, *_: (i, 0))
    whole = pl.BlockSpec((width, width), lambda i, *_: (0, 0))
    return pl.pallas_call(
        functools.partial(sums_kernel, bw),
        out_shape=jax.ShapeDtypeStruct((3, width, width), jnp.float32),
        grid_spec=pltpu.PrefetchScalarGridSpec(
            num_scalar_prefetch=2,
            grid=(rows // tile,),
            in_specs=[part] * 4 + [whole] * 2,
            out_specs=pl.BlockSpec((3, width, width), lambda i, *_: (0, 0, 0)),
        ),
        compiler_params=pltpu.CompilerParams(vmem_limit_bytes=ROOM),
        cost_estimate=pl.CostEstimate(
            flops=18 * rows * width * width, bytes_accessed=16 * rows * width, transcendentals=0
        ),
    )(bits_two, bits_one, panel_two, panel_one, image_two, image_one, inv_two, inv_one)


def rows_kernel(at_ref, two_ref, one_ref, top_ref, cov_two_ref, cov_one_ref, cross_ref):
    count = two_ref.shape[0]

    def total(ref):
        value = decode(ref[0])
        for i in range(1, count):
            value = value + decode(ref[i])
        return value

    cov_two = -at_ref[0].astype(jnp.float32) * total(two_ref)
    cov_two_ref[...] = cov_two
    cov_one = -at_ref[1].astype(jnp.float32) * (product(cov_two, top_ref[...]) + total(one_ref))
    cov_one_ref[...] = cov_one
    bw = cross_ref.shape[1]
    cross_ref[...] = cov_one_ref[:, pl.ds(pl.multiple_of(at_ref[2] * bw, bw), bw)]


def rows(at, part_two, part_one, norm_top, bw):
    width = norm_top.shape[0]
    smem = pl.BlockSpec(memory_space=pltpu.SMEM)
    vmem = pl.BlockSpec(memory_space=pltpu.VMEM)
    return pl.pallas_call(
        rows_kernel,
        out_shape=[jax.ShapeDtypeStruct((bw, n), jnp.float32) for n in (width, width, bw)],
        in_specs=[smem, vmem, vmem, vmem],
        out_specs=[vmem] * 3,
        compiler_params=pltpu.CompilerParams(vmem_limit_bytes=ROOM),
    )(at, part_two, part_one, norm_top)


def small_kernel(at_ref, own_ref, other_ref, gram_ref, top_ref, keep_ref, two_ref, top_cov_ref, one_ref, sums_ref):
    y_count, lanes = own_ref.shape[2], own_ref.shape[-1]
    tall = own_ref.shape[-2]

    for flip, ref in enumerate((own_ref, other_ref)):
        half = lax.rem(at_ref[3] + flip, 2)
        for dz in range(4):
            z = lax.rem(at_ref[2] + 4 - dz, 4)
            for dx in range(4):
                x = lax.rem(at_ref[0] + 4 - dx, 4)
                row = ((half * 4 + z) * 4 + x) * tall
                for dy in range(y_count):
                    y = lax.rem(at_ref[1] + 4 - dy, 4)
                    sums_ref[
                        :,
                        pl.ds(pl.multiple_of(row, tall), tall),
                        pl.ds(pl.multiple_of(y * lanes, lanes), lanes),
                    ] = ref[dz, dx, dy]
    top = top_ref[...]
    two = gram_ref[0] + sums_ref[0]
    two_ref[...] = two
    mixed = sums_ref[1]
    keep = jnp.concatenate(
        [
            jnp.full((top.shape[0] // 4, 1), keep_ref[i].astype(jnp.float32)) for i in range(4)
        ],
        axis=0,
    )
    top_cov = -keep * (product(two, top) - mixed.T)
    top_cov_ref[...] = top_cov
    one_ref[...] = gram_ref[1] + sums_ref[2] - product(top, top_cov, tdot) - product(mixed, top)


def small(at, own, other, gram, norm_top, bits_top):
    width = norm_top.shape[0]
    smem = pl.BlockSpec(memory_space=pltpu.SMEM)
    vmem = pl.BlockSpec(memory_space=pltpu.VMEM)
    return pl.pallas_call(
        small_kernel,
        out_shape=[jax.ShapeDtypeStruct((width, width), jnp.float32)] * 3,
        in_specs=[smem, vmem, vmem, vmem, vmem, smem],
        out_specs=[vmem] * 3,
        scratch_shapes=[pltpu.VMEM((3, width, width), jnp.float32)],
        compiler_params=pltpu.CompilerParams(vmem_limit_bytes=ROOM),
    )(at, own, other, gram, norm_top, bits_top)


def early_kernel(keep_ref, top_rows_ref, inv_two_ref, inv_one_ref, gram_ref, top_ref):
    keep = jnp.concatenate(
        [
            jnp.full((top_rows_ref.shape[0] // 4, 1), keep_ref[i].astype(jnp.float32))
            for i in range(4)
        ],
        axis=0,
    )
    top_ref[...] = product(keep * top_rows_ref[...], inv_one_ref[...])
    gram_ref[0] = product(inv_two_ref[...], inv_two_ref[...], tdot)
    gram_ref[1] = product(inv_one_ref[...], inv_one_ref[...], tdot)


def early(bits_top, panel_top, inv_two, inv_one):
    width = inv_two.shape[0]
    smem = pl.BlockSpec(memory_space=pltpu.SMEM)
    vmem = pl.BlockSpec(memory_space=pltpu.VMEM)
    return pl.pallas_call(
        early_kernel,
        out_shape=[
            jax.ShapeDtypeStruct((2, width, width), jnp.float32),
            jax.ShapeDtypeStruct((width, width), jnp.float32),
        ],
        in_specs=[smem, vmem, vmem, vmem],
        out_specs=[vmem] * 2,
        compiler_params=pltpu.CompilerParams(vmem_limit_bytes=ROOM),
    )(bits_top, panel_top, inv_two, inv_one)


def row_sums(value):
    ones = jnp.ones((8, value.shape[1]), jnp.bfloat16)
    head, tail = split(value)
    form = (((1,), (1,)), ((), ()))
    return lax.dot_general(
        ones, head, form, preferred_element_type=jnp.float32
    ) + lax.dot_general(ones, tail, form, preferred_element_type=jnp.float32)


def forms_kernel(units_ref, tile_ref, cross_ref, out_ref):
    bw = tile_ref.shape[0]
    front, back = units_ref[:, :bw], units_ref[:, bw:]
    middle = jnp.concatenate([*split(tile_ref[...]), *split(2.0 * cross_ref[...])], axis=1)
    both = dot(front, middle)
    value = (both[:, :bw] + both[:, bw : 2 * bw]) * front.astype(jnp.float32)
    value = value + (both[:, 2 * bw : 3 * bw] + both[:, 3 * bw :]) * back.astype(jnp.float32)
    out_ref[...] = row_sums(value)


def forms(units, tile, cross, step=1024):
    count, bw = units.shape[0], tile.shape[0]
    whole = pl.BlockSpec((bw, bw), lambda i: (0, 0))
    return pl.pallas_call(
        forms_kernel,
        out_shape=jax.ShapeDtypeStruct((8, count), jnp.float32),
        grid=(count // step,),
        in_specs=[pl.BlockSpec((step, 2 * bw), lambda i: (i, 0)), whole, whole],
        out_specs=pl.BlockSpec((8, step), lambda i: (0, i)),
        compiler_params=pltpu.CompilerParams(vmem_limit_bytes=ROOM),
    )(units, tile, cross)


def inner_kernel(units_ref, panel_ref, diag_ref, out_ref):
    bw = units_ref.shape[1] // 2
    back = units_ref[:, bw:]
    count = diag_ref.shape[0] // bw
    value = jnp.zeros(back.shape, jnp.float32)
    for p in range(count):
        at = slice(p * bw, (p + 1) * bw)
        both = dot(back, jnp.concatenate(split(diag_ref[at, at]), axis=1))
        value = jnp.where(panel_ref[...] == p, both[:, :bw] + both[:, bw:], value)
    out_ref[...] = row_sums(value * back.astype(jnp.float32))


def inner(units, panel, diag, step=1024):
    count, width = units.shape
    return pl.pallas_call(
        inner_kernel,
        out_shape=jax.ShapeDtypeStruct((8, count), jnp.float32),
        grid=(count // step,),
        in_specs=[
            pl.BlockSpec((step, width), lambda i: (i, 0)),
            pl.BlockSpec((step, 1), lambda i: (i, 0)),
            pl.BlockSpec(diag.shape, lambda i: (0, 0)),
        ],
        out_specs=pl.BlockSpec((8, step), lambda i: (0, i)),
        compiler_params=pltpu.CompilerParams(vmem_limit_bytes=ROOM),
    )(units, panel, diag)


class Ring:
    def __init__(self, axis, size, stride, count=4):
        self.axis, self.size, self.stride, self.count = axis, size, stride, count

    def place(self):
        return lax.axis_index(self.axis) // self.stride % self.count

    def move(self, value, step):
        pairs = []
        for i in range(self.size):
            at = i // self.stride % self.count
            pairs.append((i, i + ((at + step) % self.count - at) * self.stride))
        return lax.ppermute(value, self.axis, pairs)

    def scatter_sum(self, value, axis):
        size = value.shape[axis] // self.count

        def take(step):
            at = (self.place() + step) % self.count * size
            return lax.dynamic_slice_in_dim(value, at, size, axis)

        parts = [self.move(take(step), step) for step in range(1, self.count)]
        total = take(0)
        for part in parts:
            total = total + part
        return total

    def gather(self, value):
        return jnp.stack([value] + [self.move(value, step) for step in range(1, self.count)])


def local(
    trail_cov,
    panel_two_rows,
    diag_inv_two,
    panel_one_top,
    panel_one_rows,
    diag_inv_one,
    pattern_two,
    pattern_one,
    loadings,
    unit_block,
    block_panel,
    counts,
    shape_par,
    exposure,
):
    row_count = lax.axis_size("row")
    col_count = lax.axis_size("col")
    total_count = row_count * col_count
    row_index = lax.axis_index("row")
    col_index = lax.axis_index("col")
    ratio = col_count // row_count
    width = diag_inv_two.shape[0]
    bw = loadings.shape[1] // 2
    top_blocks = width // bw
    owner = row_index * col_count + col_index
    core = Ring("row", row_count, 1, 2)
    ring_z = Ring("row", row_count, 2)
    ring_x = Ring("col", col_count, 1)
    ring_y = Ring("col", col_count, 4)

    bits_two = lax.dynamic_slice_in_dim(pattern_two, row_index * col_count, col_count)
    bits_top = pattern_one[:top_blocks]
    bits_one = lax.dynamic_slice_in_dim(
        pattern_one, top_blocks + row_index * col_count, col_count
    )
    own_two = lax.dynamic_index_in_dim(bits_two, col_index, 0, False)
    own_one = lax.dynamic_index_in_dim(bits_one, col_index, 0, False)

    part = share(
        jnp.stack([col_index, own_two, own_one]),
        panel_two_rows, panel_one_rows, diag_inv_two, diag_inv_one, bw,
    )
    moves = [(i, i % row_count * col_count + i // row_count) for i in range(total_count)]
    part = lax.ppermute(part, BOTH, moves)
    after, before = ring_z.move(part, 1), ring_z.move(part, -1)
    far = jnp.stack([ring_z.move(after[0], 1), ring_z.move(before[1], -1)])
    held, places = [], []
    for step, piece in ((0, part), (1, after), (-1, before), (2, far)):
        at = (ring_z.place() - step) % 4 * 2
        held += [piece, core.move(piece, 1)]
        places += [at + core.place(), at + 1 - core.place()]
    places = jnp.stack(places)

    blocks = unit_block[:, 0]
    capacity = 2 * loadings.shape[0] // total_count
    hits = (blocks[:, None] == jnp.arange(total_count, dtype=jnp.int32)[None, :]).astype(jnp.int32)
    rank = jnp.sum(jnp.cumsum(hits, axis=0) * hits, axis=1) - 1
    slot = blocks * capacity + rank
    packed = jnp.zeros((total_count * capacity, 2 * bw), jnp.bfloat16).at[slot].set(loadings)
    packed = packed.reshape(total_count, capacity, 2 * bw)
    units = lax.all_to_all(packed, BOTH, split_axis=0, concat_axis=0, tiled=True)
    units = units.reshape(total_count * capacity, 2 * bw)

    side = col_index % ratio
    tiles = jnp.stack(
        [
            lax.dynamic_slice(trail_cov, ((side * row_count + j) * bw, j * bw), (bw, bw))
            for j in range(row_count)
        ]
    )
    tiles = jnp.concatenate([jnp.where(side == h, tiles, 0.0) for h in range(ratio)])
    tiles = lax.all_to_all(tiles, "col", split_axis=0, concat_axis=0, tiled=True)
    tile = lax.dynamic_index_in_dim(
        tiles, row_index * ratio + col_index // row_count, 0, keepdims=False
    )

    gram, norm_top = early(bits_top, panel_one_top, diag_inv_two, diag_inv_one)

    image_two, code_two = image(places, trail_cov, held, 0, bw)
    code_two = lax.all_to_all(code_two, "col", split_axis=0, concat_axis=0, tiled=True)
    image_one, code_one = image(places, trail_cov, held, 1, bw)
    code_one = lax.all_to_all(code_one, "col", split_axis=0, concat_axis=0, tiled=True)

    total = sums(
        bits_two, bits_one, panel_two_rows, panel_one_rows, image_two, image_one,
        diag_inv_two, diag_inv_one, bw,
    )
    total = core.scatter_sum(total, 1)
    total = ring_z.scatter_sum(total, 1)
    total = ring_x.scatter_sum(total, 1)
    total = ring_y.scatter_sum(total, 2)
    total = ring_z.gather(ring_x.gather(ring_y.gather(total)))
    spots = jnp.stack([ring_x.place(), ring_y.place(), ring_z.place(), core.place()])
    diag_two, top_cov, diag_one = small(
        spots, total, core.move(total, 1), gram, norm_top, bits_top
    )

    cov_two, cov_one, cross = rows(
        jnp.stack([own_two, own_one, block_panel[owner]]), code_two, code_one, norm_top, bw
    )
    value = forms(units, tile, cross)[0].reshape(total_count, capacity)
    returned = lax.all_to_all(value, BOTH, split_axis=0, concat_axis=0, tiled=True)
    picked = jnp.dot(
        hits.astype(jnp.float32), returned, precision=lax.Precision.HIGHEST,
        preferred_element_type=jnp.float32,
    )
    at_rank = rank[:, None] == jnp.arange(capacity, dtype=jnp.int32)[None, :]
    variance = jnp.sum(jnp.where(at_rank, picked, 0.0), axis=1)
    own_panel = jnp.sum(hits * block_panel[None, :], axis=1, keepdims=True)
    variance = variance + inner(loadings, own_panel, diag_one)[0]

    mean = exposure * jnp.exp(0.5 * variance)
    seen = counts.astype(jnp.float32)
    scale = shape_par + mean
    shape_grad = (
        lax.digamma(shape_par + seen)
        - lax.digamma(shape_par)
        + jnp.log(shape_par / scale)
        + (mean - seen) / scale
    )
    return (cov_two, top_cov, cov_one, diag_two, diag_one, shape_grad)


def solution(mesh):
    in_specs = (
        P("row", "col"),
        P("row", None),
        P(),
        P(),
        P("row", None),
        P(),
        P(),
        P(),
        P(("row", "col"), None),
        P(("row", "col"), None),
        P(),
        P(("row", "col")),
        P(("row", "col")),
        P(("row", "col")),
    )
    out_specs = (P(("row", "col"), None), P(), P(("row", "col"), None), P(), P(), P(("row", "col")))
    return jax.shard_map(local, mesh=mesh, in_specs=in_specs, out_specs=out_specs, check_vma=False)
```

```python
import functools
import jax
import jax.numpy as jnp
from jax import lax
from jax.experimental import pallas as pl
from jax.experimental.pallas import tpu as pltpu
from jax.sharding import PartitionSpec as P

BOTH = ("row", "col")

LEVELS = 32700.0
STEPS = 64.0
TINY = 1e-33
ROOM = 56 * 1024 * 1024
LIGHT = pl.CostEstimate(flops=1, bytes_accessed=1, transcendentals=0)


def split(value):
    head = value.astype(jnp.bfloat16)
    return head, (value - head.astype(jnp.float32)).astype(jnp.bfloat16)


def dot(left, right):
    return jnp.dot(left, right, preferred_element_type=jnp.float32)


def tdot(left, right):
    return lax.dot_general(
        left, right, (((0,), (0,)), ((), ())), preferred_element_type=jnp.float32
    )


def product(left, right, form=dot):
    left_head, left_tail = split(left)
    right_head, right_tail = split(right)
    return form(left_head, right_head) + (form(left_head, right_tail) + form(left_tail, right_head))


def pack(code):
    half = code.shape[-1] // 2
    return code[..., :half] * 65536 + code[..., half:]


def unpack(word):
    low = lax.shift_right_arithmetic(lax.shift_left(word, 16), 16)
    high = lax.shift_right_arithmetic(word - low, 16)
    return jnp.concatenate([high, low], axis=-1).astype(jnp.float32)


def encode(value, out_ref, *at):
    rows = value.shape[0]
    largest = jnp.max(jnp.abs(value), axis=0, keepdims=True)
    step = jnp.ceil(jnp.log2(jnp.maximum(largest, TINY)) * STEPS)
    code = jnp.round(value * (jnp.exp2(step * (-1.0 / STEPS)) * LEVELS))
    code = jnp.clip(code, -32767.0, 32767.0).astype(jnp.int32)
    out_ref[(*at, pl.ds(0, rows), slice(None))] = pack(code)
    head = pack(step.astype(jnp.int32))
    out_ref[(*at, pl.ds(rows, 8), slice(None))] = jnp.broadcast_to(head, (8, head.shape[1]))


def decode(word):
    rows = word.shape[0] - 8
    scale = jnp.exp2(unpack(word[rows : rows + 1]) * (1.0 / STEPS)) * (1.0 / LEVELS)
    return unpack(word[:rows]) * scale


def share_kernel(at_ref, two_ref, one_ref, inv_two_ref, inv_one_ref, out_ref):
    for i, (rows, inv) in enumerate(((two_ref, inv_two_ref), (one_ref, inv_one_ref))):
        keep = at_ref[1 + i].astype(jnp.float32)
        encode(product(keep * rows[...], inv[...]), out_ref, i)


def share(at, panel_two, panel_one, inv_two, inv_one, bw):
    width = inv_two.shape[0]
    rows = pl.BlockSpec((bw, width), lambda i, at: (at[0], 0))
    whole = pl.BlockSpec((width, width), lambda i, at: (0, 0))
    return pl.pallas_call(
        share_kernel,
        out_shape=jax.ShapeDtypeStruct((2, bw + 8, width // 2), jnp.int32),
        grid_spec=pltpu.PrefetchScalarGridSpec(
            num_scalar_prefetch=1,
            grid=(1,),
            in_specs=[rows, rows, whole, whole],
            out_specs=pl.BlockSpec((2, bw + 8, width // 2), lambda i, at: (0, 0, 0)),
        ),
        compiler_params=pltpu.CompilerParams(vmem_limit_bytes=ROOM),
    )(at, panel_two, panel_one, inv_two, inv_one)


def image_kernel(panel, bw, pieces, at_ref, cov_ref, *refs):
    held, (image_ref, code_ref, head_ref, tail_ref) = refs[:pieces], refs[pieces:]

    @pl.when(pl.program_id(0) == 0)
    def _():
        for i, ref in enumerate(held):
            head, tail = split(decode(ref[panel]))
            rows = pl.ds(pl.multiple_of(at_ref[i] * bw, bw), bw)
            head_ref[rows, :] = head
            tail_ref[rows, :] = tail

    cov_head, cov_tail = split(cov_ref[...])
    image = dot(cov_head, head_ref[...]) + (
        dot(cov_head, tail_ref[...]) + dot(cov_tail, head_ref[...])
    )
    image_ref[...] = image
    for i in range(image.shape[0] // bw):
        encode(image[i * bw : (i + 1) * bw], code_ref, i)


def image(at, trail_cov, held, panel, bw, tile=512):
    rows, span = trail_cov.shape
    width = 2 * held[0].shape[-1]
    every = pl.BlockSpec(held[0].shape, lambda i, at: (0, 0, 0))
    return pl.pallas_call(
        functools.partial(image_kernel, panel, bw, len(held)),
        out_shape=[
            jax.ShapeDtypeStruct((rows, width), jnp.float32),
            jax.ShapeDtypeStruct((rows // bw, bw + 8, width // 2), jnp.int32),
        ],
        grid_spec=pltpu.PrefetchScalarGridSpec(
            num_scalar_prefetch=1,
            grid=(rows // tile,),
            in_specs=[pl.BlockSpec((tile, span), lambda i, at: (i, 0))] + [every] * len(held),
            out_specs=[
                pl.BlockSpec((tile, width), lambda i, at: (i, 0)),
                pl.BlockSpec((tile // bw, bw + 8, width // 2), lambda i, at: (i, 0, 0)),
            ],
            scratch_shapes=[pltpu.VMEM((span, width), jnp.bfloat16)] * 2,
        ),
        compiler_params=pltpu.CompilerParams(vmem_limit_bytes=ROOM),
        cost_estimate=LIGHT,
    )(at, trail_cov, *held)


def sums_kernel(
    bw, bits_two_ref, bits_one_ref, two_ref, one_ref, image_two_ref, image_one_ref,
    inv_two_ref, inv_one_ref, out_ref,
):
    step = pl.program_id(0)

    @pl.when(step == 0)
    def _():
        out_ref[...] = jnp.zeros_like(out_ref)

    count = two_ref.shape[0] // bw

    def masked(ref, bits_ref):
        keep = [
            jnp.full((bw, 1), bits_ref[step * count + i].astype(jnp.float32)) for i in range(count)
        ]
        keep = jnp.concatenate(keep, axis=0)
        return ref[...] * keep, keep

    two, keep_two = masked(two_ref, bits_two_ref)
    one, _ = masked(one_ref, bits_one_ref)
    image_two = split(image_two_ref[...] * keep_two)
    image_one = split(image_one_ref[...])
    two, one = split(two), split(one)
    for i, (left, right) in enumerate(((two, image_two), (one, image_two), (one, image_one))):
        out_ref[i] += tdot(left[0], right[0]) + (tdot(left[0], right[1]) + tdot(left[1], right[0]))

    @pl.when(step == pl.num_programs(0) - 1)
    def _():
        for i, inv in enumerate((inv_two_ref, inv_one_ref, inv_one_ref)):
            out_ref[i] = product(inv[...], out_ref[i], tdot)


def sums(bits_two, bits_one, panel_two, panel_one, image_two, image_one, inv_two, inv_one, bw, tile=512):
    rows, width = panel_two.shape
    part = pl.BlockSpec((tile, width), lambda i, *_: (i, 0))
    whole = pl.BlockSpec((width, width), lambda i, *_: (0, 0))
    return pl.pallas_call(
        functools.partial(sums_kernel, bw),
        out_shape=jax.ShapeDtypeStruct((3, width, width), jnp.float32),
        grid_spec=pltpu.PrefetchScalarGridSpec(
            num_scalar_prefetch=2,
            grid=(rows // tile,),
            in_specs=[part] * 4 + [whole] * 2,
            out_specs=pl.BlockSpec((3, width, width), lambda i, *_: (0, 0, 0)),
        ),
        compiler_params=pltpu.CompilerParams(vmem_limit_bytes=ROOM),
        cost_estimate=LIGHT,
    )(bits_two, bits_one, panel_two, panel_one, image_two, image_one, inv_two, inv_one)


def rows_kernel(at_ref, two_ref, one_ref, top_ref, cov_two_ref, cov_one_ref, cross_ref):
    count = two_ref.shape[0]

    def total(ref):
        value = decode(ref[0])
        for i in range(1, count):
            value = value + decode(ref[i])
        return value

    cov_two = -at_ref[0].astype(jnp.float32) * total(two_ref)
    cov_two_ref[...] = cov_two
    cov_one = -at_ref[1].astype(jnp.float32) * (product(cov_two, top_ref[...]) + total(one_ref))
    cov_one_ref[...] = cov_one
    bw = cross_ref.shape[1]
    cross_ref[...] = cov_one_ref[:, pl.ds(pl.multiple_of(at_ref[2] * bw, bw), bw)]


def rows(at, part_two, part_one, norm_top, bw):
    width = norm_top.shape[0]
    smem = pl.BlockSpec(memory_space=pltpu.SMEM)
    vmem = pl.BlockSpec(memory_space=pltpu.VMEM)
    return pl.pallas_call(
        rows_kernel,
        out_shape=[jax.ShapeDtypeStruct((bw, n), jnp.float32) for n in (width, width, bw)],
        in_specs=[smem, vmem, vmem, vmem],
        out_specs=[vmem] * 3,
        compiler_params=pltpu.CompilerParams(vmem_limit_bytes=ROOM),
    )(at, part_two, part_one, norm_top)


def small_kernel(at_ref, own_ref, other_ref, gram_ref, top_ref, keep_ref, two_ref, top_cov_ref, one_ref, sums_ref):
    y_count, lanes = own_ref.shape[2], own_ref.shape[-1]
    tall = own_ref.shape[-2]

    for flip, ref in enumerate((own_ref, other_ref)):
        half = lax.rem(at_ref[3] + flip, 2)
        for dz in range(4):
            z = lax.rem(at_ref[2] + 4 - dz, 4)
            for dx in range(4):
                x = lax.rem(at_ref[0] + 4 - dx, 4)
                row = ((half * 4 + z) * 4 + x) * tall
                for dy in range(y_count):
                    y = lax.rem(at_ref[1] + 4 - dy, 4)
                    sums_ref[
                        :,
                        pl.ds(pl.multiple_of(row, tall), tall),
                        pl.ds(pl.multiple_of(y * lanes, lanes), lanes),
                    ] = ref[dz, dx, dy]
    top = top_ref[...]
    two = gram_ref[0] + sums_ref[0]
    two_ref[...] = two
    mixed = sums_ref[1]
    keep = jnp.concatenate(
        [
            jnp.full((top.shape[0] // 4, 1), keep_ref[i].astype(jnp.float32)) for i in range(4)
        ],
        axis=0,
    )
    top_cov = -keep * (product(two, top) - mixed.T)
    top_cov_ref[...] = top_cov
    one_ref[...] = gram_ref[1] + sums_ref[2] - product(top, top_cov, tdot) - product(mixed, top)


def small(at, own, other, gram, norm_top, bits_top):
    width = norm_top.shape[0]
    smem = pl.BlockSpec(memory_space=pltpu.SMEM)
    vmem = pl.BlockSpec(memory_space=pltpu.VMEM)
    return pl.pallas_call(
        small_kernel,
        out_shape=[jax.ShapeDtypeStruct((width, width), jnp.float32)] * 3,
        in_specs=[smem, vmem, vmem, vmem, vmem, smem],
        out_specs=[vmem] * 3,
        scratch_shapes=[pltpu.VMEM((3, width, width), jnp.float32)],
        compiler_params=pltpu.CompilerParams(vmem_limit_bytes=ROOM),
    )(at, own, other, gram, norm_top, bits_top)


def early_kernel(keep_ref, top_rows_ref, inv_two_ref, inv_one_ref, gram_ref, top_ref):
    keep = jnp.concatenate(
        [
            jnp.full((top_rows_ref.shape[0] // 4, 1), keep_ref[i].astype(jnp.float32))
            for i in range(4)
        ],
        axis=0,
    )
    top_ref[...] = product(keep * top_rows_ref[...], inv_one_ref[...])
    gram_ref[0] = product(inv_two_ref[...], inv_two_ref[...], tdot)
    gram_ref[1] = product(inv_one_ref[...], inv_one_ref[...], tdot)


def early(bits_top, panel_top, inv_two, inv_one):
    width = inv_two.shape[0]
    smem = pl.BlockSpec(memory_space=pltpu.SMEM)
    vmem = pl.BlockSpec(memory_space=pltpu.VMEM)
    return pl.pallas_call(
        early_kernel,
        out_shape=[
            jax.ShapeDtypeStruct((2, width, width), jnp.float32),
            jax.ShapeDtypeStruct((width, width), jnp.float32),
        ],
        in_specs=[smem, vmem, vmem, vmem],
        out_specs=[vmem] * 2,
        compiler_params=pltpu.CompilerParams(vmem_limit_bytes=ROOM),
    )(bits_top, panel_top, inv_two, inv_one)


def row_sums(value):
    ones = jnp.ones((8, value.shape[1]), jnp.bfloat16)
    head, tail = split(value)
    form = (((1,), (1,)), ((), ()))
    return lax.dot_general(
        ones, head, form, preferred_element_type=jnp.float32
    ) + lax.dot_general(ones, tail, form, preferred_element_type=jnp.float32)


def forms_kernel(units_ref, tile_ref, cross_ref, out_ref):
    bw = tile_ref.shape[0]
    front, back = units_ref[:, :bw], units_ref[:, bw:]
    middle = jnp.concatenate([*split(tile_ref[...]), *split(2.0 * cross_ref[...])], axis=1)
    both = dot(front, middle)
    value = (both[:, :bw] + both[:, bw : 2 * bw]) * front.astype(jnp.float32)
    value = value + (both[:, 2 * bw : 3 * bw] + both[:, 3 * bw :]) * back.astype(jnp.float32)
    out_ref[...] = row_sums(value)


def forms(units, tile, cross, step=1024):
    count, bw = units.shape[0], tile.shape[0]
    whole = pl.BlockSpec((bw, bw), lambda i: (0, 0))
    return pl.pallas_call(
        forms_kernel,
        out_shape=jax.ShapeDtypeStruct((8, count), jnp.float32),
        grid=(count // step,),
        in_specs=[pl.BlockSpec((step, 2 * bw), lambda i: (i, 0)), whole, whole],
        out_specs=pl.BlockSpec((8, step), lambda i: (0, i)),
        compiler_params=pltpu.CompilerParams(vmem_limit_bytes=ROOM),
    )(units, tile, cross)


def inner_kernel(units_ref, panel_ref, diag_ref, out_ref):
    bw = units_ref.shape[1] // 2
    back = units_ref[:, bw:]
    count = diag_ref.shape[0] // bw
    value = jnp.zeros(back.shape, jnp.float32)
    for p in range(count):
        at = slice(p * bw, (p + 1) * bw)
        both = dot(back, jnp.concatenate(split(diag_ref[at, at]), axis=1))
        value = jnp.where(panel_ref[...] == p, both[:, :bw] + both[:, bw:], value)
    out_ref[...] = row_sums(value * back.astype(jnp.float32))


def inner(units, panel, diag, step=1024):
    count, width = units.shape
    return pl.pallas_call(
        inner_kernel,
        out_shape=jax.ShapeDtypeStruct((8, count), jnp.float32),
        grid=(count // step,),
        in_specs=[
            pl.BlockSpec((step, width), lambda i: (i, 0)),
            pl.BlockSpec((step, 1), lambda i: (i, 0)),
            pl.BlockSpec(diag.shape, lambda i: (0, 0)),
        ],
        out_specs=pl.BlockSpec((8, step), lambda i: (0, i)),
        compiler_params=pltpu.CompilerParams(vmem_limit_bytes=ROOM),
    )(units, panel, diag)


class Ring:
    def __init__(self, axis, size, stride, count=4):
        self.axis, self.size, self.stride, self.count = axis, size, stride, count

    def place(self):
        return lax.axis_index(self.axis) // self.stride % self.count

    def move(self, value, step):
        pairs = []
        for i in range(self.size):
            at = i // self.stride % self.count
            pairs.append((i, i + ((at + step) % self.count - at) * self.stride))
        return lax.ppermute(value, self.axis, pairs)

    def scatter_sum(self, value, axis):
        size = value.shape[axis] // self.count

        def take(step):
            at = (self.place() + step) % self.count * size
            return lax.dynamic_slice_in_dim(value, at, size, axis)

        parts = [self.move(take(step), step) for step in range(1, self.count)]
        total = take(0)
        for part in parts:
            total = total + part
        return total

    def gather(self, value):
        return jnp.stack([value] + [self.move(value, step) for step in range(1, self.count)])


def spread_plan(row_count, col_count):
    plan = []
    for r in range(row_count):
        z = r // 2
        first = col_count // row_count * r
        for c in range(col_count):
            x, y = c % 4, c // 4
            x_first = first % 4
            side = 0 if x in (x_first, (x_first - 1) % 4) else 1
            half = 0 if x in (x_first, (x_first + 1) % 4) else 1
            j = y % 4 * 2 + half
            plan.append((side * row_count + j, j * col_count + first + side))
    return plan


def local(
    trail_cov,
    panel_two_rows,
    diag_inv_two,
    panel_one_top,
    panel_one_rows,
    diag_inv_one,
    pattern_two,
    pattern_one,
    loadings,
    unit_block,
    block_panel,
    counts,
    shape_par,
    exposure,
):
    row_count = lax.axis_size("row")
    col_count = lax.axis_size("col")
    total_count = row_count * col_count
    row_index = lax.axis_index("row")
    col_index = lax.axis_index("col")
    ratio = col_count // row_count
    width = diag_inv_two.shape[0]
    bw = loadings.shape[1] // 2
    top_blocks = width // bw
    owner = row_index * col_count + col_index
    core = Ring("row", row_count, 1, 2)
    ring_z = Ring("row", row_count, 2)
    ring_x = Ring("col", col_count, 1)
    ring_y = Ring("col", col_count, 4)

    bits_two = lax.dynamic_slice_in_dim(pattern_two, row_index * col_count, col_count)
    bits_top = pattern_one[:top_blocks]
    bits_one = lax.dynamic_slice_in_dim(
        pattern_one, top_blocks + row_index * col_count, col_count
    )
    own_two = lax.dynamic_index_in_dim(bits_two, col_index, 0, False)
    own_one = lax.dynamic_index_in_dim(bits_one, col_index, 0, False)

    spread = spread_plan(row_count, col_count)
    chosen = jnp.array([block for block, _ in spread], jnp.int32)[owner]
    part = share(
        jnp.stack([chosen, bits_two[chosen], bits_one[chosen]]),
        panel_two_rows, panel_one_rows, diag_inv_two, diag_inv_one, bw,
    )
    blocks, side = unit_block[:, 0], col_index % ratio
    part, blocks, side = lax.optimization_barrier((part, blocks, side))
    part = lax.ppermute(part, BOTH, [(i, j) for i, (_, j) in enumerate(spread)])
    held, places = [], []
    for step in range(4):
        piece = ring_z.move(part, step) if step else part
        at = (ring_z.place() - step) % 4 * 2
        held += [piece, core.move(piece, 1)]
        places += [at + core.place(), at + 1 - core.place()]
    places = jnp.stack(places)

    tiles = jnp.stack(
        [
            lax.dynamic_slice(trail_cov, ((side * row_count + j) * bw, j * bw), (bw, bw))
            for j in range(row_count)
        ]
    )
    at = col_index % row_count
    pairs = [
        (r * col_count + ratio * r + h, r * col_count + h * row_count)
        for r in range(row_count)
        for h in range(ratio)
    ]
    tiles = lax.ppermute(tiles, BOTH, pairs)
    half = row_count // 2
    while half:
        pairs = [(c, c + half) for c in range(0, col_count, 2 * half)]
        handed = lax.ppermute(tiles[half:], "col", pairs)
        tiles = jnp.where(at // half % 2 == 1, handed, tiles[:half])
        half //= 2
    tile = tiles[0]

    capacity = 2 * loadings.shape[0] // total_count
    hits = (blocks[:, None] == jnp.arange(total_count, dtype=jnp.int32)[None, :]).astype(jnp.int32)
    rank = jnp.sum(jnp.cumsum(hits, axis=0) * hits, axis=1) - 1
    slot = blocks * capacity + rank
    packed = jnp.zeros((total_count * capacity, 2 * bw), jnp.bfloat16).at[slot].set(loadings)
    packed = packed.reshape(total_count, capacity, 2 * bw)
    packed, held[2] = lax.optimization_barrier((packed, held[2]))
    units = lax.all_to_all(packed, BOTH, split_axis=0, concat_axis=0, tiled=True)
    units = units.reshape(total_count * capacity, 2 * bw)

    gram, norm_top = early(bits_top, panel_one_top, diag_inv_two, diag_inv_one)
    places, norm_top = lax.optimization_barrier((places, norm_top))

    image_two, code_two = image(places, trail_cov, held, 0, bw)
    code_two, units = lax.optimization_barrier((code_two, units))
    code_two = lax.all_to_all(code_two, "col", split_axis=0, concat_axis=0, tiled=True)
    image_one, code_one = image(places, trail_cov, held, 1, bw)
    code_one, code_two = lax.optimization_barrier((code_one, code_two))
    code_one = lax.all_to_all(code_one, "col", split_axis=0, concat_axis=0, tiled=True)

    total = sums(
        bits_two, bits_one, panel_two_rows, panel_one_rows, image_two, image_one,
        diag_inv_two, diag_inv_one, bw,
    )
    total = core.scatter_sum(total, 1)
    total = ring_z.scatter_sum(total, 1)
    total = ring_x.scatter_sum(total, 1)
    total = ring_y.scatter_sum(total, 2)
    total, code_one = lax.optimization_barrier((total, code_one))
    total = ring_x.gather(ring_y.gather(total))
    cov_two, cov_one, cross = rows(
        jnp.stack([own_two, own_one, block_panel[owner]]), code_two, code_one, norm_top, bw
    )
    value = forms(units, tile, cross)[0].reshape(total_count, capacity)
    total, value = lax.optimization_barrier((total, value))
    returned = lax.all_to_all(value, BOTH, split_axis=0, concat_axis=0, tiled=True)
    total = ring_z.gather(total)
    total, returned = lax.optimization_barrier((total, returned))
    other = core.move(total, 1)
    spots = jnp.stack([ring_x.place(), ring_y.place(), ring_z.place(), core.place()])
    diag_two, top_cov, diag_one = small(spots, total, other, gram, norm_top, bits_top)
    picked = jnp.dot(
        hits.astype(jnp.float32), returned, precision=lax.Precision.HIGHEST,
        preferred_element_type=jnp.float32,
    )
    at_rank = rank[:, None] == jnp.arange(capacity, dtype=jnp.int32)[None, :]
    variance = jnp.sum(jnp.where(at_rank, picked, 0.0), axis=1)
    own_panel = jnp.sum(hits * block_panel[None, :], axis=1, keepdims=True)
    variance = variance + inner(loadings, own_panel, diag_one)[0]

    mean = exposure * jnp.exp(0.5 * variance)
    seen = counts.astype(jnp.float32)
    scale = shape_par + mean
    shape_grad = (
        lax.digamma(shape_par + seen)
        - lax.digamma(shape_par)
        + jnp.log(shape_par / scale)
        + (mean - seen) / scale
    )
    return (cov_two, top_cov, cov_one, diag_two, diag_one, shape_grad)


def solution(mesh):
    in_specs = (
        P("row", "col"),
        P("row", None),
        P(),
        P(),
        P("row", None),
        P(),
        P(),
        P(),
        P(("row", "col"), None),
        P(("row", "col"), None),
        P(),
        P(("row", "col")),
        P(("row", "col")),
        P(("row", "col")),
    )
    out_specs = (P(("row", "col"), None), P(), P(("row", "col"), None), P(), P(), P(("row", "col")))
    return jax.shard_map(local, mesh=mesh, in_specs=in_specs, out_specs=out_specs, check_vma=False)
```

```python
import functools
import jax
import jax.numpy as jnp
from jax import lax
from jax.experimental import pallas as pl
from jax.experimental.pallas import tpu as pltpu
from jax.sharding import PartitionSpec as P

BOTH = ("row", "col")

LEVELS = 32700.0
STEPS = 64.0
TINY = 1e-33
ROOM = 56 * 1024 * 1024
LIGHT = pl.CostEstimate(flops=1, bytes_accessed=1, transcendentals=0)


def split(value):
    head = value.astype(jnp.bfloat16)
    return head, (value - head.astype(jnp.float32)).astype(jnp.bfloat16)


def dot(left, right):
    return jnp.dot(left, right, preferred_element_type=jnp.float32)


def tdot(left, right):
    return lax.dot_general(
        left, right, (((0,), (0,)), ((), ())), preferred_element_type=jnp.float32
    )


def product(left, right, form=dot):
    left_head, left_tail = split(left)
    right_head, right_tail = split(right)
    return form(left_head, right_head) + (form(left_head, right_tail) + form(left_tail, right_head))


def pack(code):
    half = code.shape[-1] // 2
    return code[..., :half] * 65536 + code[..., half:]


def unpack(word):
    low = lax.shift_right_arithmetic(lax.shift_left(word, 16), 16)
    high = lax.shift_right_arithmetic(word - low, 16)
    return jnp.concatenate([high, low], axis=-1).astype(jnp.float32)


def encode(value, out_ref, *at):
    rows = value.shape[0]
    largest = jnp.max(jnp.abs(value), axis=0, keepdims=True)
    step = jnp.ceil(jnp.log2(jnp.maximum(largest, TINY)) * STEPS)
    code = jnp.round(value * (jnp.exp2(step * (-1.0 / STEPS)) * LEVELS))
    code = jnp.clip(code, -32767.0, 32767.0).astype(jnp.int32)
    out_ref[(*at, pl.ds(0, rows), slice(None))] = pack(code)
    head = pack(step.astype(jnp.int32))
    out_ref[(*at, pl.ds(rows, 8), slice(None))] = jnp.broadcast_to(head, (8, head.shape[1]))


def decode(word):
    rows = word.shape[0] - 8
    scale = jnp.exp2(unpack(word[rows : rows + 1]) * (1.0 / STEPS)) * (1.0 / LEVELS)
    return unpack(word[:rows]) * scale


def chosen(row, col):
    first = lax.rem(2 * row, 4)
    x, y = lax.rem(col, 4), col // 4
    here = (x == first) | (x == lax.rem(first + 3, 4))
    left = (x == first) | (x == first + 1)
    return jnp.where(here, 0, 8) + 2 * y + jnp.where(left, 0, 1)


def share_kernel(at_ref, bits_two_ref, bits_one_ref, two_ref, one_ref, inv_two_ref, inv_one_ref, out_ref):
    block = 16 * at_ref[0] + chosen(at_ref[0], at_ref[1])
    skip = bits_one_ref.shape[0] - bits_two_ref.shape[0]
    keep_two = bits_two_ref[block].astype(jnp.float32)
    keep_one = bits_one_ref[skip + block].astype(jnp.float32)
    encode(product(keep_two * two_ref[...], inv_two_ref[...]), out_ref, 0)
    encode(product(keep_one * one_ref[...], inv_one_ref[...]), out_ref, 1)


def share(at, bits_two, bits_one, panel_two, panel_one, inv_two, inv_one, bw):
    width = inv_two.shape[0]
    rows = pl.BlockSpec((bw, width), lambda i, at, *_: (chosen(at[0], at[1]), 0))
    whole = pl.BlockSpec((width, width), lambda i, *_: (0, 0))
    return pl.pallas_call(
        share_kernel,
        out_shape=jax.ShapeDtypeStruct((2, bw + 8, width // 2), jnp.int32),
        grid_spec=pltpu.PrefetchScalarGridSpec(
            num_scalar_prefetch=3,
            grid=(1,),
            in_specs=[rows, rows, whole, whole],
            out_specs=pl.BlockSpec((2, bw + 8, width // 2), lambda i, *_: (0, 0, 0)),
        ),
        compiler_params=pltpu.CompilerParams(vmem_limit_bytes=ROOM),
        cost_estimate=LIGHT,
    )(at, bits_two, bits_one, panel_two, panel_one, inv_two, inv_one)


def tiles_kernel(at_ref, tile_ref, out_ref):
    out_ref[0] = tile_ref[...]


def tiles_of(at, trail_cov, count, bw):
    return pl.pallas_call(
        tiles_kernel,
        out_shape=jax.ShapeDtypeStruct((count, bw, bw), jnp.float32),
        grid_spec=pltpu.PrefetchScalarGridSpec(
            num_scalar_prefetch=1,
            grid=(count,),
            in_specs=[pl.BlockSpec((bw, bw), lambda j, at: (lax.rem(at[1], 2) * count + j, j))],
            out_specs=pl.BlockSpec((1, bw, bw), lambda j, at: (j, 0, 0)),
        ),
        cost_estimate=LIGHT,
    )(at, trail_cov)


def image_kernel(bw, pieces, at_ref, cov_ref, *refs):
    held, (two_ref, one_ref, code_ref, head_ref, tail_ref) = refs[:pieces], refs[pieces:]
    width = two_ref.shape[1]

    @pl.when(pl.program_id(0) == 0)
    def _():
        z, core = at_ref[0] // 2, lax.rem(at_ref[0], 2)
        for i, ref in enumerate(held):
            block = lax.rem(z + 4 - i // 2, 4) * 2 + lax.rem(core + i, 2)
            rows = pl.ds(pl.multiple_of(block * bw, bw), bw)
            for panel in range(2):
                head, tail = split(decode(ref[panel]))
                head_ref[rows, panel * width : (panel + 1) * width] = head
                tail_ref[rows, panel * width : (panel + 1) * width] = tail

    cov_head, cov_tail = split(cov_ref[...])
    for panel, image_ref in enumerate((two_ref, one_ref)):
        at = slice(panel * width, (panel + 1) * width)
        image = dot(cov_head, head_ref[:, at]) + (
            dot(cov_head, tail_ref[:, at]) + dot(cov_tail, head_ref[:, at])
        )
        image_ref[...] = image
        for i in range(image.shape[0] // bw):
            encode(image[i * bw : (i + 1) * bw], code_ref, i, panel)


def image(at, trail_cov, held, bw, tile=512):
    rows, span = trail_cov.shape
    width = 2 * held[0].shape[-1]
    every = pl.BlockSpec(held[0].shape, lambda i, at: (0, 0, 0))
    return pl.pallas_call(
        functools.partial(image_kernel, bw, len(held)),
        out_shape=[jax.ShapeDtypeStruct((rows, width), jnp.float32)] * 2
        + [jax.ShapeDtypeStruct((rows // bw, 2, bw + 8, width // 2), jnp.int32)],
        grid_spec=pltpu.PrefetchScalarGridSpec(
            num_scalar_prefetch=1,
            grid=(rows // tile,),
            in_specs=[pl.BlockSpec((tile, span), lambda i, at: (i, 0))] + [every] * len(held),
            out_specs=[pl.BlockSpec((tile, width), lambda i, at: (i, 0))] * 2
            + [pl.BlockSpec((tile // bw, 2, bw + 8, width // 2), lambda i, at: (i, 0, 0, 0))],
            scratch_shapes=[pltpu.VMEM((span, 2 * width), jnp.bfloat16)] * 2,
        ),
        compiler_params=pltpu.CompilerParams(vmem_limit_bytes=ROOM),
        cost_estimate=LIGHT,
    )(at, trail_cov, *held)


def sums_kernel(
    bw, at_ref, bits_two_ref, bits_one_ref, two_ref, one_ref, image_two_ref, image_one_ref,
    inv_two_ref, inv_one_ref, out_ref,
):
    step = pl.program_id(0)

    @pl.when(step == 0)
    def _():
        out_ref[...] = jnp.zeros_like(out_ref)

    count = two_ref.shape[0] // bw
    first = 16 * at_ref[0] + step * count
    skip = bits_one_ref.shape[0] - bits_two_ref.shape[0]

    def masked(ref, bits_ref, base):
        keep = [
            jnp.full((bw, 1), bits_ref[base + i].astype(jnp.float32)) for i in range(count)
        ]
        keep = jnp.concatenate(keep, axis=0)
        return ref[...] * keep, keep

    two, keep_two = masked(two_ref, bits_two_ref, first)
    one, _ = masked(one_ref, bits_one_ref, skip + first)
    image_two = split(image_two_ref[...] * keep_two)
    image_one = split(image_one_ref[...])
    two, one = split(two), split(one)
    for i, (left, right) in enumerate(((two, image_two), (one, image_two), (one, image_one))):
        out_ref[i] += tdot(left[0], right[0]) + (tdot(left[0], right[1]) + tdot(left[1], right[0]))

    @pl.when(step == pl.num_programs(0) - 1)
    def _():
        for i, inv in enumerate((inv_two_ref, inv_one_ref, inv_one_ref)):
            out_ref[i] = product(inv[...], out_ref[i], tdot)


def sums(at, bits_two, bits_one, panel_two, panel_one, image_two, image_one, inv_two, inv_one, bw, tile=512):
    rows, width = panel_two.shape
    part = pl.BlockSpec((tile, width), lambda i, *_: (i, 0))
    whole = pl.BlockSpec((width, width), lambda i, *_: (0, 0))
    return pl.pallas_call(
        functools.partial(sums_kernel, bw),
        out_shape=jax.ShapeDtypeStruct((3, width, width), jnp.float32),
        grid_spec=pltpu.PrefetchScalarGridSpec(
            num_scalar_prefetch=3,
            grid=(rows // tile,),
            in_specs=[part] * 4 + [whole] * 2,
            out_specs=pl.BlockSpec((3, width, width), lambda i, *_: (0, 0, 0)),
        ),
        compiler_params=pltpu.CompilerParams(vmem_limit_bytes=ROOM),
        cost_estimate=LIGHT,
    )(at, bits_two, bits_one, panel_two, panel_one, image_two, image_one, inv_two, inv_one)


def rows_kernel(at_ref, bits_two_ref, bits_one_ref, panel_ref, code_ref, top_ref, cov_two_ref, cov_one_ref, cross_ref):
    count = code_ref.shape[0]
    block = 16 * at_ref[0] + at_ref[1]
    skip = bits_one_ref.shape[0] - bits_two_ref.shape[0]
    keep_two = bits_two_ref[block].astype(jnp.float32)
    keep_one = bits_one_ref[skip + block].astype(jnp.float32)

    def total(panel):
        value = decode(code_ref[0, panel])
        for i in range(1, count):
            value = value + decode(code_ref[i, panel])
        return value

    cov_two = -keep_two * total(0)
    cov_two_ref[...] = cov_two
    cov_one = -keep_one * (product(cov_two, top_ref[...]) + total(1))
    cov_one_ref[...] = cov_one
    bw = cross_ref.shape[1]
    cross_ref[...] = cov_one_ref[:, pl.ds(pl.multiple_of(panel_ref[block] * bw, bw), bw)]


def rows(at, bits_two, bits_one, panel, code, norm_top, bw):
    width = norm_top.shape[0]
    smem = pl.BlockSpec(memory_space=pltpu.SMEM)
    vmem = pl.BlockSpec(memory_space=pltpu.VMEM)
    return pl.pallas_call(
        rows_kernel,
        out_shape=[jax.ShapeDtypeStruct((bw, n), jnp.float32) for n in (width, width, bw)],
        in_specs=[smem] * 4 + [vmem] * 2,
        out_specs=[vmem] * 3,
        compiler_params=pltpu.CompilerParams(vmem_limit_bytes=ROOM),
        cost_estimate=LIGHT,
    )(at, bits_two, bits_one, panel, code, norm_top)


def small_kernel(at_ref, own_ref, other_ref, gram_ref, top_ref, keep_ref, two_ref, top_cov_ref, one_ref, sums_ref):
    y_count, lanes = own_ref.shape[2], own_ref.shape[-1]
    tall = own_ref.shape[-2]

    own_z, own_core = at_ref[0] // 2, lax.rem(at_ref[0], 2)
    own_x, own_y = lax.rem(at_ref[1], 4), at_ref[1] // 4
    for flip, ref in enumerate((own_ref, other_ref)):
        half = lax.rem(own_core + flip, 2)
        for dz in range(4):
            z = lax.rem(own_z + 4 - dz, 4)
            for dx in range(4):
                x = lax.rem(own_x + 4 - dx, 4)
                row = ((half * 4 + z) * 4 + x) * tall
                for dy in range(y_count):
                    y = lax.rem(own_y + 4 - dy, 4)
                    sums_ref[
                        :,
                        pl.ds(pl.multiple_of(row, tall), tall),
                        pl.ds(pl.multiple_of(y * lanes, lanes), lanes),
                    ] = ref[dz, dx, dy]
    top = top_ref[...]
    two = gram_ref[0] + sums_ref[0]
    two_ref[...] = two
    mixed = sums_ref[1]
    keep = jnp.concatenate(
        [
            jnp.full((top.shape[0] // 4, 1), keep_ref[i].astype(jnp.float32)) for i in range(4)
        ],
        axis=0,
    )
    top_cov = -keep * (product(two, top) - mixed.T)
    top_cov_ref[...] = top_cov
    one_ref[...] = gram_ref[1] + sums_ref[2] - product(top, top_cov, tdot) - product(mixed, top)


def small(at, own, other, gram, norm_top, bits_top):
    width = norm_top.shape[0]
    smem = pl.BlockSpec(memory_space=pltpu.SMEM)
    vmem = pl.BlockSpec(memory_space=pltpu.VMEM)
    return pl.pallas_call(
        small_kernel,
        out_shape=[jax.ShapeDtypeStruct((width, width), jnp.float32)] * 3,
        in_specs=[smem, vmem, vmem, vmem, vmem, smem],
        out_specs=[vmem] * 3,
        scratch_shapes=[pltpu.VMEM((3, width, width), jnp.float32)],
        compiler_params=pltpu.CompilerParams(vmem_limit_bytes=ROOM),
        cost_estimate=LIGHT,
    )(at, own, other, gram, norm_top, bits_top)


def early_kernel(keep_ref, top_rows_ref, inv_two_ref, inv_one_ref, gram_ref, top_ref):
    keep = jnp.concatenate(
        [
            jnp.full((top_rows_ref.shape[0] // 4, 1), keep_ref[i].astype(jnp.float32))
            for i in range(4)
        ],
        axis=0,
    )
    top_ref[...] = product(keep * top_rows_ref[...], inv_one_ref[...])
    gram_ref[0] = product(inv_two_ref[...], inv_two_ref[...], tdot)
    gram_ref[1] = product(inv_one_ref[...], inv_one_ref[...], tdot)


def early(bits_top, panel_top, inv_two, inv_one):
    width = inv_two.shape[0]
    smem = pl.BlockSpec(memory_space=pltpu.SMEM)
    vmem = pl.BlockSpec(memory_space=pltpu.VMEM)
    return pl.pallas_call(
        early_kernel,
        out_shape=[
            jax.ShapeDtypeStruct((2, width, width), jnp.float32),
            jax.ShapeDtypeStruct((width, width), jnp.float32),
        ],
        in_specs=[smem, vmem, vmem, vmem],
        out_specs=[vmem] * 2,
        compiler_params=pltpu.CompilerParams(vmem_limit_bytes=ROOM),
        cost_estimate=LIGHT,
    )(bits_top, panel_top, inv_two, inv_one)


def row_sums(value):
    ones = jnp.ones((8, value.shape[1]), jnp.bfloat16)
    head, tail = split(value)
    form = (((1,), (1,)), ((), ()))
    return lax.dot_general(
        ones, head, form, preferred_element_type=jnp.float32
    ) + lax.dot_general(ones, tail, form, preferred_element_type=jnp.float32)


def forms_kernel(units_ref, tile_ref, cross_ref, out_ref):
    bw = tile_ref.shape[0]
    front, back = units_ref[:, :bw], units_ref[:, bw:]
    middle = jnp.concatenate([*split(tile_ref[...]), *split(2.0 * cross_ref[...])], axis=1)
    both = dot(front, middle)
    value = (both[:, :bw] + both[:, bw : 2 * bw]) * front.astype(jnp.float32)
    value = value + (both[:, 2 * bw : 3 * bw] + both[:, 3 * bw :]) * back.astype(jnp.float32)
    out_ref[...] = row_sums(value)


def forms(units, tile, cross, step=1024):
    count, bw = units.shape[0], tile.shape[0]
    whole = pl.BlockSpec((bw, bw), lambda i: (0, 0))
    return pl.pallas_call(
        forms_kernel,
        out_shape=jax.ShapeDtypeStruct((8, count), jnp.float32),
        grid=(count // step,),
        in_specs=[pl.BlockSpec((step, 2 * bw), lambda i: (i, 0)), whole, whole],
        out_specs=pl.BlockSpec((8, step), lambda i: (0, i)),
        compiler_params=pltpu.CompilerParams(vmem_limit_bytes=ROOM),
        cost_estimate=LIGHT,
    )(units, tile, cross)


def inner_kernel(units_ref, panel_ref, diag_ref, out_ref):
    bw = units_ref.shape[1] // 2
    back = units_ref[:, bw:]
    count = diag_ref.shape[0] // bw
    value = jnp.zeros(back.shape, jnp.float32)
    for p in range(count):
        at = slice(p * bw, (p + 1) * bw)
        both = dot(back, jnp.concatenate(split(diag_ref[at, at]), axis=1))
        value = jnp.where(panel_ref[...] == p, both[:, :bw] + both[:, bw:], value)
    out_ref[...] = row_sums(value * back.astype(jnp.float32))


def inner(units, panel, diag, step=1024):
    count, width = units.shape
    return pl.pallas_call(
        inner_kernel,
        out_shape=jax.ShapeDtypeStruct((8, count), jnp.float32),
        grid=(count // step,),
        in_specs=[
            pl.BlockSpec((step, width), lambda i: (i, 0)),
            pl.BlockSpec((step, 1), lambda i: (i, 0)),
            pl.BlockSpec(diag.shape, lambda i: (0, 0)),
        ],
        out_specs=pl.BlockSpec((8, step), lambda i: (0, i)),
        compiler_params=pltpu.CompilerParams(vmem_limit_bytes=ROOM),
        cost_estimate=LIGHT,
    )(units, panel, diag)


class Ring:
    def __init__(self, axis, size, stride, count=4):
        self.axis, self.size, self.stride, self.count = axis, size, stride, count

    def place(self):
        return lax.axis_index(self.axis) // self.stride % self.count

    def move(self, value, step):
        pairs = []
        for i in range(self.size):
            at = i // self.stride % self.count
            pairs.append((i, i + ((at + step) % self.count - at) * self.stride))
        return lax.ppermute(value, self.axis, pairs)

    def scatter_sum(self, value, axis):
        size = value.shape[axis] // self.count

        def take(step):
            at = (self.place() + step) % self.count * size
            return lax.dynamic_slice_in_dim(value, at, size, axis)

        parts = [self.move(take(step), step) for step in range(1, self.count)]
        total = take(0)
        for part in parts:
            total = total + part
        return total

    def gather(self, value):
        return jnp.stack([value] + [self.move(value, step) for step in range(1, self.count)])


def spread_pairs(row_count, col_count):
    pairs = []
    for r in range(row_count):
        for c in range(col_count):
            first, x, y = 2 * r % 4, c % 4, c // 4
            side = 0 if x in (first, (first + 3) % 4) else 1
            j = 2 * y + (0 if x in (first, first + 1) else 1)
            pairs.append((r * col_count + c, j * col_count + 2 * r + side))
    return pairs


def local(
    trail_cov,
    panel_two_rows,
    diag_inv_two,
    panel_one_top,
    panel_one_rows,
    diag_inv_one,
    pattern_two,
    pattern_one,
    loadings,
    unit_block,
    block_panel,
    counts,
    shape_par,
    exposure,
):
    row_count = lax.axis_size("row")
    col_count = lax.axis_size("col")
    total_count = row_count * col_count
    row_index = lax.axis_index("row")
    col_index = lax.axis_index("col")
    ratio = col_count // row_count
    width = diag_inv_two.shape[0]
    bw = loadings.shape[1] // 2
    top_blocks = width // bw
    core = Ring("row", row_count, 1, 2)
    ring_z = Ring("row", row_count, 2)
    ring_x = Ring("col", col_count, 1)
    ring_y = Ring("col", col_count, 4)

    at = jnp.stack([row_index, col_index]).astype(jnp.int32)
    bits_top = pattern_one[:top_blocks]

    part = share(
        at, pattern_two, pattern_one, panel_two_rows, panel_one_rows, diag_inv_two, diag_inv_one, bw
    )
    blocks = unit_block[:, 0]
    part, blocks = lax.optimization_barrier((part, blocks))
    part = lax.ppermute(part, BOTH, spread_pairs(row_count, col_count))
    held = []
    for step in range(4):
        piece = ring_z.move(part, step) if step else part
        held += [piece, core.move(piece, 1)]

    tiles = tiles_of(at, trail_cov, row_count, bw)
    turn = col_index % row_count
    pairs = [
        (r * col_count + ratio * r + h, r * col_count + h * row_count)
        for r in range(row_count)
        for h in range(ratio)
    ]
    tiles = lax.ppermute(tiles, BOTH, pairs)
    half = row_count // 2
    while half:
        pairs = [(c, c + half) for c in range(0, col_count, 2 * half)]
        handed = lax.ppermute(tiles[half:], "col", pairs)
        tiles = jnp.where(turn // half % 2 == 1, handed, tiles[:half])
        half //= 2
    tile = tiles[0]

    capacity = 2 * loadings.shape[0] // total_count
    hits = (blocks[:, None] == jnp.arange(total_count, dtype=jnp.int32)[None, :]).astype(jnp.int32)
    rank = jnp.sum(jnp.cumsum(hits, axis=0) * hits, axis=1) - 1
    slot = blocks * capacity + rank
    packed = jnp.zeros((total_count * capacity, 2 * bw), jnp.bfloat16).at[slot].set(loadings)
    packed = packed.reshape(total_count, capacity, 2 * bw)
    packed, held[2], held[4], held[6] = lax.optimization_barrier((packed, held[2], held[4], held[6]))
    units = lax.all_to_all(packed, BOTH, split_axis=0, concat_axis=0, tiled=True)
    units = units.reshape(total_count * capacity, 2 * bw)

    image_two, image_one, code = image(at, trail_cov, held, bw)
    code, units = lax.optimization_barrier((code, units))
    code = lax.all_to_all(code, "col", split_axis=0, concat_axis=0, tiled=True)

    total = sums(
        at, pattern_two, pattern_one, panel_two_rows, panel_one_rows, image_two, image_one,
        diag_inv_two, diag_inv_one, bw,
    )
    bits_top, total = lax.optimization_barrier((bits_top, total))
    gram, norm_top = early(bits_top, panel_one_top, diag_inv_two, diag_inv_one)
    total = core.scatter_sum(total, 1)
    total = ring_z.scatter_sum(total, 1)
    total, norm_top = lax.optimization_barrier((total, norm_top))
    total = ring_x.scatter_sum(total, 1)
    total = ring_y.scatter_sum(total, 2)
    total, tile = lax.optimization_barrier((total, tile))
    total = ring_y.gather(total)
    total = ring_x.gather(total)
    total, code = lax.optimization_barrier((total, code))
    total = ring_z.gather(total)
    cov_two, cov_one, cross = rows(
        at, pattern_two, pattern_one, block_panel, code, norm_top, bw
    )
    value = forms(units, tile, cross)[0].reshape(total_count, capacity)
    returned = lax.all_to_all(value, BOTH, split_axis=0, concat_axis=0, tiled=True)
    other = core.move(total, 1)
    diag_two, top_cov, diag_one = small(at, total, other, gram, norm_top, bits_top)
    own_panel = jnp.sum(hits * block_panel[None, :], axis=1, keepdims=True)
    within = inner(loadings, own_panel, diag_one)[0]
    within, returned = lax.optimization_barrier((within, returned))
    picked = jnp.dot(
        hits.astype(jnp.float32), returned, precision=lax.Precision.HIGHEST,
        preferred_element_type=jnp.float32,
    )
    at_rank = rank[:, None] == jnp.arange(capacity, dtype=jnp.int32)[None, :]
    variance = jnp.sum(jnp.where(at_rank, picked, 0.0), axis=1)
    variance = variance + within

    mean = exposure * jnp.exp(0.5 * variance)
    seen = counts.astype(jnp.float32)
    scale = shape_par + mean
    shape_grad = (
        lax.digamma(shape_par + seen)
        - lax.digamma(shape_par)
        + jnp.log(shape_par / scale)
        + (mean - seen) / scale
    )
    return (cov_two, top_cov, cov_one, diag_two, diag_one, shape_grad)


def solution(mesh):
    in_specs = (
        P("row", "col"),
        P("row", None),
        P(),
        P(),
        P("row", None),
        P(),
        P(),
        P(),
        P(("row", "col"), None),
        P(("row", "col"), None),
        P(),
        P(("row", "col")),
        P(("row", "col")),
        P(("row", "col")),
    )
    out_specs = (P(("row", "col"), None), P(), P(("row", "col"), None), P(), P(), P(("row", "col")))
    return jax.shard_map(local, mesh=mesh, in_specs=in_specs, out_specs=out_specs, check_vma=False)
```

```python
import functools
import jax
import jax.numpy as jnp
from jax import lax
from jax.experimental import pallas as pl
from jax.experimental.pallas import tpu as pltpu
from jax.sharding import PartitionSpec as P

BOTH = ("row", "col")

LEVELS = 32700.0
STEPS = 64.0
TINY = 1e-33
ROOM = 56 * 1024 * 1024
LIGHT = pl.CostEstimate(flops=1, bytes_accessed=1, transcendentals=0)


def split(value):
    head = value.astype(jnp.bfloat16)
    return head, (value - head.astype(jnp.float32)).astype(jnp.bfloat16)


def dot(left, right):
    return jnp.dot(left, right, preferred_element_type=jnp.float32)


def tdot(left, right):
    return lax.dot_general(
        left, right, (((0,), (0,)), ((), ())), preferred_element_type=jnp.float32
    )


def product(left, right, form=dot):
    left_head, left_tail = split(left)
    right_head, right_tail = split(right)
    return form(left_head, right_head) + (form(left_head, right_tail) + form(left_tail, right_head))


def pack(code):
    half = code.shape[-1] // 2
    return code[..., :half] * 65536 + code[..., half:]


def unpack(word):
    low = lax.shift_right_arithmetic(lax.shift_left(word, 16), 16)
    high = lax.shift_right_arithmetic(word - low, 16)
    return jnp.concatenate([high, low], axis=-1).astype(jnp.float32)


def encode(value, out_ref, *at, first=0):
    rows = value.shape[0]
    largest = jnp.max(jnp.abs(value), axis=0, keepdims=True)
    step = jnp.ceil(jnp.log2(jnp.maximum(largest, TINY)) * STEPS)
    code = jnp.round(value * (jnp.exp2(step * (-1.0 / STEPS)) * LEVELS))
    code = jnp.clip(code, -32767.0, 32767.0).astype(jnp.int32)
    out_ref[(*at, pl.ds(first, rows), slice(None))] = pack(code)
    head = pack(step.astype(jnp.int32))
    out_ref[(*at, pl.ds(first + rows, 8), slice(None))] = jnp.broadcast_to(head, (8, head.shape[1]))


def decode(word):
    rows = word.shape[0] - 8
    scale = jnp.exp2(unpack(word[rows : rows + 1]) * (1.0 / STEPS)) * (1.0 / LEVELS)
    return unpack(word[:rows]) * scale


def chosen(row, col):
    first = lax.rem(2 * row, 4)
    x, y = lax.rem(col, 4), col // 4
    here = (x == first) | (x == lax.rem(first + 3, 4))
    left = (x == first) | (x == first + 1)
    return jnp.where(here, 0, 8) + 2 * y + jnp.where(left, 0, 1)


def share_kernel(at_ref, bits_two_ref, bits_one_ref, two_ref, one_ref, inv_two_ref, inv_one_ref, out_ref):
    block = 16 * at_ref[0] + chosen(at_ref[0], at_ref[1])
    skip = bits_one_ref.shape[0] - bits_two_ref.shape[0]
    keep_two = bits_two_ref[block].astype(jnp.float32)
    keep_one = bits_one_ref[skip + block].astype(jnp.float32)
    encode(product(keep_two * two_ref[...], inv_two_ref[...]), out_ref, 0)
    encode(product(keep_one * one_ref[...], inv_one_ref[...]), out_ref, 1)


def share(at, bits_two, bits_one, panel_two, panel_one, inv_two, inv_one, bw):
    width = inv_two.shape[0]
    rows = pl.BlockSpec((bw, width), lambda i, at, *_: (chosen(at[0], at[1]), 0))
    whole = pl.BlockSpec((width, width), lambda i, *_: (0, 0))
    return pl.pallas_call(
        share_kernel,
        out_shape=jax.ShapeDtypeStruct((2, bw + 8, width // 2), jnp.int32),
        grid_spec=pltpu.PrefetchScalarGridSpec(
            num_scalar_prefetch=3,
            grid=(1,),
            in_specs=[rows, rows, whole, whole],
            out_specs=pl.BlockSpec((2, bw + 8, width // 2), lambda i, *_: (0, 0, 0)),
        ),
        compiler_params=pltpu.CompilerParams(vmem_limit_bytes=ROOM),
        cost_estimate=LIGHT,
    )(at, bits_two, bits_one, panel_two, panel_one, inv_two, inv_one)


def encode_tile(tile, out_ref, block, first):
    bw = tile.shape[0]
    largest = jnp.max(jnp.abs(tile), axis=0, keepdims=True)
    step = jnp.ceil(jnp.log2(jnp.maximum(largest, TINY)) * STEPS)
    code = jnp.round(tile * (jnp.exp2(step * (-1.0 / STEPS)) * LEVELS))
    code = pack(jnp.clip(code, -32767.0, 32767.0).astype(jnp.int32))
    tall, wide = bw // 4, bw // 2
    out_ref[block, pl.ds(first, tall), :] = jnp.concatenate(
        [code[i * tall : (i + 1) * tall] for i in range(4)], axis=1
    )
    head = jnp.broadcast_to(pack(step.astype(jnp.int32)), (8, wide))
    out_ref[block, pl.ds(first + tall, 8), :] = jnp.concatenate([head] * 4, axis=1)


def decode_tile(word, bw):
    tall, wide = bw // 4, bw // 2
    code = jnp.concatenate(
        [word[:tall, i * wide : (i + 1) * wide] for i in range(4)]
        + [word[tall : tall + 8, :wide]],
        axis=0,
    )
    return decode(code)


def image_kernel(bw, pieces, at_ref, cov_ref, *refs):
    held, (two_ref, one_ref, code_ref, head_ref, tail_ref) = refs[:pieces], refs[pieces:]
    width = two_ref.shape[1]

    @pl.when(pl.program_id(0) == 0)
    def _():
        z, core = at_ref[0] // 2, lax.rem(at_ref[0], 2)
        for i, ref in enumerate(held):
            block = lax.rem(z + 4 - i // 2, 4) * 2 + lax.rem(core + i, 2)
            rows = pl.ds(pl.multiple_of(block * bw, bw), bw)
            for panel in range(2):
                head, tail = split(decode(ref[panel]))
                head_ref[rows, panel * width : (panel + 1) * width] = head
                tail_ref[rows, panel * width : (panel + 1) * width] = tail

    cov_head, cov_tail = split(cov_ref[...])
    for panel, image_ref in enumerate((two_ref, one_ref)):
        at = slice(panel * width, (panel + 1) * width)
        image = dot(cov_head, head_ref[:, at]) + (
            dot(cov_head, tail_ref[:, at]) + dot(cov_tail, head_ref[:, at])
        )
        image_ref[...] = image
        for i in range(image.shape[0] // bw):
            encode(image[i * bw : (i + 1) * bw], code_ref, i, first=panel * (bw + 8))

    for i in range(cov_ref.shape[0] // bw):
        block = pl.program_id(0) * (cov_ref.shape[0] // bw) + i

        @pl.when(at_ref[1] == 2 * at_ref[0] + block // pieces)
        def _():
            columns = pl.ds(pl.multiple_of(lax.rem(block, pieces) * bw, bw), bw)
            encode_tile(cov_ref[i * bw : (i + 1) * bw, columns], code_ref, i, 2 * (bw + 8))


def image(at, trail_cov, held, bw, tile=512):
    rows, span = trail_cov.shape
    width = 2 * held[0].shape[-1]
    tall = 2 * (bw + 8) + bw // 4 + 8
    every = pl.BlockSpec(held[0].shape, lambda i, at: (0, 0, 0))
    return pl.pallas_call(
        functools.partial(image_kernel, bw, len(held)),
        out_shape=[jax.ShapeDtypeStruct((rows, width), jnp.float32)] * 2
        + [jax.ShapeDtypeStruct((rows // bw, tall, width // 2), jnp.int32)],
        grid_spec=pltpu.PrefetchScalarGridSpec(
            num_scalar_prefetch=1,
            grid=(rows // tile,),
            in_specs=[pl.BlockSpec((tile, span), lambda i, at: (i, 0))] + [every] * len(held),
            out_specs=[pl.BlockSpec((tile, width), lambda i, at: (i, 0))] * 2
            + [pl.BlockSpec((tile // bw, tall, width // 2), lambda i, at: (i, 0, 0))],
            scratch_shapes=[pltpu.VMEM((span, 2 * width), jnp.bfloat16)] * 2,
        ),
        compiler_params=pltpu.CompilerParams(vmem_limit_bytes=ROOM),
        cost_estimate=LIGHT,
    )(at, trail_cov, *held)


def sums_kernel(
    bw, at_ref, bits_two_ref, bits_one_ref, two_ref, one_ref, image_two_ref, image_one_ref,
    inv_two_ref, inv_one_ref, keep_ref, give_ref, sums_ref,
):
    step = pl.program_id(0)

    @pl.when(step == 0)
    def _():
        sums_ref[...] = jnp.zeros_like(sums_ref)

    count = two_ref.shape[0] // bw
    first = 16 * at_ref[0] + step * count
    skip = bits_one_ref.shape[0] - bits_two_ref.shape[0]

    def masked(ref, bits_ref, base):
        keep = [
            jnp.full((bw, 1), bits_ref[base + i].astype(jnp.float32)) for i in range(count)
        ]
        keep = jnp.concatenate(keep, axis=0)
        return ref[...] * keep, keep

    two, keep_two = masked(two_ref, bits_two_ref, first)
    one, _ = masked(one_ref, bits_one_ref, skip + first)
    image_two = split(image_two_ref[...] * keep_two)
    image_one = split(image_one_ref[...])
    two, one = split(two), split(one)
    for i, (left, right) in enumerate(((two, image_two), (one, image_two), (one, image_one))):
        sums_ref[i] += tdot(left[0], right[0]) + (tdot(left[0], right[1]) + tdot(left[1], right[0]))

    @pl.when(step == pl.num_programs(0) - 1)
    def _():
        half = keep_ref.shape[1]
        core = lax.rem(at_ref[0], 2)
        for i, inv in enumerate((inv_two_ref, inv_one_ref, inv_one_ref)):
            sums_ref[i] = product(inv[...], sums_ref[i], tdot)
            keep_ref[i] = sums_ref[i, pl.ds(pl.multiple_of(core * half, half), half), :]
            give_ref[i] = sums_ref[i, pl.ds(pl.multiple_of((1 - core) * half, half), half), :]


def sums(at, bits_two, bits_one, panel_two, panel_one, image_two, image_one, inv_two, inv_one, bw, tile=512):
    rows, width = panel_two.shape
    part = pl.BlockSpec((tile, width), lambda i, *_: (i, 0))
    whole = pl.BlockSpec((width, width), lambda i, *_: (0, 0))
    half = (3, width // 2, width)
    return pl.pallas_call(
        functools.partial(sums_kernel, bw),
        out_shape=[jax.ShapeDtypeStruct(half, jnp.float32)] * 2,
        grid_spec=pltpu.PrefetchScalarGridSpec(
            num_scalar_prefetch=3,
            grid=(rows // tile,),
            in_specs=[part] * 4 + [whole] * 2,
            out_specs=[pl.BlockSpec(half, lambda i, *_: (0, 0, 0))] * 2,
            scratch_shapes=[pltpu.VMEM((3, width, width), jnp.float32)],
        ),
        compiler_params=pltpu.CompilerParams(vmem_limit_bytes=ROOM),
        cost_estimate=LIGHT,
    )(at, bits_two, bits_one, panel_two, panel_one, image_two, image_one, inv_two, inv_one)


def call(kernel, at, inputs, shapes):
    vmem = pl.BlockSpec(memory_space=pltpu.VMEM)
    return pl.pallas_call(
        kernel,
        out_shape=[jax.ShapeDtypeStruct(*shape) for shape in shapes],
        in_specs=[pl.BlockSpec(memory_space=pltpu.SMEM)] + [vmem] * len(inputs),
        out_specs=[vmem] * len(shapes),
        compiler_params=pltpu.CompilerParams(vmem_limit_bytes=ROOM),
        cost_estimate=LIGHT,
    )(at, *inputs)


def part_of(place, step, size):
    return pl.ds(pl.multiple_of(lax.rem(place + step, 4) * size, size), size)


def fold_z_kernel(at_ref, own_ref, got_ref, mine_ref, *code_refs):
    size = mine_ref.shape[1]
    for step, ref in enumerate((mine_ref, *code_refs)):
        at = part_of(at_ref[0] // 2, step, size)
        for i in range(3):
            value = own_ref[i, at, :] + got_ref[i, at, :]
            if step:
                encode(value, ref, i)
            else:
                ref[i] = value


def fold_z(at, own, got):
    count, size, width = own.shape[0], own.shape[1] // 4, own.shape[2]
    return call(
        fold_z_kernel, at, [own, got],
        [((count, size, width), jnp.float32)] + [((count, size + 8, width // 2), jnp.int32)] * 3,
    )


def fold_x_kernel(at_ref, own_ref, *refs):
    codes, outs, total_ref = refs[:3], refs[3:7], refs[7]
    size = outs[0].shape[1]
    for i in range(3):
        value = own_ref[i]
        for ref in codes:
            value = value + decode(ref[i])
        total_ref[i] = value
    for step, ref in enumerate(outs):
        ref[...] = total_ref[:, part_of(lax.rem(at_ref[1], 4), step, size), :]


def fold_x(at, own, codes):
    count, size, width = own.shape
    part, whole = ((count, size // 4, width), jnp.float32), ((count, size, width), jnp.float32)
    return call(fold_x_kernel, at, [own, *codes], [part] * 4 + [whole])[:4]


def fold_y_kernel(at_ref, *refs):
    parts, outs, total_ref = refs[:4], refs[4:8], refs[8]
    total_ref[...] = (parts[0][...] + parts[1][...]) + (parts[2][...] + parts[3][...])
    size = outs[0].shape[2]
    for step, ref in enumerate(outs):
        ref[...] = total_ref[:, :, part_of(at_ref[1] // 4, step, size)]


def fold_y(at, parts):
    count, size, width = parts[0].shape
    part, whole = ((count, size, width // 4), jnp.float32), ((count, size, width), jnp.float32)
    return call(fold_y_kernel, at, parts, [part] * 4 + [whole])[:4]


def unfold_kernel(at_ref, *refs):
    parts, (code_ref, total_ref) = refs[:4], refs[4:]
    size, lanes = parts[0].shape[2:]
    for dx, ref in enumerate(parts):
        for dy in range(4):
            total_ref[
                :,
                part_of(lax.rem(at_ref[1], 4) + 4, -dx, size),
                part_of(at_ref[1] // 4 + 4, -dy, lanes),
            ] = ref[dy]
    for i in range(3):
        encode(total_ref[i], code_ref, i)


def unfold(at, parts):
    _, count, size, lanes = parts[0].shape
    return call(
        unfold_kernel, at, parts,
        [
            ((count, 4 * size + 8, 2 * lanes), jnp.int32),
            ((count, 4 * size, 4 * lanes), jnp.float32),
        ],
    )[0]


def rows_kernel(at_ref, bits_two_ref, bits_one_ref, panel_ref, code_ref, top_ref, cov_two_ref, cov_one_ref, cross_ref, tile_ref):
    count, bw = code_ref.shape[0], tile_ref.shape[0]
    tile_ref[...] = decode_tile(code_ref[2 * at_ref[0] + at_ref[1] // 8, 2 * (bw + 8) :], bw)
    block = 16 * at_ref[0] + at_ref[1]
    skip = bits_one_ref.shape[0] - bits_two_ref.shape[0]
    keep_two = bits_two_ref[block].astype(jnp.float32)
    keep_one = bits_one_ref[skip + block].astype(jnp.float32)

    def total(panel):
        at = slice(panel * (bw + 8), (panel + 1) * (bw + 8))
        value = decode(code_ref[0, at])
        for i in range(1, count):
            value = value + decode(code_ref[i, at])
        return value

    cov_two = -keep_two * total(0)
    cov_two_ref[...] = cov_two
    cov_one = -keep_one * (product(cov_two, top_ref[...]) + total(1))
    cov_one_ref[...] = cov_one
    cross_ref[...] = cov_one_ref[:, pl.ds(pl.multiple_of(panel_ref[block] * bw, bw), bw)]


def rows(at, bits_two, bits_one, panel, code, norm_top, bw):
    width = norm_top.shape[0]
    smem = pl.BlockSpec(memory_space=pltpu.SMEM)
    vmem = pl.BlockSpec(memory_space=pltpu.VMEM)
    return pl.pallas_call(
        rows_kernel,
        out_shape=[jax.ShapeDtypeStruct((bw, n), jnp.float32) for n in (width, width, bw, bw)],
        in_specs=[smem] * 4 + [vmem] * 2,
        out_specs=[vmem] * 4,
        compiler_params=pltpu.CompilerParams(vmem_limit_bytes=ROOM),
        cost_estimate=LIGHT,
    )(at, bits_two, bits_one, panel, code, norm_top)


def small_kernel(at_ref, keep_ref, gram_ref, top_ref, *refs):
    held, (two_ref, top_cov_ref, one_ref, sums_ref) = refs[:8], refs[8:]
    size = held[0].shape[1] - 8
    z, core = at_ref[0] // 2, lax.rem(at_ref[0], 2)
    for i, ref in enumerate(held):
        block = lax.rem(core + i, 2) * 4 + lax.rem(z + 4 - i // 2, 4)
        rows = pl.ds(pl.multiple_of(block * size, size), size)
        for j in range(3):
            sums_ref[j, rows, :] = decode(ref[j])
    top = top_ref[...]
    two = gram_ref[0] + sums_ref[0]
    two_ref[...] = two
    mixed = sums_ref[1]
    keep = jnp.concatenate(
        [
            jnp.full((top.shape[0] // 4, 1), keep_ref[i].astype(jnp.float32)) for i in range(4)
        ],
        axis=0,
    )
    top_cov = -keep * (product(two, top) - mixed.T)
    top_cov_ref[...] = top_cov
    one_ref[...] = gram_ref[1] + sums_ref[2] - product(top, top_cov, tdot) - product(mixed, top)


def small(at, held, gram, norm_top, bits_top):
    width = norm_top.shape[0]
    smem = pl.BlockSpec(memory_space=pltpu.SMEM)
    vmem = pl.BlockSpec(memory_space=pltpu.VMEM)
    return pl.pallas_call(
        small_kernel,
        out_shape=[jax.ShapeDtypeStruct((width, width), jnp.float32)] * 3,
        in_specs=[smem] * 2 + [vmem] * 10,
        out_specs=[vmem] * 3,
        scratch_shapes=[pltpu.VMEM((3, width, width), jnp.float32)],
        compiler_params=pltpu.CompilerParams(vmem_limit_bytes=ROOM),
        cost_estimate=LIGHT,
    )(at, bits_top, gram, norm_top, *held)


def early_kernel(keep_ref, top_rows_ref, inv_two_ref, inv_one_ref, gram_ref, top_ref):
    keep = jnp.concatenate(
        [
            jnp.full((top_rows_ref.shape[0] // 4, 1), keep_ref[i].astype(jnp.float32))
            for i in range(4)
        ],
        axis=0,
    )
    top_ref[...] = product(keep * top_rows_ref[...], inv_one_ref[...])
    gram_ref[0] = product(inv_two_ref[...], inv_two_ref[...], tdot)
    gram_ref[1] = product(inv_one_ref[...], inv_one_ref[...], tdot)


def early(bits_top, panel_top, inv_two, inv_one):
    width = inv_two.shape[0]
    smem = pl.BlockSpec(memory_space=pltpu.SMEM)
    vmem = pl.BlockSpec(memory_space=pltpu.VMEM)
    return pl.pallas_call(
        early_kernel,
        out_shape=[
            jax.ShapeDtypeStruct((2, width, width), jnp.float32),
            jax.ShapeDtypeStruct((width, width), jnp.float32),
        ],
        in_specs=[smem, vmem, vmem, vmem],
        out_specs=[vmem] * 2,
        compiler_params=pltpu.CompilerParams(vmem_limit_bytes=ROOM),
        cost_estimate=LIGHT,
    )(bits_top, panel_top, inv_two, inv_one)


def row_sums(value):
    ones = jnp.ones((8, value.shape[1]), jnp.bfloat16)
    head, tail = split(value)
    form = (((1,), (1,)), ((), ()))
    return lax.dot_general(
        ones, head, form, preferred_element_type=jnp.float32
    ) + lax.dot_general(ones, tail, form, preferred_element_type=jnp.float32)


def forms_kernel(units_ref, tile_ref, cross_ref, out_ref):
    bw = tile_ref.shape[0]
    front, back = units_ref[:, :bw], units_ref[:, bw:]
    middle = jnp.concatenate([*split(tile_ref[...]), *split(2.0 * cross_ref[...])], axis=1)
    both = dot(front, middle)
    value = (both[:, :bw] + both[:, bw : 2 * bw]) * front.astype(jnp.float32)
    value = value + (both[:, 2 * bw : 3 * bw] + both[:, 3 * bw :]) * back.astype(jnp.float32)
    out_ref[...] = row_sums(value)


def forms(units, tile, cross, step=1024):
    count, bw = units.shape[0], tile.shape[0]
    whole = pl.BlockSpec((bw, bw), lambda i: (0, 0))
    return pl.pallas_call(
        forms_kernel,
        out_shape=jax.ShapeDtypeStruct((8, count), jnp.float32),
        grid=(count // step,),
        in_specs=[pl.BlockSpec((step, 2 * bw), lambda i: (i, 0)), whole, whole],
        out_specs=pl.BlockSpec((8, step), lambda i: (0, i)),
        compiler_params=pltpu.CompilerParams(vmem_limit_bytes=ROOM),
        cost_estimate=LIGHT,
    )(units, tile, cross)


def inner_kernel(units_ref, panel_ref, diag_ref, out_ref):
    bw = units_ref.shape[1] // 2
    back = units_ref[:, bw:]
    count = diag_ref.shape[0] // bw
    value = jnp.zeros(back.shape, jnp.float32)
    for p in range(count):
        at = slice(p * bw, (p + 1) * bw)
        both = dot(back, jnp.concatenate(split(diag_ref[at, at]), axis=1))
        value = jnp.where(panel_ref[...] == p, both[:, :bw] + both[:, bw:], value)
    out_ref[...] = row_sums(value * back.astype(jnp.float32))


def inner(units, panel, diag, step=1024):
    count, width = units.shape
    return pl.pallas_call(
        inner_kernel,
        out_shape=jax.ShapeDtypeStruct((8, count), jnp.float32),
        grid=(count // step,),
        in_specs=[
            pl.BlockSpec((step, width), lambda i: (i, 0)),
            pl.BlockSpec((step, 1), lambda i: (i, 0)),
            pl.BlockSpec(diag.shape, lambda i: (0, 0)),
        ],
        out_specs=pl.BlockSpec((8, step), lambda i: (0, i)),
        compiler_params=pltpu.CompilerParams(vmem_limit_bytes=ROOM),
        cost_estimate=LIGHT,
    )(units, panel, diag)


class Ring:
    def __init__(self, axis, size, stride, count=4):
        self.axis, self.size, self.stride, self.count = axis, size, stride, count

    def move(self, value, step):
        pairs = []
        for i in range(self.size):
            at = i // self.stride % self.count
            pairs.append((i, i + ((at + step) % self.count - at) * self.stride))
        return lax.ppermute(value, self.axis, pairs)

    def others(self, parts):
        return [self.move(part, step + 1) for step, part in enumerate(parts)]


def spread_pairs(row_count, col_count):
    pairs = []
    for r in range(row_count):
        for c in range(col_count):
            first, x, y = 2 * r % 4, c % 4, c // 4
            side = 0 if x in (first, (first + 3) % 4) else 1
            j = 2 * y + (0 if x in (first, first + 1) else 1)
            pairs.append((r * col_count + c, j * col_count + 2 * r + side))
    return pairs


def local(
    trail_cov,
    panel_two_rows,
    diag_inv_two,
    panel_one_top,
    panel_one_rows,
    diag_inv_one,
    pattern_two,
    pattern_one,
    loadings,
    unit_block,
    block_panel,
    counts,
    shape_par,
    exposure,
):
    row_count = lax.axis_size("row")
    col_count = lax.axis_size("col")
    total_count = row_count * col_count
    row_index = lax.axis_index("row")
    col_index = lax.axis_index("col")
    width = diag_inv_two.shape[0]
    bw = loadings.shape[1] // 2
    top_blocks = width // bw
    core = Ring("row", row_count, 1, 2)
    ring_z = Ring("row", row_count, 2)
    ring_x = Ring("col", col_count, 1)
    ring_y = Ring("col", col_count, 4)

    at = jnp.stack([row_index, col_index]).astype(jnp.int32)
    bits_top = pattern_one[:top_blocks]

    part = share(
        at, pattern_two, pattern_one, panel_two_rows, panel_one_rows, diag_inv_two, diag_inv_one, bw
    )
    blocks = unit_block[:, 0]
    part, blocks = lax.optimization_barrier((part, blocks))
    part = lax.ppermute(part, BOTH, spread_pairs(row_count, col_count))

    held = []
    for step in range(4):
        piece = ring_z.move(part, step) if step else part
        held += [piece, core.move(piece, 1)]

    capacity = 2 * loadings.shape[0] // total_count
    hits = (blocks[:, None] == jnp.arange(total_count, dtype=jnp.int32)[None, :]).astype(jnp.int32)
    rank = jnp.sum(jnp.cumsum(hits, axis=0) * hits, axis=1) - 1
    slot = blocks * capacity + rank
    packed = jnp.zeros((total_count * capacity, 2 * bw), jnp.bfloat16).at[slot].set(loadings)
    packed = packed.reshape(total_count, capacity, 2 * bw)
    packed, held[2], held[4], held[6] = lax.optimization_barrier((packed, held[2], held[4], held[6]))
    units = lax.all_to_all(packed, BOTH, split_axis=0, concat_axis=0, tiled=True)
    units = units.reshape(total_count * capacity, 2 * bw)

    image_two, image_one, code = image(at, trail_cov, held, bw)
    code, units = lax.optimization_barrier((code, units))
    code = lax.all_to_all(code, "col", split_axis=0, concat_axis=0, tiled=True)

    keep, give = sums(
        at, pattern_two, pattern_one, panel_two_rows, panel_one_rows, image_two, image_one,
        diag_inv_two, diag_inv_one, bw,
    )
    bits_top, keep = lax.optimization_barrier((bits_top, keep))
    gram, norm_top = early(bits_top, panel_one_top, diag_inv_two, diag_inv_one)
    mine, *codes = fold_z(at, keep, core.move(give, 1))
    mine, *parts = fold_x(at, mine, ring_z.others(codes))
    mine, norm_top = lax.optimization_barrier((mine, norm_top))
    mine, *parts = fold_y(at, [mine, *ring_x.others(parts)])
    total = mine
    for part in ring_y.others(parts):
        total = total + part
    total = jnp.stack([total, *ring_y.others([total] * 3)])
    total = unfold(at, [total, *ring_x.others([total] * 3)])
    total, code = lax.optimization_barrier((total, code))
    whole = []
    for piece in [total, *ring_z.others([total] * 3)]:
        whole += [piece, core.move(piece, 1)]
    cov_two, cov_one, cross, tile = rows(
        at, pattern_two, pattern_one, block_panel, code, norm_top, bw
    )
    value = forms(units, tile, cross)[0].reshape(total_count, capacity)
    returned = lax.all_to_all(value, BOTH, split_axis=0, concat_axis=0, tiled=True)
    diag_two, top_cov, diag_one = small(at, whole, gram, norm_top, bits_top)
    own_panel = jnp.sum(hits * block_panel[None, :], axis=1, keepdims=True)
    within = inner(loadings, own_panel, diag_one)[0]
    within, returned = lax.optimization_barrier((within, returned))
    picked = jnp.dot(
        hits.astype(jnp.float32), returned, precision=lax.Precision.HIGHEST,
        preferred_element_type=jnp.float32,
    )
    at_rank = rank[:, None] == jnp.arange(capacity, dtype=jnp.int32)[None, :]
    variance = jnp.sum(jnp.where(at_rank, picked, 0.0), axis=1)
    variance = variance + within

    mean = exposure * jnp.exp(0.5 * variance)
    seen = counts.astype(jnp.float32)
    scale = shape_par + mean
    shape_grad = (
        lax.digamma(shape_par + seen)
        - lax.digamma(shape_par)
        + jnp.log(shape_par / scale)
        + (mean - seen) / scale
    )
    return (cov_two, top_cov, cov_one, diag_two, diag_one, shape_grad)


def solution(mesh):
    in_specs = (
        P("row", "col"),
        P("row", None),
        P(),
        P(),
        P("row", None),
        P(),
        P(),
        P(),
        P(("row", "col"), None),
        P(("row", "col"), None),
        P(),
        P(("row", "col")),
        P(("row", "col")),
        P(("row", "col")),
    )
    out_specs = (P(("row", "col"), None), P(), P(("row", "col"), None), P(), P(), P(("row", "col")))
    return jax.shard_map(local, mesh=mesh, in_specs=in_specs, out_specs=out_specs, check_vma=False)
```

```python
import functools
import jax
import jax.numpy as jnp
from jax import lax
from jax.experimental import pallas as pl
from jax.experimental.pallas import tpu as pltpu
from jax.sharding import PartitionSpec as P

BOTH = ("row", "col")

LEVELS = 32700.0
STEPS = 64.0
TINY = 1e-33
ROOM = 56 * 1024 * 1024
LIGHT = pl.CostEstimate(flops=1, bytes_accessed=1, transcendentals=0)


def split(value):
    head = value.astype(jnp.bfloat16)
    return head, (value - head.astype(jnp.float32)).astype(jnp.bfloat16)


def dot(left, right):
    return jnp.dot(left, right, preferred_element_type=jnp.float32)


def tdot(left, right):
    return lax.dot_general(
        left, right, (((0,), (0,)), ((), ())), preferred_element_type=jnp.float32
    )


def product(left, right, form=dot):
    left_head, left_tail = split(left)
    right_head, right_tail = split(right)
    return form(left_head, right_head) + (form(left_head, right_tail) + form(left_tail, right_head))


def pack(code):
    half = code.shape[-1] // 2
    return code[..., :half] * 65536 + code[..., half:]


def unpack(word):
    low = lax.shift_right_arithmetic(lax.shift_left(word, 16), 16)
    high = lax.shift_right_arithmetic(word - low, 16)
    return jnp.concatenate([high, low], axis=-1).astype(jnp.float32)


def encode(value, out_ref, *at, first=0):
    rows = value.shape[0]
    largest = jnp.max(jnp.abs(value), axis=0, keepdims=True)
    step = jnp.ceil(jnp.log2(jnp.maximum(largest, TINY)) * STEPS)
    code = jnp.round(value * (jnp.exp2(step * (-1.0 / STEPS)) * LEVELS))
    code = jnp.clip(code, -32767.0, 32767.0).astype(jnp.int32)
    out_ref[(*at, pl.ds(first, rows), slice(None))] = pack(code)
    head = pack(step.astype(jnp.int32))
    out_ref[(*at, pl.ds(first + rows, 8), slice(None))] = jnp.broadcast_to(head, (8, head.shape[1]))


def decode(word):
    rows = word.shape[0] - 8
    scale = jnp.exp2(unpack(word[rows : rows + 1]) * (1.0 / STEPS)) * (1.0 / LEVELS)
    return unpack(word[:rows]) * scale


def chosen(row, col):
    first = lax.rem(2 * row, 4)
    x, y = lax.rem(col, 4), col // 4
    here = (x == first) | (x == lax.rem(first + 3, 4))
    left = (x == first) | (x == first + 1)
    return jnp.where(here, 0, 8) + 2 * y + jnp.where(left, 0, 1)


def share_kernel(at_ref, bits_two_ref, bits_one_ref, two_ref, one_ref, inv_two_ref, inv_one_ref, out_ref):
    block = 16 * at_ref[0] + chosen(at_ref[0], at_ref[1])
    skip = bits_one_ref.shape[0] - bits_two_ref.shape[0]
    keep_two = bits_two_ref[block].astype(jnp.float32)
    keep_one = bits_one_ref[skip + block].astype(jnp.float32)
    encode(product(keep_two * two_ref[...], inv_two_ref[...]), out_ref, 0)
    encode(product(keep_one * one_ref[...], inv_one_ref[...]), out_ref, 1)


def share(at, bits_two, bits_one, panel_two, panel_one, inv_two, inv_one, bw):
    width = inv_two.shape[0]
    rows = pl.BlockSpec((bw, width), lambda i, at, *_: (chosen(at[0], at[1]), 0))
    whole = pl.BlockSpec((width, width), lambda i, *_: (0, 0))
    return pl.pallas_call(
        share_kernel,
        out_shape=jax.ShapeDtypeStruct((2, bw + 8, width // 2), jnp.int32),
        grid_spec=pltpu.PrefetchScalarGridSpec(
            num_scalar_prefetch=3,
            grid=(1,),
            in_specs=[rows, rows, whole, whole],
            out_specs=pl.BlockSpec((2, bw + 8, width // 2), lambda i, *_: (0, 0, 0)),
        ),
        compiler_params=pltpu.CompilerParams(vmem_limit_bytes=ROOM),
        cost_estimate=LIGHT,
    )(at, bits_two, bits_one, panel_two, panel_one, inv_two, inv_one)


def encode_tile(tile, out_ref, block, first):
    bw = tile.shape[0]
    largest = jnp.max(jnp.abs(tile), axis=0, keepdims=True)
    step = jnp.ceil(jnp.log2(jnp.maximum(largest, TINY)) * STEPS)
    code = jnp.round(tile * (jnp.exp2(step * (-1.0 / STEPS)) * LEVELS))
    code = pack(jnp.clip(code, -32767.0, 32767.0).astype(jnp.int32))
    tall, wide = bw // 4, bw // 2
    out_ref[block, pl.ds(first, tall), :] = jnp.concatenate(
        [code[i * tall : (i + 1) * tall] for i in range(4)], axis=1
    )
    head = jnp.broadcast_to(pack(step.astype(jnp.int32)), (8, wide))
    out_ref[block, pl.ds(first + tall, 8), :] = jnp.concatenate([head] * 4, axis=1)


def decode_tile(word, bw):
    tall, wide = bw // 4, bw // 2
    code = jnp.concatenate(
        [word[:tall, i * wide : (i + 1) * wide] for i in range(4)]
        + [word[tall : tall + 8, :wide]],
        axis=0,
    )
    return decode(code)


def image_kernel(bw, pieces, at_ref, cov_ref, *refs):
    held, (two_ref, one_ref, code_ref, head_ref, tail_ref) = refs[:pieces], refs[pieces:]
    width = two_ref.shape[1]

    @pl.when(pl.program_id(0) == 0)
    def _():
        z, core = at_ref[0] // 2, lax.rem(at_ref[0], 2)
        for i, ref in enumerate(held):
            block = lax.rem(z + 4 - i // 2, 4) * 2 + lax.rem(core + i, 2)
            rows = pl.ds(pl.multiple_of(block * bw, bw), bw)
            for panel in range(2):
                head, tail = split(decode(ref[panel]))
                head_ref[rows, panel * width : (panel + 1) * width] = head
                tail_ref[rows, panel * width : (panel + 1) * width] = tail

    cov_head, cov_tail = split(cov_ref[...])
    for panel, image_ref in enumerate((two_ref, one_ref)):
        at = slice(panel * width, (panel + 1) * width)
        image = dot(cov_head, head_ref[:, at]) + (
            dot(cov_head, tail_ref[:, at]) + dot(cov_tail, head_ref[:, at])
        )
        image_ref[...] = image
        for i in range(image.shape[0] // bw):
            encode(image[i * bw : (i + 1) * bw], code_ref, i, first=panel * (bw + 8))

    for i in range(cov_ref.shape[0] // bw):
        block = pl.program_id(0) * (cov_ref.shape[0] // bw) + i

        @pl.when(at_ref[1] == 2 * at_ref[0] + block // pieces)
        def _():
            columns = pl.ds(pl.multiple_of(lax.rem(block, pieces) * bw, bw), bw)
            encode_tile(cov_ref[i * bw : (i + 1) * bw, columns], code_ref, i, 2 * (bw + 8))


def image(at, trail_cov, held, bw, tile=512):
    rows, span = trail_cov.shape
    width = 2 * held[0].shape[-1]
    tall = 2 * (bw + 8) + bw // 4 + 8
    every = pl.BlockSpec(held[0].shape, lambda i, at: (0, 0, 0))
    return pl.pallas_call(
        functools.partial(image_kernel, bw, len(held)),
        out_shape=[jax.ShapeDtypeStruct((rows, width), jnp.float32)] * 2
        + [jax.ShapeDtypeStruct((rows // bw, tall, width // 2), jnp.int32)],
        grid_spec=pltpu.PrefetchScalarGridSpec(
            num_scalar_prefetch=1,
            grid=(rows // tile,),
            in_specs=[pl.BlockSpec((tile, span), lambda i, at: (i, 0))] + [every] * len(held),
            out_specs=[pl.BlockSpec((tile, width), lambda i, at: (i, 0))] * 2
            + [pl.BlockSpec((tile // bw, tall, width // 2), lambda i, at: (i, 0, 0))],
            scratch_shapes=[pltpu.VMEM((span, 2 * width), jnp.bfloat16)] * 2,
        ),
        compiler_params=pltpu.CompilerParams(vmem_limit_bytes=ROOM),
        cost_estimate=LIGHT,
    )(at, trail_cov, *held)


def sums_kernel(
    bw, at_ref, bits_two_ref, bits_one_ref, two_ref, one_ref, image_two_ref, image_one_ref,
    inv_two_ref, inv_one_ref, keep_ref, give_ref, sums_ref,
):
    step = pl.program_id(0)

    @pl.when(step == 0)
    def _():
        sums_ref[...] = jnp.zeros_like(sums_ref)

    count = two_ref.shape[0] // bw
    first = 16 * at_ref[0] + step * count
    skip = bits_one_ref.shape[0] - bits_two_ref.shape[0]

    def masked(ref, bits_ref, base):
        keep = [
            jnp.full((bw, 1), bits_ref[base + i].astype(jnp.float32)) for i in range(count)
        ]
        keep = jnp.concatenate(keep, axis=0)
        return ref[...] * keep, keep

    two, keep_two = masked(two_ref, bits_two_ref, first)
    one, _ = masked(one_ref, bits_one_ref, skip + first)
    image_two = split(image_two_ref[...] * keep_two)
    image_one = split(image_one_ref[...])
    two, one = split(two), split(one)
    for i, (left, right) in enumerate(((two, image_two), (one, image_two), (one, image_one))):
        sums_ref[i] += tdot(left[0], right[0]) + (tdot(left[0], right[1]) + tdot(left[1], right[0]))

    @pl.when(step == pl.num_programs(0) - 1)
    def _():
        half = keep_ref.shape[1]
        core = lax.rem(at_ref[0], 2)
        for i, inv in enumerate((inv_two_ref, inv_one_ref, inv_one_ref)):
            sums_ref[i] = product(inv[...], sums_ref[i], tdot)
            keep_ref[i] = sums_ref[i, pl.ds(pl.multiple_of(core * half, half), half), :]
            give_ref[i] = sums_ref[i, pl.ds(pl.multiple_of((1 - core) * half, half), half), :]


def sums(at, bits_two, bits_one, panel_two, panel_one, image_two, image_one, inv_two, inv_one, bw, tile=512):
    rows, width = panel_two.shape
    part = pl.BlockSpec((tile, width), lambda i, *_: (i, 0))
    whole = pl.BlockSpec((width, width), lambda i, *_: (0, 0))
    half = (3, width // 2, width)
    return pl.pallas_call(
        functools.partial(sums_kernel, bw),
        out_shape=[jax.ShapeDtypeStruct(half, jnp.float32)] * 2,
        grid_spec=pltpu.PrefetchScalarGridSpec(
            num_scalar_prefetch=3,
            grid=(rows // tile,),
            in_specs=[part] * 4 + [whole] * 2,
            out_specs=[pl.BlockSpec(half, lambda i, *_: (0, 0, 0))] * 2,
            scratch_shapes=[pltpu.VMEM((3, width, width), jnp.float32)],
        ),
        compiler_params=pltpu.CompilerParams(vmem_limit_bytes=ROOM),
        cost_estimate=LIGHT,
    )(at, bits_two, bits_one, panel_two, panel_one, image_two, image_one, inv_two, inv_one)


def call(kernel, at, inputs, shapes):
    vmem = pl.BlockSpec(memory_space=pltpu.VMEM)
    return pl.pallas_call(
        kernel,
        out_shape=[jax.ShapeDtypeStruct(*shape) for shape in shapes],
        in_specs=[pl.BlockSpec(memory_space=pltpu.SMEM)] + [vmem] * len(inputs),
        out_specs=[vmem] * len(shapes),
        compiler_params=pltpu.CompilerParams(vmem_limit_bytes=ROOM),
        cost_estimate=LIGHT,
    )(at, *inputs)


def part_of(place, step, size):
    return pl.ds(pl.multiple_of(lax.rem(place + step, 4) * size, size), size)


def fold_z_kernel(at_ref, own_ref, got_ref, mine_ref, *code_refs):
    size = mine_ref.shape[1]
    for step, ref in enumerate((mine_ref, *code_refs)):
        at = part_of(at_ref[0] // 2, step, size)
        for i in range(3):
            value = own_ref[i, at, :] + got_ref[i, at, :]
            if step:
                encode(value, ref, i)
            else:
                ref[i] = value


def fold_z(at, own, got):
    count, size, width = own.shape[0], own.shape[1] // 4, own.shape[2]
    return call(
        fold_z_kernel, at, [own, got],
        [((count, size, width), jnp.float32)] + [((count, size + 8, width // 2), jnp.int32)] * 3,
    )


def fold_x_kernel(at_ref, own_ref, *refs):
    codes, outs, total_ref = refs[:3], refs[3:7], refs[7]
    size = outs[0].shape[1]
    for i in range(3):
        value = own_ref[i]
        for ref in codes:
            value = value + decode(ref[i])
        total_ref[i] = value
    for step, ref in enumerate(outs):
        ref[...] = total_ref[:, part_of(lax.rem(at_ref[1], 4), step, size), :]


def fold_x(at, own, codes):
    count, size, width = own.shape
    part, whole = ((count, size // 4, width), jnp.float32), ((count, size, width), jnp.float32)
    return call(fold_x_kernel, at, [own, *codes], [part] * 4 + [whole])[:4]


def fold_y_kernel(at_ref, *refs):
    parts, (out_ref, held_ref) = refs[:4], refs[4:]
    for dy, ref in enumerate(parts):
        held_ref[lax.rem(at_ref[1] // 4 + 4 - dy, 4)] = ref[...]
    out_ref[...] = (held_ref[0] + held_ref[1]) + (held_ref[2] + held_ref[3])


def fold_y(at, parts):
    shape = parts[0].shape
    return call(
        fold_y_kernel, at, parts, [(shape, jnp.float32), ((4, *shape), jnp.float32)]
    )[0]


def unfold_kernel(at_ref, *refs):
    parts, (code_ref, total_ref) = refs[:4], refs[4:]
    size = parts[0].shape[1]
    for dx, ref in enumerate(parts):
        total_ref[:, part_of(lax.rem(at_ref[1], 4) + 4, -dx, size), :] = ref[...]
    for i in range(3):
        encode(total_ref[i], code_ref, i)


def unfold(at, parts):
    count, size, width = parts[0].shape
    return call(
        unfold_kernel, at, parts,
        [
            ((count, 4 * size + 8, width // 2), jnp.int32),
            ((count, 4 * size, width), jnp.float32),
        ],
    )[0]


def rows_kernel(at_ref, bits_two_ref, bits_one_ref, panel_ref, code_ref, top_ref, cov_two_ref, cov_one_ref, cross_ref, tile_ref):
    count, bw = code_ref.shape[0], tile_ref.shape[0]
    tile_ref[...] = decode_tile(code_ref[2 * at_ref[0] + at_ref[1] // 8, 2 * (bw + 8) :], bw)
    block = 16 * at_ref[0] + at_ref[1]
    skip = bits_one_ref.shape[0] - bits_two_ref.shape[0]
    keep_two = bits_two_ref[block].astype(jnp.float32)
    keep_one = bits_one_ref[skip + block].astype(jnp.float32)

    def total(panel):
        at = slice(panel * (bw + 8), (panel + 1) * (bw + 8))
        value = decode(code_ref[0, at])
        for i in range(1, count):
            value = value + decode(code_ref[i, at])
        return value

    cov_two = -keep_two * total(0)
    cov_two_ref[...] = cov_two
    cov_one = -keep_one * (product(cov_two, top_ref[...]) + total(1))
    cov_one_ref[...] = cov_one
    cross_ref[...] = cov_one_ref[:, pl.ds(pl.multiple_of(panel_ref[block] * bw, bw), bw)]


def rows(at, bits_two, bits_one, panel, code, norm_top, bw):
    width = norm_top.shape[0]
    smem = pl.BlockSpec(memory_space=pltpu.SMEM)
    vmem = pl.BlockSpec(memory_space=pltpu.VMEM)
    return pl.pallas_call(
        rows_kernel,
        out_shape=[jax.ShapeDtypeStruct((bw, n), jnp.float32) for n in (width, width, bw, bw)],
        in_specs=[smem] * 4 + [vmem] * 2,
        out_specs=[vmem] * 4,
        compiler_params=pltpu.CompilerParams(vmem_limit_bytes=ROOM),
        cost_estimate=LIGHT,
    )(at, bits_two, bits_one, panel, code, norm_top)


def small_kernel(at_ref, keep_ref, gram_ref, top_ref, *refs):
    held, (two_ref, top_cov_ref, one_ref, sums_ref) = refs[:8], refs[8:]
    size = held[0].shape[1] - 8
    z, core = at_ref[0] // 2, lax.rem(at_ref[0], 2)
    for i, ref in enumerate(held):
        block = lax.rem(core + i, 2) * 4 + lax.rem(z + 4 - i // 2, 4)
        rows = pl.ds(pl.multiple_of(block * size, size), size)
        for j in range(3):
            sums_ref[j, rows, :] = decode(ref[j])
    top = top_ref[...]
    two = gram_ref[0] + sums_ref[0]
    two_ref[...] = two
    mixed = sums_ref[1]
    keep = jnp.concatenate(
        [
            jnp.full((top.shape[0] // 4, 1), keep_ref[i].astype(jnp.float32)) for i in range(4)
        ],
        axis=0,
    )
    top_cov = -keep * (product(two, top) - mixed.T)
    top_cov_ref[...] = top_cov
    one_ref[...] = gram_ref[1] + sums_ref[2] - product(top, top_cov, tdot) - product(mixed, top)


def small(at, held, gram, norm_top, bits_top):
    width = norm_top.shape[0]
    smem = pl.BlockSpec(memory_space=pltpu.SMEM)
    vmem = pl.BlockSpec(memory_space=pltpu.VMEM)
    return pl.pallas_call(
        small_kernel,
        out_shape=[jax.ShapeDtypeStruct((width, width), jnp.float32)] * 3,
        in_specs=[smem] * 2 + [vmem] * 10,
        out_specs=[vmem] * 3,
        scratch_shapes=[pltpu.VMEM((3, width, width), jnp.float32)],
        compiler_params=pltpu.CompilerParams(vmem_limit_bytes=ROOM),
        cost_estimate=LIGHT,
    )(at, bits_top, gram, norm_top, *held)


def early_kernel(keep_ref, top_rows_ref, inv_two_ref, inv_one_ref, gram_ref, top_ref):
    keep = jnp.concatenate(
        [
            jnp.full((top_rows_ref.shape[0] // 4, 1), keep_ref[i].astype(jnp.float32))
            for i in range(4)
        ],
        axis=0,
    )
    top_ref[...] = product(keep * top_rows_ref[...], inv_one_ref[...])
    gram_ref[0] = product(inv_two_ref[...], inv_two_ref[...], tdot)
    gram_ref[1] = product(inv_one_ref[...], inv_one_ref[...], tdot)


def early(bits_top, panel_top, inv_two, inv_one):
    width = inv_two.shape[0]
    smem = pl.BlockSpec(memory_space=pltpu.SMEM)
    vmem = pl.BlockSpec(memory_space=pltpu.VMEM)
    return pl.pallas_call(
        early_kernel,
        out_shape=[
            jax.ShapeDtypeStruct((2, width, width), jnp.float32),
            jax.ShapeDtypeStruct((width, width), jnp.float32),
        ],
        in_specs=[smem, vmem, vmem, vmem],
        out_specs=[vmem] * 2,
        compiler_params=pltpu.CompilerParams(vmem_limit_bytes=ROOM),
        cost_estimate=LIGHT,
    )(bits_top, panel_top, inv_two, inv_one)


def row_sums(value):
    ones = jnp.ones((8, value.shape[1]), jnp.bfloat16)
    head, tail = split(value)
    form = (((1,), (1,)), ((), ()))
    return lax.dot_general(
        ones, head, form, preferred_element_type=jnp.float32
    ) + lax.dot_general(ones, tail, form, preferred_element_type=jnp.float32)


def forms_kernel(units_ref, tile_ref, cross_ref, out_ref):
    bw = tile_ref.shape[0]
    front, back = units_ref[:, :bw], units_ref[:, bw:]
    middle = jnp.concatenate([*split(tile_ref[...]), *split(2.0 * cross_ref[...])], axis=1)
    both = dot(front, middle)
    value = (both[:, :bw] + both[:, bw : 2 * bw]) * front.astype(jnp.float32)
    value = value + (both[:, 2 * bw : 3 * bw] + both[:, 3 * bw :]) * back.astype(jnp.float32)
    out_ref[...] = row_sums(value)


def forms(units, tile, cross, step=1024):
    count, bw = units.shape[0], tile.shape[0]
    whole = pl.BlockSpec((bw, bw), lambda i: (0, 0))
    return pl.pallas_call(
        forms_kernel,
        out_shape=jax.ShapeDtypeStruct((8, count), jnp.float32),
        grid=(count // step,),
        in_specs=[pl.BlockSpec((step, 2 * bw), lambda i: (i, 0)), whole, whole],
        out_specs=pl.BlockSpec((8, step), lambda i: (0, i)),
        compiler_params=pltpu.CompilerParams(vmem_limit_bytes=ROOM),
        cost_estimate=LIGHT,
    )(units, tile, cross)


def inner_kernel(units_ref, panel_ref, diag_ref, out_ref):
    bw = units_ref.shape[1] // 2
    back = units_ref[:, bw:]
    count = diag_ref.shape[0] // bw
    value = jnp.zeros(back.shape, jnp.float32)
    for p in range(count):
        at = slice(p * bw, (p + 1) * bw)
        both = dot(back, jnp.concatenate(split(diag_ref[at, at]), axis=1))
        value = jnp.where(panel_ref[...] == p, both[:, :bw] + both[:, bw:], value)
    out_ref[...] = row_sums(value * back.astype(jnp.float32))


def inner(units, panel, diag, step=1024):
    count, width = units.shape
    return pl.pallas_call(
        inner_kernel,
        out_shape=jax.ShapeDtypeStruct((8, count), jnp.float32),
        grid=(count // step,),
        in_specs=[
            pl.BlockSpec((step, width), lambda i: (i, 0)),
            pl.BlockSpec((step, 1), lambda i: (i, 0)),
            pl.BlockSpec(diag.shape, lambda i: (0, 0)),
        ],
        out_specs=pl.BlockSpec((8, step), lambda i: (0, i)),
        compiler_params=pltpu.CompilerParams(vmem_limit_bytes=ROOM),
        cost_estimate=LIGHT,
    )(units, panel, diag)


class Ring:
    def __init__(self, axis, size, stride, count=4):
        self.axis, self.size, self.stride, self.count = axis, size, stride, count

    def move(self, value, step):
        pairs = []
        for i in range(self.size):
            at = i // self.stride % self.count
            pairs.append((i, i + ((at + step) % self.count - at) * self.stride))
        return lax.ppermute(value, self.axis, pairs)

    def others(self, parts):
        return [self.move(part, step + 1) for step, part in enumerate(parts)]


def spread_pairs(row_count, col_count):
    pairs = []
    for r in range(row_count):
        for c in range(col_count):
            first, x, y = 2 * r % 4, c % 4, c // 4
            side = 0 if x in (first, (first + 3) % 4) else 1
            j = 2 * y + (0 if x in (first, first + 1) else 1)
            pairs.append((r * col_count + c, j * col_count + 2 * r + side))
    return pairs


def local(
    trail_cov,
    panel_two_rows,
    diag_inv_two,
    panel_one_top,
    panel_one_rows,
    diag_inv_one,
    pattern_two,
    pattern_one,
    loadings,
    unit_block,
    block_panel,
    counts,
    shape_par,
    exposure,
):
    row_count = lax.axis_size("row")
    col_count = lax.axis_size("col")
    total_count = row_count * col_count
    row_index = lax.axis_index("row")
    col_index = lax.axis_index("col")
    width = diag_inv_two.shape[0]
    bw = loadings.shape[1] // 2
    top_blocks = width // bw
    core = Ring("row", row_count, 1, 2)
    ring_z = Ring("row", row_count, 2)
    ring_x = Ring("col", col_count, 1)
    ring_y = Ring("col", col_count, 4)

    at = jnp.stack([row_index, col_index]).astype(jnp.int32)
    bits_top = pattern_one[:top_blocks]

    part = share(
        at, pattern_two, pattern_one, panel_two_rows, panel_one_rows, diag_inv_two, diag_inv_one, bw
    )
    blocks = unit_block[:, 0]
    part, blocks = lax.optimization_barrier((part, blocks))
    part = lax.ppermute(part, BOTH, spread_pairs(row_count, col_count))

    capacity = 2 * loadings.shape[0] // total_count
    hits = (blocks[:, None] == jnp.arange(total_count, dtype=jnp.int32)[None, :]).astype(jnp.int32)
    rank = jnp.sum(jnp.cumsum(hits, axis=0) * hits, axis=1) - 1
    slot = blocks * capacity + rank
    packed = jnp.zeros((total_count * capacity, 2 * bw), jnp.bfloat16).at[slot].set(loadings)
    packed = packed.reshape(total_count, capacity, 2 * bw)
    part, packed = lax.optimization_barrier((part, packed))
    held = []
    for step in range(4):
        piece = ring_z.move(part, step) if step else part
        held += [piece, core.move(piece, 1)]

    packed, held[2], held[4], held[6] = lax.optimization_barrier(
        (packed, held[2], held[4], held[6])
    )
    units = lax.all_to_all(packed, BOTH, split_axis=0, concat_axis=0, tiled=True)
    units = units.reshape(total_count * capacity, 2 * bw)

    image_two, image_one, code = image(at, trail_cov, held, bw)
    code, units = lax.optimization_barrier((code, units))
    code = lax.all_to_all(code, "col", split_axis=0, concat_axis=0, tiled=True)

    keep, give = sums(
        at, pattern_two, pattern_one, panel_two_rows, panel_one_rows, image_two, image_one,
        diag_inv_two, diag_inv_one, bw,
    )
    bits_top, keep = lax.optimization_barrier((bits_top, keep))
    gram, norm_top = early(bits_top, panel_one_top, diag_inv_two, diag_inv_one)
    mine, *codes = fold_z(at, keep, core.move(give, 1))
    mine, *parts = fold_x(at, mine, ring_z.others(codes))
    mine, norm_top = lax.optimization_barrier((mine, norm_top))
    total = mine
    for part in ring_x.others(parts):
        total = total + part
    total, code = lax.optimization_barrier((total, code))
    total = fold_y(at, [total, *ring_y.others([total] * 3)])
    cov_two, cov_one, cross, tile = rows(
        at, pattern_two, pattern_one, block_panel, code, norm_top, bw
    )
    value = forms(units, tile, cross)[0].reshape(total_count, capacity)
    total, value = lax.optimization_barrier((total, value))
    parts = [total, *ring_x.others([total] * 3)]
    total = unfold(at, parts)
    whole = []
    for piece in [total, *ring_z.others([total] * 3)]:
        whole += [piece, core.move(piece, 1)]
    returned = lax.all_to_all(value, BOTH, split_axis=0, concat_axis=0, tiled=True)
    diag_two, top_cov, diag_one = small(at, whole, gram, norm_top, bits_top)
    own_panel = jnp.sum(hits * block_panel[None, :], axis=1, keepdims=True)
    within = inner(loadings, own_panel, diag_one)[0]
    within, returned = lax.optimization_barrier((within, returned))
    picked = jnp.dot(
        hits.astype(jnp.float32), returned, precision=lax.Precision.HIGHEST,
        preferred_element_type=jnp.float32,
    )
    at_rank = rank[:, None] == jnp.arange(capacity, dtype=jnp.int32)[None, :]
    variance = jnp.sum(jnp.where(at_rank, picked, 0.0), axis=1)
    variance = variance + within

    mean = exposure * jnp.exp(0.5 * variance)
    seen = counts.astype(jnp.float32)
    scale = shape_par + mean
    shape_grad = (
        lax.digamma(shape_par + seen)
        - lax.digamma(shape_par)
        + jnp.log(shape_par / scale)
        + (mean - seen) / scale
    )
    return (cov_two, top_cov, cov_one, diag_two, diag_one, shape_grad)


def solution(mesh):
    in_specs = (
        P("row", "col"),
        P("row", None),
        P(),
        P(),
        P("row", None),
        P(),
        P(),
        P(),
        P(("row", "col"), None),
        P(("row", "col"), None),
        P(),
        P(("row", "col")),
        P(("row", "col")),
        P(("row", "col")),
    )
    out_specs = (P(("row", "col"), None), P(), P(("row", "col"), None), P(), P(), P(("row", "col")))
    return jax.shard_map(local, mesh=mesh, in_specs=in_specs, out_specs=out_specs, check_vma=False)
```

```python
import functools
import jax
import jax.numpy as jnp
from jax import lax
from jax.experimental import pallas as pl
from jax.experimental.pallas import tpu as pltpu
from jax.sharding import PartitionSpec as P

BOTH = ("row", "col")

LEVELS = 32700.0
STEPS = 64.0
TINY = 1e-33
ROOM = 56 * 1024 * 1024
LIGHT = pl.CostEstimate(flops=1, bytes_accessed=1, transcendentals=0)


def split(value):
    head = value.astype(jnp.bfloat16)
    return head, (value - head.astype(jnp.float32)).astype(jnp.bfloat16)


def dot(left, right):
    return jnp.dot(left, right, preferred_element_type=jnp.float32)


def tdot(left, right):
    return lax.dot_general(
        left, right, (((0,), (0,)), ((), ())), preferred_element_type=jnp.float32
    )


def product(left, right, form=dot):
    left_head, left_tail = split(left)
    right_head, right_tail = split(right)
    return form(left_head, right_head) + (form(left_head, right_tail) + form(left_tail, right_head))


def pack(code):
    half = code.shape[-1] // 2
    return code[..., :half] * 65536 + code[..., half:]


def unpack(word):
    low = lax.shift_right_arithmetic(lax.shift_left(word, 16), 16)
    high = lax.shift_right_arithmetic(word - low, 16)
    return jnp.concatenate([high, low], axis=-1).astype(jnp.float32)


def encode(value, out_ref, *at, first=0):
    rows = value.shape[0]
    largest = jnp.max(jnp.abs(value), axis=0, keepdims=True)
    step = jnp.ceil(jnp.log2(jnp.maximum(largest, TINY)) * STEPS)
    code = jnp.round(value * (jnp.exp2(step * (-1.0 / STEPS)) * LEVELS))
    code = jnp.clip(code, -32767.0, 32767.0).astype(jnp.int32)
    out_ref[(*at, pl.ds(first, rows), slice(None))] = pack(code)
    head = pack(step.astype(jnp.int32))
    out_ref[(*at, pl.ds(first + rows, 8), slice(None))] = jnp.broadcast_to(head, (8, head.shape[1]))


def decode(word):
    rows = word.shape[0] - 8
    scale = jnp.exp2(unpack(word[rows : rows + 1]) * (1.0 / STEPS)) * (1.0 / LEVELS)
    return unpack(word[:rows]) * scale


def chosen(row, col):
    first = lax.rem(2 * row, 4)
    x, y = lax.rem(col, 4), col // 4
    here = (x == first) | (x == lax.rem(first + 3, 4))
    left = (x == first) | (x == first + 1)
    return jnp.where(here, 0, 8) + 2 * y + jnp.where(left, 0, 1)


def share_kernel(at_ref, bits_two_ref, bits_one_ref, two_ref, one_ref, inv_two_ref, inv_one_ref, out_ref):
    block = 16 * at_ref[0] + chosen(at_ref[0], at_ref[1])
    skip = bits_one_ref.shape[0] - bits_two_ref.shape[0]
    keep_two = bits_two_ref[block].astype(jnp.float32)
    keep_one = bits_one_ref[skip + block].astype(jnp.float32)
    encode(product(keep_two * two_ref[...], inv_two_ref[...]), out_ref, 0)
    encode(product(keep_one * one_ref[...], inv_one_ref[...]), out_ref, 1)


def share(at, bits_two, bits_one, panel_two, panel_one, inv_two, inv_one, bw):
    width = inv_two.shape[0]
    rows = pl.BlockSpec((bw, width), lambda i, at, *_: (chosen(at[0], at[1]), 0))
    whole = pl.BlockSpec((width, width), lambda i, *_: (0, 0))
    return pl.pallas_call(
        share_kernel,
        out_shape=jax.ShapeDtypeStruct((2, bw + 8, width // 2), jnp.int32),
        grid_spec=pltpu.PrefetchScalarGridSpec(
            num_scalar_prefetch=3,
            grid=(1,),
            in_specs=[rows, rows, whole, whole],
            out_specs=pl.BlockSpec((2, bw + 8, width // 2), lambda i, *_: (0, 0, 0)),
        ),
        compiler_params=pltpu.CompilerParams(vmem_limit_bytes=ROOM),
        cost_estimate=LIGHT,
    )(at, bits_two, bits_one, panel_two, panel_one, inv_two, inv_one)


def encode_tile(tile, out_ref, block, first):
    bw = tile.shape[0]
    largest = jnp.max(jnp.abs(tile), axis=0, keepdims=True)
    step = jnp.ceil(jnp.log2(jnp.maximum(largest, TINY)) * STEPS)
    code = jnp.round(tile * (jnp.exp2(step * (-1.0 / STEPS)) * LEVELS))
    code = pack(jnp.clip(code, -32767.0, 32767.0).astype(jnp.int32))
    tall, wide = bw // 4, bw // 2
    out_ref[block, pl.ds(first, tall), :] = jnp.concatenate(
        [code[i * tall : (i + 1) * tall] for i in range(4)], axis=1
    )
    head = jnp.broadcast_to(pack(step.astype(jnp.int32)), (8, wide))
    out_ref[block, pl.ds(first + tall, 8), :] = jnp.concatenate([head] * 4, axis=1)


def decode_tile(word, bw):
    tall, wide = bw // 4, bw // 2
    code = jnp.concatenate(
        [word[:tall, i * wide : (i + 1) * wide] for i in range(4)]
        + [word[tall : tall + 8, :wide]],
        axis=0,
    )
    return decode(code)


def tiles_kernel(at_ref, *refs):
    given, out_ref = refs[:-1], refs[-1]
    bw = given[0].shape[0]
    for i, ref in enumerate(given):
        for side in range(2):

            @pl.when(at_ref[1] == 2 * at_ref[0] + side)
            def _():
                encode_tile(ref[...], out_ref, side * len(given) + i, 0)


def tiles_of(at, trail_cov, count, bw):
    def block(j):
        return pl.BlockSpec((bw, bw), lambda i, at: (lax.rem(at[1], 2) * count + j, j))

    shape = (2 * count, bw // 4 + 8, 2 * bw)
    return pl.pallas_call(
        tiles_kernel,
        out_shape=jax.ShapeDtypeStruct(shape, jnp.int32),
        grid_spec=pltpu.PrefetchScalarGridSpec(
            num_scalar_prefetch=1,
            grid=(1,),
            in_specs=[block(j) for j in range(count)],
            out_specs=pl.BlockSpec(shape, lambda i, at: (0, 0, 0)),
        ),
        compiler_params=pltpu.CompilerParams(vmem_limit_bytes=ROOM),
        cost_estimate=LIGHT,
    )(at, *[trail_cov] * count)


def image_kernel(bw, pieces, at_ref, cov_ref, *refs):
    held, (two_ref, one_ref, own_two_ref, own_one_ref) = refs[:pieces], refs[pieces : pieces + 4]
    to_x, to_y = refs[pieces + 4 : pieces + 7], refs[pieces + 7 : pieces + 10]
    head_ref, tail_ref = refs[pieces + 10 :]
    width = two_ref.shape[1]
    step = pl.program_id(0)
    x, y = lax.rem(at_ref[1], 4), at_ref[1] // 4
    here = lax.rem(y + 1 + step, 4)

    @pl.when(step == 0)
    def _():
        z, core = at_ref[0] // 2, lax.rem(at_ref[0], 2)
        for i, ref in enumerate(held):
            block = lax.rem(z + 4 - i // 2, 4) * 2 + lax.rem(core + i, 2)
            rows = pl.ds(pl.multiple_of(block * bw, bw), bw)
            for panel in range(2):
                head, tail = split(decode(ref[panel]))
                head_ref[rows, panel * width : (panel + 1) * width] = head
                tail_ref[rows, panel * width : (panel + 1) * width] = tail

    cov_head, cov_tail = split(cov_ref[...])
    for panel, image_ref in enumerate((two_ref, one_ref)):
        at = slice(panel * width, (panel + 1) * width)
        image_ref[...] = dot(cov_head, head_ref[:, at]) + (
            dot(cov_head, tail_ref[:, at]) + dot(cov_tail, head_ref[:, at])
        )
    own_two_ref[here] = two_ref[part_of(x, 0, bw), :]
    for i, ref in enumerate(to_x):
        encode(two_ref[part_of(x, i + 1, bw), :], ref, here)
    for i, ref in enumerate(to_y):

        @pl.when(step == i)
        def _():
            for j in range(4):
                encode(one_ref[j * bw : (j + 1) * bw], ref, j)

    @pl.when(step == 3)
    def _():
        for j in range(4):
            own_one_ref[j] = one_ref[j * bw : (j + 1) * bw]


def image(at, trail_cov, held, bw):
    rows, span = trail_cov.shape
    width = 2 * held[0].shape[-1]
    tile = 4 * bw

    def turned(i, at):
        return (lax.rem(at[1] // 4 + 1 + i, 4), 0)

    def fixed(*shape):
        return pl.BlockSpec(shape, lambda i, at: (0,) * len(shape))

    code = (4, bw + 8, width // 2)
    return pl.pallas_call(
        functools.partial(image_kernel, bw, len(held)),
        out_shape=[jax.ShapeDtypeStruct((rows, width), jnp.float32)] * 2
        + [jax.ShapeDtypeStruct((4, bw, width), jnp.float32)] * 2
        + [jax.ShapeDtypeStruct(code, jnp.int32)] * 6,
        grid_spec=pltpu.PrefetchScalarGridSpec(
            num_scalar_prefetch=1,
            grid=(rows // tile,),
            in_specs=[pl.BlockSpec((tile, span), turned)] + [fixed(*held[0].shape)] * len(held),
            out_specs=[pl.BlockSpec((tile, width), turned)] * 2
            + [fixed(4, bw, width)] * 2
            + [fixed(*code)] * 6,
            scratch_shapes=[pltpu.VMEM((span, 2 * width), jnp.bfloat16)] * 2,
        ),
        compiler_params=pltpu.CompilerParams(vmem_limit_bytes=ROOM),
        cost_estimate=LIGHT,
    )(at, trail_cov, *held)


def fold_image_kernel(at_ref, own_two_ref, own_one_ref, *refs):
    codes, outs = (refs[:3], refs[3:6]), (refs[6:10], refs[10:14])
    place = at_ref[1] // 4, lax.rem(at_ref[1], 4)
    for panel, own_ref in enumerate((own_two_ref, own_one_ref)):
        for step, out_ref in enumerate(outs[panel]):
            block = lax.rem(place[panel] + step, 4)
            value = own_ref[block]
            for ref in codes[panel]:
                value = value + decode(ref[block])
            if step:
                encode(value, out_ref)
            else:
                out_ref[...] = value


def fold_image(at, own_two, own_one, codes):
    _, bw, width = own_two.shape
    part, code = ((bw, width), jnp.float32), ((bw + 8, width // 2), jnp.int32)
    return call(fold_image_kernel, at, [own_two, own_one, *codes], ([part] + [code] * 3) * 2)


def sums_kernel(
    bw, at_ref, bits_two_ref, bits_one_ref, two_ref, one_ref, image_two_ref, image_one_ref,
    inv_two_ref, inv_one_ref, keep_ref, give_ref, sums_ref,
):
    step = pl.program_id(0)

    @pl.when(step == 0)
    def _():
        sums_ref[...] = jnp.zeros_like(sums_ref)

    count = two_ref.shape[0] // bw
    first = 16 * at_ref[0] + step * count
    skip = bits_one_ref.shape[0] - bits_two_ref.shape[0]

    def masked(ref, bits_ref, base):
        keep = [
            jnp.full((bw, 1), bits_ref[base + i].astype(jnp.float32)) for i in range(count)
        ]
        keep = jnp.concatenate(keep, axis=0)
        return ref[...] * keep, keep

    two, keep_two = masked(two_ref, bits_two_ref, first)
    one, _ = masked(one_ref, bits_one_ref, skip + first)
    image_two = split(image_two_ref[...] * keep_two)
    image_one = split(image_one_ref[...])
    two, one = split(two), split(one)
    for i, (left, right) in enumerate(((two, image_two), (one, image_two), (one, image_one))):
        sums_ref[i] += tdot(left[0], right[0]) + (tdot(left[0], right[1]) + tdot(left[1], right[0]))

    @pl.when(step == pl.num_programs(0) - 1)
    def _():
        half = keep_ref.shape[1]
        core = lax.rem(at_ref[0], 2)
        for i, inv in enumerate((inv_two_ref, inv_one_ref, inv_one_ref)):
            sums_ref[i] = product(inv[...], sums_ref[i], tdot)
            keep_ref[i] = sums_ref[i, pl.ds(pl.multiple_of(core * half, half), half), :]
            give_ref[i] = sums_ref[i, pl.ds(pl.multiple_of((1 - core) * half, half), half), :]


def sums(at, bits_two, bits_one, panel_two, panel_one, image_two, image_one, inv_two, inv_one, bw, tile=512):
    rows, width = panel_two.shape
    part = pl.BlockSpec((tile, width), lambda i, *_: (i, 0))
    whole = pl.BlockSpec((width, width), lambda i, *_: (0, 0))
    half = (3, width // 2, width)
    return pl.pallas_call(
        functools.partial(sums_kernel, bw),
        out_shape=[jax.ShapeDtypeStruct(half, jnp.float32)] * 2,
        grid_spec=pltpu.PrefetchScalarGridSpec(
            num_scalar_prefetch=3,
            grid=(rows // tile,),
            in_specs=[part] * 4 + [whole] * 2,
            out_specs=[pl.BlockSpec(half, lambda i, *_: (0, 0, 0))] * 2,
            scratch_shapes=[pltpu.VMEM((3, width, width), jnp.float32)],
        ),
        compiler_params=pltpu.CompilerParams(vmem_limit_bytes=ROOM),
        cost_estimate=LIGHT,
    )(at, bits_two, bits_one, panel_two, panel_one, image_two, image_one, inv_two, inv_one)


def call(kernel, at, inputs, shapes):
    vmem = pl.BlockSpec(memory_space=pltpu.VMEM)
    return pl.pallas_call(
        kernel,
        out_shape=[jax.ShapeDtypeStruct(*shape) for shape in shapes],
        in_specs=[pl.BlockSpec(memory_space=pltpu.SMEM)] + [vmem] * len(inputs),
        out_specs=[vmem] * len(shapes),
        compiler_params=pltpu.CompilerParams(vmem_limit_bytes=ROOM),
        cost_estimate=LIGHT,
    )(at, *inputs)


def part_of(place, step, size):
    return pl.ds(pl.multiple_of(lax.rem(place + step, 4) * size, size), size)


def fold_z_kernel(at_ref, own_ref, got_ref, mine_ref, codes_ref):
    size = mine_ref.shape[1]
    z = at_ref[0] // 2
    for step in range(4):
        at = part_of(z, step, size)
        for i in range(3):
            value = own_ref[i, at, :] + got_ref[i, at, :]
            if step:
                encode(value, codes_ref, lax.rem(z + step, 4), i)
            else:
                mine_ref[i] = value


def fold_z(at, own, got):
    count, size, width = own.shape[0], own.shape[1] // 4, own.shape[2]
    return call(
        fold_z_kernel, at, [own, got],
        [((count, size, width), jnp.float32), ((4, count, size + 8, width // 2), jnp.int32)],
    )


def fold_x_kernel(at_ref, own_ref, codes_ref, *refs):
    outs, total_ref = refs[:4], refs[4]
    size = outs[0].shape[1]
    z = at_ref[0] // 2
    for i in range(3):
        value = own_ref[i]
        for step in range(1, 4):
            value = value + decode(codes_ref[lax.rem(z + step, 4), i])
        total_ref[i] = value
    for step, ref in enumerate(outs):
        ref[...] = total_ref[:, part_of(lax.rem(at_ref[1], 4), step, size), :]


def fold_x(at, own, codes):
    count, size, width = own.shape
    part, whole = ((count, size // 4, width), jnp.float32), ((count, size, width), jnp.float32)
    return call(fold_x_kernel, at, [own, codes], [part] * 4 + [whole])[:4]


def fold_y_kernel(at_ref, *refs):
    parts, (out_ref, held_ref) = refs[:4], refs[4:]
    for dy, ref in enumerate(parts):
        held_ref[lax.rem(at_ref[1] // 4 + 4 - dy, 4)] = ref[...]
    out_ref[...] = (held_ref[0] + held_ref[1]) + (held_ref[2] + held_ref[3])


def fold_y(at, parts):
    shape = parts[0].shape
    return call(
        fold_y_kernel, at, parts, [(shape, jnp.float32), ((4, *shape), jnp.float32)]
    )[0]


def unfold_kernel(at_ref, *refs):
    parts, (code_ref, total_ref) = refs[:4], refs[4:]
    size = parts[0].shape[1]
    for dx, ref in enumerate(parts):
        total_ref[:, part_of(lax.rem(at_ref[1], 4) + 4, -dx, size), :] = ref[...]
    for i in range(3):
        encode(total_ref[i], code_ref, i)


def unfold(at, parts):
    count, size, width = parts[0].shape
    return call(
        unfold_kernel, at, parts,
        [
            ((count, 4 * size + 8, width // 2), jnp.int32),
            ((count, 4 * size, width), jnp.float32),
        ],
    )[0]


def rows_kernel(
    at_ref, bits_two_ref, bits_one_ref, panel_ref, own_two_ref, own_one_ref, tiles_ref, top_ref, *refs
):
    codes, (cov_two_ref, cov_one_ref, cross_ref, tile_ref) = refs[:6], refs[6:]
    bw = tile_ref.shape[0]
    tile_ref[...] = decode_tile(tiles_ref[2 * at_ref[0] + at_ref[1] // 8], bw)
    block = 16 * at_ref[0] + at_ref[1]
    skip = bits_one_ref.shape[0] - bits_two_ref.shape[0]
    keep_two = bits_two_ref[block].astype(jnp.float32)
    keep_one = bits_one_ref[skip + block].astype(jnp.float32)

    def total(own_ref, parts):
        value = own_ref[...]
        for ref in parts:
            value = value + decode(ref[...])
        return value

    cov_two = -keep_two * total(own_two_ref, codes[:3])
    cov_two_ref[...] = cov_two
    cov_one = -keep_one * (product(cov_two, top_ref[...]) + total(own_one_ref, codes[3:]))
    cov_one_ref[...] = cov_one
    cross_ref[...] = cov_one_ref[:, pl.ds(pl.multiple_of(panel_ref[block] * bw, bw), bw)]


def rows(at, bits_two, bits_one, panel, own_two, own_one, codes, tiles, norm_top, bw):
    width = norm_top.shape[0]
    smem = pl.BlockSpec(memory_space=pltpu.SMEM)
    vmem = pl.BlockSpec(memory_space=pltpu.VMEM)
    return pl.pallas_call(
        rows_kernel,
        out_shape=[jax.ShapeDtypeStruct((bw, n), jnp.float32) for n in (width, width, bw, bw)],
        in_specs=[smem] * 4 + [vmem] * 10,
        out_specs=[vmem] * 4,
        compiler_params=pltpu.CompilerParams(vmem_limit_bytes=ROOM),
        cost_estimate=LIGHT,
    )(at, bits_two, bits_one, panel, own_two, own_one, tiles, norm_top, *codes)


def small_kernel(at_ref, keep_ref, gram_ref, top_ref, *refs):
    held, (two_ref, top_cov_ref, one_ref, sums_ref) = refs[:8], refs[8:]
    size = held[0].shape[1] - 8
    z, core = at_ref[0] // 2, lax.rem(at_ref[0], 2)
    for i, ref in enumerate(held):
        block = lax.rem(core + i, 2) * 4 + lax.rem(z + 4 - i // 2, 4)
        rows = pl.ds(pl.multiple_of(block * size, size), size)
        for j in range(3):
            sums_ref[j, rows, :] = decode(ref[j])
    top = top_ref[...]
    two = gram_ref[0] + sums_ref[0]
    two_ref[...] = two
    mixed = sums_ref[1]
    keep = jnp.concatenate(
        [
            jnp.full((top.shape[0] // 4, 1), keep_ref[i].astype(jnp.float32)) for i in range(4)
        ],
        axis=0,
    )
    top_cov = -keep * (product(two, top) - mixed.T)
    top_cov_ref[...] = top_cov
    one_ref[...] = gram_ref[1] + sums_ref[2] - product(top, top_cov, tdot) - product(mixed, top)


def small(at, held, gram, norm_top, bits_top):
    width = norm_top.shape[0]
    smem = pl.BlockSpec(memory_space=pltpu.SMEM)
    vmem = pl.BlockSpec(memory_space=pltpu.VMEM)
    return pl.pallas_call(
        small_kernel,
        out_shape=[jax.ShapeDtypeStruct((width, width), jnp.float32)] * 3,
        in_specs=[smem] * 2 + [vmem] * 10,
        out_specs=[vmem] * 3,
        scratch_shapes=[pltpu.VMEM((3, width, width), jnp.float32)],
        compiler_params=pltpu.CompilerParams(vmem_limit_bytes=ROOM),
        cost_estimate=LIGHT,
    )(at, bits_top, gram, norm_top, *held)


def early_kernel(keep_ref, top_rows_ref, inv_two_ref, inv_one_ref, gram_ref, top_ref):
    keep = jnp.concatenate(
        [
            jnp.full((top_rows_ref.shape[0] // 4, 1), keep_ref[i].astype(jnp.float32))
            for i in range(4)
        ],
        axis=0,
    )
    top_ref[...] = product(keep * top_rows_ref[...], inv_one_ref[...])
    gram_ref[0] = product(inv_two_ref[...], inv_two_ref[...], tdot)
    gram_ref[1] = product(inv_one_ref[...], inv_one_ref[...], tdot)


def early(bits_top, panel_top, inv_two, inv_one):
    width = inv_two.shape[0]
    smem = pl.BlockSpec(memory_space=pltpu.SMEM)
    vmem = pl.BlockSpec(memory_space=pltpu.VMEM)
    return pl.pallas_call(
        early_kernel,
        out_shape=[
            jax.ShapeDtypeStruct((2, width, width), jnp.float32),
            jax.ShapeDtypeStruct((width, width), jnp.float32),
        ],
        in_specs=[smem, vmem, vmem, vmem],
        out_specs=[vmem] * 2,
        compiler_params=pltpu.CompilerParams(vmem_limit_bytes=ROOM),
        cost_estimate=LIGHT,
    )(bits_top, panel_top, inv_two, inv_one)


def row_sums(value):
    ones = jnp.ones((8, value.shape[1]), jnp.bfloat16)
    head, tail = split(value)
    form = (((1,), (1,)), ((), ()))
    return lax.dot_general(
        ones, head, form, preferred_element_type=jnp.float32
    ) + lax.dot_general(ones, tail, form, preferred_element_type=jnp.float32)


def forms_kernel(units_ref, tile_ref, cross_ref, out_ref):
    bw = tile_ref.shape[0]
    front, back = units_ref[:, :bw], units_ref[:, bw:]
    middle = jnp.concatenate([*split(tile_ref[...]), *split(2.0 * cross_ref[...])], axis=1)
    both = dot(front, middle)
    value = (both[:, :bw] + both[:, bw : 2 * bw]) * front.astype(jnp.float32)
    value = value + (both[:, 2 * bw : 3 * bw] + both[:, 3 * bw :]) * back.astype(jnp.float32)
    out_ref[...] = row_sums(value)


def forms(units, tile, cross, step=1024):
    count, bw = units.shape[0], tile.shape[0]
    whole = pl.BlockSpec((bw, bw), lambda i: (0, 0))
    return pl.pallas_call(
        forms_kernel,
        out_shape=jax.ShapeDtypeStruct((8, count), jnp.float32),
        grid=(count // step,),
        in_specs=[pl.BlockSpec((step, 2 * bw), lambda i: (i, 0)), whole, whole],
        out_specs=pl.BlockSpec((8, step), lambda i: (0, i)),
        compiler_params=pltpu.CompilerParams(vmem_limit_bytes=ROOM),
        cost_estimate=LIGHT,
    )(units, tile, cross)


def inner_kernel(units_ref, panel_ref, diag_ref, out_ref):
    bw = units_ref.shape[1] // 2
    back = units_ref[:, bw:]
    count = diag_ref.shape[0] // bw
    value = jnp.zeros(back.shape, jnp.float32)
    for p in range(count):
        at = slice(p * bw, (p + 1) * bw)
        both = dot(back, jnp.concatenate(split(diag_ref[at, at]), axis=1))
        value = jnp.where(panel_ref[...] == p, both[:, :bw] + both[:, bw:], value)
    out_ref[...] = row_sums(value * back.astype(jnp.float32))


def inner(units, panel, diag, step=1024):
    count, width = units.shape
    return pl.pallas_call(
        inner_kernel,
        out_shape=jax.ShapeDtypeStruct((8, count), jnp.float32),
        grid=(count // step,),
        in_specs=[
            pl.BlockSpec((step, width), lambda i: (i, 0)),
            pl.BlockSpec((step, 1), lambda i: (i, 0)),
            pl.BlockSpec(diag.shape, lambda i: (0, 0)),
        ],
        out_specs=pl.BlockSpec((8, step), lambda i: (0, i)),
        compiler_params=pltpu.CompilerParams(vmem_limit_bytes=ROOM),
        cost_estimate=LIGHT,
    )(units, panel, diag)


class Ring:
    def __init__(self, axis, size, stride, count=4):
        self.axis, self.size, self.stride, self.count = axis, size, stride, count

    def move(self, value, step):
        pairs = []
        for i in range(self.size):
            at = i // self.stride % self.count
            pairs.append((i, i + ((at + step) % self.count - at) * self.stride))
        return lax.ppermute(value, self.axis, pairs)

    def others(self, parts):
        return [self.move(part, step + 1) for step, part in enumerate(parts)]


def spread_pairs(row_count, col_count):
    pairs = []
    for r in range(row_count):
        for c in range(col_count):
            first, x, y = 2 * r % 4, c % 4, c // 4
            side = 0 if x in (first, (first + 3) % 4) else 1
            j = 2 * y + (0 if x in (first, first + 1) else 1)
            pairs.append((r * col_count + c, j * col_count + 2 * r + side))
    return pairs


def local(
    trail_cov,
    panel_two_rows,
    diag_inv_two,
    panel_one_top,
    panel_one_rows,
    diag_inv_one,
    pattern_two,
    pattern_one,
    loadings,
    unit_block,
    block_panel,
    counts,
    shape_par,
    exposure,
):
    row_count = lax.axis_size("row")
    col_count = lax.axis_size("col")
    total_count = row_count * col_count
    row_index = lax.axis_index("row")
    col_index = lax.axis_index("col")
    width = diag_inv_two.shape[0]
    bw = loadings.shape[1] // 2
    top_blocks = width // bw
    core = Ring("row", row_count, 1, 2)
    ring_z = Ring("row", row_count, 2)
    ring_x = Ring("col", col_count, 1)
    ring_y = Ring("col", col_count, 4)

    at = jnp.stack([row_index, col_index]).astype(jnp.int32)
    bits_top = pattern_one[:top_blocks]

    part = share(
        at, pattern_two, pattern_one, panel_two_rows, panel_one_rows, diag_inv_two, diag_inv_one, bw
    )
    blocks = unit_block[:, 0]
    part, blocks = lax.optimization_barrier((part, blocks))
    part = lax.ppermute(part, BOTH, spread_pairs(row_count, col_count))

    capacity = 2 * loadings.shape[0] // total_count
    hits = (blocks[:, None] == jnp.arange(total_count, dtype=jnp.int32)[None, :]).astype(jnp.int32)
    rank = jnp.sum(jnp.cumsum(hits, axis=0) * hits, axis=1) - 1
    slot = blocks * capacity + rank
    packed = jnp.zeros((total_count * capacity, 2 * bw), jnp.bfloat16).at[slot].set(loadings)
    packed = packed.reshape(total_count, capacity, 2 * bw)
    part, packed = lax.optimization_barrier((part, packed))
    held = []
    for step in range(4):
        piece = ring_z.move(part, step) if step else part
        held += [piece, core.move(piece, 1)]

    part, turn = lax.optimization_barrier((part, at))
    tiles = tiles_of(turn, trail_cov, row_count, bw)
    packed, tiles, held[2], held[4], held[6] = lax.optimization_barrier(
        (packed, tiles, held[2], held[4], held[6])
    )
    units = lax.all_to_all(packed, BOTH, split_axis=0, concat_axis=0, tiled=True)
    units = units.reshape(total_count * capacity, 2 * bw)

    tiles, units = lax.optimization_barrier((tiles, units))
    tiles = lax.all_to_all(tiles, "col", split_axis=0, concat_axis=0, tiled=True)
    image_two, image_one, own_two, own_one, *codes = image(at, trail_cov, held, bw)
    far_x, far_y = codes[1], codes[4]
    near = [ring_x.move(codes[0], 1), ring_x.move(codes[2], 3)]
    near += [ring_y.move(codes[3], 1), ring_y.move(codes[5], 3)]
    bits_top, own_two = lax.optimization_barrier((bits_top, own_two))
    gram, norm_top = early(bits_top, panel_one_top, diag_inv_two, diag_inv_one)
    image_two, image_one, near, norm_top, tiles = lax.optimization_barrier(
        (image_two, image_one, near, norm_top, tiles)
    )
    far = [ring_x.move(far_x, 2), ring_y.move(far_y, 2)]

    keep, give = sums(
        at, pattern_two, pattern_one, panel_two_rows, panel_one_rows, image_two, image_one,
        diag_inv_two, diag_inv_one, bw,
    )
    keep, give, far = lax.optimization_barrier((keep, give, far))
    codes = [near[0], far[0], near[1], near[2], far[1], near[3]]
    mine, parts = fold_z(at, keep, core.move(give, 1))
    parts = lax.all_to_all(
        parts, "row", split_axis=0, concat_axis=0, tiled=True,
        axis_index_groups=[[2 * z + c for z in range(4)] for c in range(2)],
    )
    own_two, *two, own_one, one_a, one_b, one_c = fold_image(at, own_two, own_one, codes)
    codes = ring_y.others(two) + ring_x.others([one_a, one_b, one_c])
    mine, *parts = fold_x(at, mine, parts)
    total = mine
    for part in ring_x.others(parts):
        total = total + part
    total = fold_y(at, [total, *ring_y.others([total] * 3)])
    cov_two, cov_one, cross, tile = rows(
        at, pattern_two, pattern_one, block_panel, own_two, own_one, codes, tiles, norm_top, bw
    )
    value = forms(units, tile, cross)[0].reshape(total_count, capacity)
    total, value = lax.optimization_barrier((total, value))
    parts = [total, *ring_x.others([total] * 3)]
    total = unfold(at, parts)
    whole = []
    for piece in [total, *ring_z.others([total] * 3)]:
        whole += [piece, core.move(piece, 1)]
    returned = lax.all_to_all(value, BOTH, split_axis=0, concat_axis=0, tiled=True)
    diag_two, top_cov, diag_one = small(at, whole, gram, norm_top, bits_top)
    own_panel = jnp.sum(hits * block_panel[None, :], axis=1, keepdims=True)
    within = inner(loadings, own_panel, diag_one)[0]
    within, returned = lax.optimization_barrier((within, returned))
    picked = jnp.dot(
        hits.astype(jnp.float32), returned, precision=lax.Precision.HIGHEST,
        preferred_element_type=jnp.float32,
    )
    at_rank = rank[:, None] == jnp.arange(capacity, dtype=jnp.int32)[None, :]
    variance = jnp.sum(jnp.where(at_rank, picked, 0.0), axis=1)
    variance = variance + within

    mean = exposure * jnp.exp(0.5 * variance)
    seen = counts.astype(jnp.float32)
    scale = shape_par + mean
    shape_grad = (
        lax.digamma(shape_par + seen)
        - lax.digamma(shape_par)
        + jnp.log(shape_par / scale)
        + (mean - seen) / scale
    )
    return (cov_two, top_cov, cov_one, diag_two, diag_one, shape_grad)


def solution(mesh):
    in_specs = (
        P("row", "col"),
        P("row", None),
        P(),
        P(),
        P("row", None),
        P(),
        P(),
        P(),
        P(("row", "col"), None),
        P(("row", "col"), None),
        P(),
        P(("row", "col")),
        P(("row", "col")),
        P(("row", "col")),
    )
    out_specs = (P(("row", "col"), None), P(), P(("row", "col"), None), P(), P(), P(("row", "col")))
    return jax.shard_map(local, mesh=mesh, in_specs=in_specs, out_specs=out_specs, check_vma=False)
```

```python
import functools
import jax
import jax.numpy as jnp
from jax import lax
from jax.experimental import pallas as pl
from jax.experimental.pallas import tpu as pltpu
from jax.sharding import PartitionSpec as P

BOTH = ("row", "col")

LEVELS = 32700.0
STEPS = 64.0
TINY = 1e-33
ROOM = 56 * 1024 * 1024
LIGHT = pl.CostEstimate(flops=1, bytes_accessed=1, transcendentals=0)


def split(value):
    head = value.astype(jnp.bfloat16)
    return head, (value - head.astype(jnp.float32)).astype(jnp.bfloat16)


def dot(left, right):
    return jnp.dot(left, right, preferred_element_type=jnp.float32)


def tdot(left, right):
    return lax.dot_general(
        left, right, (((0,), (0,)), ((), ())), preferred_element_type=jnp.float32
    )


def product(left, right, form=dot):
    left_head, left_tail = split(left)
    right_head, right_tail = split(right)
    return form(left_head, right_head) + (form(left_head, right_tail) + form(left_tail, right_head))


def pack(code):
    half = code.shape[-1] // 2
    return code[..., :half] * 65536 + code[..., half:]


def unpack(word):
    low = lax.shift_right_arithmetic(lax.shift_left(word, 16), 16)
    high = lax.shift_right_arithmetic(word - low, 16)
    return jnp.concatenate([high, low], axis=-1).astype(jnp.float32)


def encode(value, out_ref, *at, first=0):
    rows = value.shape[0]
    largest = jnp.max(jnp.abs(value), axis=0, keepdims=True)
    step = jnp.ceil(jnp.log2(jnp.maximum(largest, TINY)) * STEPS)
    code = jnp.round(value * (jnp.exp2(step * (-1.0 / STEPS)) * LEVELS))
    code = jnp.clip(code, -32767.0, 32767.0).astype(jnp.int32)
    out_ref[(*at, pl.ds(first, rows), slice(None))] = pack(code)
    head = pack(step.astype(jnp.int32))
    out_ref[(*at, pl.ds(first + rows, 8), slice(None))] = jnp.broadcast_to(head, (8, head.shape[1]))


def decode(word):
    rows = word.shape[0] - 8
    scale = jnp.exp2(unpack(word[rows : rows + 1]) * (1.0 / STEPS)) * (1.0 / LEVELS)
    return unpack(word[:rows]) * scale


def chosen(row, col):
    first = lax.rem(2 * row, 4)
    x, y = lax.rem(col, 4), col // 4
    here = (x == first) | (x == lax.rem(first + 3, 4))
    left = (x == first) | (x == first + 1)
    return jnp.where(here, 0, 8) + 2 * y + jnp.where(left, 0, 1)


def share_kernel(at_ref, bits_two_ref, bits_one_ref, two_ref, one_ref, inv_two_ref, inv_one_ref, out_ref):
    block = 16 * at_ref[0] + chosen(at_ref[0], at_ref[1])
    skip = bits_one_ref.shape[0] - bits_two_ref.shape[0]
    keep_two = bits_two_ref[block].astype(jnp.float32)
    keep_one = bits_one_ref[skip + block].astype(jnp.float32)
    encode(product(keep_two * two_ref[...], inv_two_ref[...]), out_ref, 0)
    encode(product(keep_one * one_ref[...], inv_one_ref[...]), out_ref, 1)


def share(at, bits_two, bits_one, panel_two, panel_one, inv_two, inv_one, bw):
    width = inv_two.shape[0]
    rows = pl.BlockSpec((bw, width), lambda i, at, *_: (chosen(at[0], at[1]), 0))
    whole = pl.BlockSpec((width, width), lambda i, *_: (0, 0))
    return pl.pallas_call(
        share_kernel,
        out_shape=jax.ShapeDtypeStruct((2, bw + 8, width // 2), jnp.int32),
        grid_spec=pltpu.PrefetchScalarGridSpec(
            num_scalar_prefetch=3,
            grid=(1,),
            in_specs=[rows, rows, whole, whole],
            out_specs=pl.BlockSpec((2, bw + 8, width // 2), lambda i, *_: (0, 0, 0)),
        ),
        compiler_params=pltpu.CompilerParams(vmem_limit_bytes=ROOM),
        cost_estimate=LIGHT,
    )(at, bits_two, bits_one, panel_two, panel_one, inv_two, inv_one)


def encode_tile(tile, out_ref, block, first):
    bw = tile.shape[0]
    largest = jnp.max(jnp.abs(tile), axis=0, keepdims=True)
    step = jnp.ceil(jnp.log2(jnp.maximum(largest, TINY)) * STEPS)
    code = jnp.round(tile * (jnp.exp2(step * (-1.0 / STEPS)) * LEVELS))
    code = pack(jnp.clip(code, -32767.0, 32767.0).astype(jnp.int32))
    tall, wide = bw // 4, bw // 2
    out_ref[block, pl.ds(first, tall), :] = jnp.concatenate(
        [code[i * tall : (i + 1) * tall] for i in range(4)], axis=1
    )
    head = jnp.broadcast_to(pack(step.astype(jnp.int32)), (8, wide))
    out_ref[block, pl.ds(first + tall, 8), :] = jnp.concatenate([head] * 4, axis=1)


def decode_tile(word, bw):
    tall, wide = bw // 4, bw // 2
    code = jnp.concatenate(
        [word[:tall, i * wide : (i + 1) * wide] for i in range(4)]
        + [word[tall : tall + 8, :wide]],
        axis=0,
    )
    return decode(code)


def tiles_kernel(at_ref, *refs):
    given, out_ref = refs[:-1], refs[-1]
    bw = given[0].shape[0]
    for i, ref in enumerate(given):
        for side in range(2):

            @pl.when(at_ref[1] == 2 * at_ref[0] + side)
            def _():
                encode_tile(ref[...], out_ref, side * len(given) + i, 0)


def tiles_of(at, trail_cov, count, bw):
    def block(j):
        return pl.BlockSpec((bw, bw), lambda i, at: (lax.rem(at[1], 2) * count + j, j))

    shape = (2 * count, bw // 4 + 8, 2 * bw)
    return pl.pallas_call(
        tiles_kernel,
        out_shape=jax.ShapeDtypeStruct(shape, jnp.int32),
        grid_spec=pltpu.PrefetchScalarGridSpec(
            num_scalar_prefetch=1,
            grid=(1,),
            in_specs=[block(j) for j in range(count)],
            out_specs=pl.BlockSpec(shape, lambda i, at: (0, 0, 0)),
        ),
        compiler_params=pltpu.CompilerParams(vmem_limit_bytes=ROOM),
        cost_estimate=LIGHT,
    )(at, *[trail_cov] * count)


def image_kernel(bw, pieces, at_ref, cov_ref, *refs):
    held, (two_ref, one_ref, own_two_ref, own_one_ref) = refs[:pieces], refs[pieces : pieces + 4]
    to_x, to_y = refs[pieces + 4 : pieces + 7], refs[pieces + 7 : pieces + 10]
    head_ref, tail_ref = refs[pieces + 10 :]
    width = two_ref.shape[1]
    step = pl.program_id(0)
    x, y = lax.rem(at_ref[1], 4), at_ref[1] // 4
    here = lax.rem(y + 1 + step, 4)

    @pl.when(step == 0)
    def _():
        z, core = at_ref[0] // 2, lax.rem(at_ref[0], 2)
        for i, ref in enumerate(held):
            block = lax.rem(z + 4 - i // 2, 4) * 2 + lax.rem(core + i, 2)
            rows = pl.ds(pl.multiple_of(block * bw, bw), bw)
            for panel in range(2):
                head, tail = split(decode(ref[panel]))
                head_ref[rows, panel * width : (panel + 1) * width] = head
                tail_ref[rows, panel * width : (panel + 1) * width] = tail

    cov_head, cov_tail = split(cov_ref[...])
    for panel, image_ref in enumerate((two_ref, one_ref)):
        at = slice(panel * width, (panel + 1) * width)
        image_ref[...] = dot(cov_head, head_ref[:, at]) + (
            dot(cov_head, tail_ref[:, at]) + dot(cov_tail, head_ref[:, at])
        )
    own_two_ref[here] = two_ref[part_of(x, 0, bw), :]
    for i, ref in enumerate(to_x):
        encode(two_ref[part_of(x, i + 1, bw), :], ref, here)
    for i, ref in enumerate(to_y):

        @pl.when(step == i)
        def _():
            for j in range(4):
                encode(one_ref[j * bw : (j + 1) * bw], ref, j)

    @pl.when(step == 3)
    def _():
        for j in range(4):
            own_one_ref[j] = one_ref[j * bw : (j + 1) * bw]


def image(at, trail_cov, held, bw):
    rows, span = trail_cov.shape
    width = 2 * held[0].shape[-1]
    tile = 4 * bw

    def turned(i, at):
        return (lax.rem(at[1] // 4 + 1 + i, 4), 0)

    def fixed(*shape):
        return pl.BlockSpec(shape, lambda i, at: (0,) * len(shape))

    code = (4, bw + 8, width // 2)
    return pl.pallas_call(
        functools.partial(image_kernel, bw, len(held)),
        out_shape=[jax.ShapeDtypeStruct((rows, width), jnp.float32)] * 2
        + [jax.ShapeDtypeStruct((4, bw, width), jnp.float32)] * 2
        + [jax.ShapeDtypeStruct(code, jnp.int32)] * 6,
        grid_spec=pltpu.PrefetchScalarGridSpec(
            num_scalar_prefetch=1,
            grid=(rows // tile,),
            in_specs=[pl.BlockSpec((tile, span), turned)] + [fixed(*held[0].shape)] * len(held),
            out_specs=[pl.BlockSpec((tile, width), turned)] * 2
            + [fixed(4, bw, width)] * 2
            + [fixed(*code)] * 6,
            scratch_shapes=[pltpu.VMEM((span, 2 * width), jnp.bfloat16)] * 2,
        ),
        compiler_params=pltpu.CompilerParams(vmem_limit_bytes=ROOM),
        cost_estimate=LIGHT,
    )(at, trail_cov, *held)


def fold_image_kernel(at_ref, own_two_ref, own_one_ref, *refs):
    codes, outs = (refs[:3], refs[3:6]), (refs[6:10], refs[10:14])
    place = at_ref[1] // 4, lax.rem(at_ref[1], 4)
    for panel, own_ref in enumerate((own_two_ref, own_one_ref)):
        for step, out_ref in enumerate(outs[panel]):
            block = lax.rem(place[panel] + step, 4)
            value = own_ref[block]
            for ref in codes[panel]:
                value = value + decode(ref[block])
            if step:
                encode(value, out_ref)
            else:
                out_ref[...] = value


def fold_image(at, own_two, own_one, codes):
    _, bw, width = own_two.shape
    part, code = ((bw, width), jnp.float32), ((bw + 8, width // 2), jnp.int32)
    return call(fold_image_kernel, at, [own_two, own_one, *codes], ([part] + [code] * 3) * 2)


def sums_kernel(
    bw, at_ref, bits_two_ref, bits_one_ref, two_ref, one_ref, image_two_ref, image_one_ref,
    inv_two_ref, inv_one_ref, keep_ref, give_ref, sums_ref,
):
    step = pl.program_id(0)

    @pl.when(step == 0)
    def _():
        sums_ref[...] = jnp.zeros_like(sums_ref)

    count = two_ref.shape[0] // bw
    first = 16 * at_ref[0] + step * count
    skip = bits_one_ref.shape[0] - bits_two_ref.shape[0]

    def masked(ref, bits_ref, base):
        keep = [
            jnp.full((bw, 1), bits_ref[base + i].astype(jnp.float32)) for i in range(count)
        ]
        keep = jnp.concatenate(keep, axis=0)
        return ref[...] * keep, keep

    two, keep_two = masked(two_ref, bits_two_ref, first)
    one, _ = masked(one_ref, bits_one_ref, skip + first)
    image_two = split(image_two_ref[...] * keep_two)
    image_one = split(image_one_ref[...])
    two, one = split(two), split(one)
    for i, (left, right) in enumerate(((two, image_two), (one, image_two), (one, image_one))):
        sums_ref[i] += tdot(left[0], right[0]) + (tdot(left[0], right[1]) + tdot(left[1], right[0]))

    @pl.when(step == pl.num_programs(0) - 1)
    def _():
        half = keep_ref.shape[1]
        core = lax.rem(at_ref[0], 2)
        for i, inv in enumerate((inv_two_ref, inv_one_ref, inv_one_ref)):
            sums_ref[i] = product(inv[...], sums_ref[i], tdot)
            keep_ref[i] = sums_ref[i, pl.ds(pl.multiple_of(core * half, half), half), :]
            give_ref[i] = sums_ref[i, pl.ds(pl.multiple_of((1 - core) * half, half), half), :]


def sums(at, bits_two, bits_one, panel_two, panel_one, image_two, image_one, inv_two, inv_one, bw, tile=512):
    rows, width = panel_two.shape
    part = pl.BlockSpec((tile, width), lambda i, *_: (i, 0))
    whole = pl.BlockSpec((width, width), lambda i, *_: (0, 0))
    half = (3, width // 2, width)
    return pl.pallas_call(
        functools.partial(sums_kernel, bw),
        out_shape=[jax.ShapeDtypeStruct(half, jnp.float32)] * 2,
        grid_spec=pltpu.PrefetchScalarGridSpec(
            num_scalar_prefetch=3,
            grid=(rows // tile,),
            in_specs=[part] * 4 + [whole] * 2,
            out_specs=[pl.BlockSpec(half, lambda i, *_: (0, 0, 0))] * 2,
            scratch_shapes=[pltpu.VMEM((3, width, width), jnp.float32)],
        ),
        compiler_params=pltpu.CompilerParams(vmem_limit_bytes=ROOM),
        cost_estimate=LIGHT,
    )(at, bits_two, bits_one, panel_two, panel_one, image_two, image_one, inv_two, inv_one)


def call(kernel, at, inputs, shapes):
    vmem = pl.BlockSpec(memory_space=pltpu.VMEM)
    return pl.pallas_call(
        kernel,
        out_shape=[jax.ShapeDtypeStruct(*shape) for shape in shapes],
        in_specs=[pl.BlockSpec(memory_space=pltpu.SMEM)] + [vmem] * len(inputs),
        out_specs=[vmem] * len(shapes),
        compiler_params=pltpu.CompilerParams(vmem_limit_bytes=ROOM),
        cost_estimate=LIGHT,
    )(at, *inputs)


def part_of(place, step, size):
    return pl.ds(pl.multiple_of(lax.rem(place + step, 4) * size, size), size)


def fold_z_kernel(at_ref, own_ref, got_ref, mine_ref, codes_ref):
    size = mine_ref.shape[1]
    z = at_ref[0] // 2
    for step in range(4):
        at = part_of(z, step, size)
        for i in range(3):
            value = own_ref[i, at, :] + got_ref[i, at, :]
            if step:
                encode(value, codes_ref, lax.rem(z + step, 4), i)
            else:
                mine_ref[i] = value


def fold_z(at, own, got):
    count, size, width = own.shape[0], own.shape[1] // 4, own.shape[2]
    return call(
        fold_z_kernel, at, [own, got],
        [((count, size, width), jnp.float32), ((4, count, size + 8, width // 2), jnp.int32)],
    )


def fold_x_kernel(at_ref, own_ref, codes_ref, *refs):
    outs, total_ref = refs[:4], refs[4]
    size = outs[0].shape[1]
    z = at_ref[0] // 2
    for i in range(3):
        value = own_ref[i]
        for step in range(1, 4):
            value = value + decode(codes_ref[lax.rem(z + step, 4), i])
        total_ref[i] = value
    for step, ref in enumerate(outs):
        ref[...] = total_ref[:, part_of(lax.rem(at_ref[1], 4), step, size), :]


def fold_x(at, own, codes):
    count, size, width = own.shape
    part, whole = ((count, size // 4, width), jnp.float32), ((count, size, width), jnp.float32)
    return call(fold_x_kernel, at, [own, codes], [part] * 4 + [whole])[:4]


def fold_y_kernel(at_ref, *refs):
    parts, (out_ref, held_ref) = refs[:4], refs[4:]
    for dy, ref in enumerate(parts):
        held_ref[lax.rem(at_ref[1] // 4 + 4 - dy, 4)] = ref[...]
    out_ref[...] = (held_ref[0] + held_ref[1]) + (held_ref[2] + held_ref[3])


def fold_y(at, parts):
    shape = parts[0].shape
    return call(
        fold_y_kernel, at, parts, [(shape, jnp.float32), ((4, *shape), jnp.float32)]
    )[0]


def unfold_kernel(at_ref, *refs):
    parts, (code_ref, total_ref) = refs[:4], refs[4:]
    size = parts[0].shape[1]
    for dx, ref in enumerate(parts):
        total_ref[:, part_of(lax.rem(at_ref[1], 4) + 4, -dx, size), :] = ref[...]
    for i in range(3):
        encode(total_ref[i], code_ref, i)


def unfold(at, parts):
    count, size, width = parts[0].shape
    return call(
        unfold_kernel, at, parts,
        [
            ((count, 4 * size + 8, width // 2), jnp.int32),
            ((count, 4 * size, width), jnp.float32),
        ],
    )[0]


def rows_kernel(
    at_ref, bits_two_ref, bits_one_ref, panel_ref, own_two_ref, own_one_ref, tiles_ref, top_ref, *refs
):
    codes, (cov_two_ref, cov_one_ref, cross_ref, tile_ref) = refs[:6], refs[6:]
    bw = tile_ref.shape[0]
    tile_ref[...] = decode_tile(tiles_ref[2 * at_ref[0] + at_ref[1] // 8], bw)
    block = 16 * at_ref[0] + at_ref[1]
    skip = bits_one_ref.shape[0] - bits_two_ref.shape[0]
    keep_two = bits_two_ref[block].astype(jnp.float32)
    keep_one = bits_one_ref[skip + block].astype(jnp.float32)

    def total(own_ref, parts):
        value = own_ref[...]
        for ref in parts:
            value = value + decode(ref[...])
        return value

    cov_two = -keep_two * total(own_two_ref, codes[:3])
    cov_two_ref[...] = cov_two
    cov_one = -keep_one * (product(cov_two, top_ref[...]) + total(own_one_ref, codes[3:]))
    cov_one_ref[...] = cov_one
    cross_ref[...] = cov_one_ref[:, pl.ds(pl.multiple_of(panel_ref[block] * bw, bw), bw)]


def rows(at, bits_two, bits_one, panel, own_two, own_one, codes, tiles, norm_top, bw):
    width = norm_top.shape[0]
    smem = pl.BlockSpec(memory_space=pltpu.SMEM)
    vmem = pl.BlockSpec(memory_space=pltpu.VMEM)
    return pl.pallas_call(
        rows_kernel,
        out_shape=[jax.ShapeDtypeStruct((bw, n), jnp.float32) for n in (width, width, bw, bw)],
        in_specs=[smem] * 4 + [vmem] * 10,
        out_specs=[vmem] * 4,
        compiler_params=pltpu.CompilerParams(vmem_limit_bytes=ROOM),
        cost_estimate=LIGHT,
    )(at, bits_two, bits_one, panel, own_two, own_one, tiles, norm_top, *codes)


def small_kernel(at_ref, keep_ref, gram_ref, top_ref, *refs):
    held, (two_ref, top_cov_ref, one_ref, sums_ref) = refs[:8], refs[8:]
    size = held[0].shape[1] - 8
    z, core = at_ref[0] // 2, lax.rem(at_ref[0], 2)
    for i, ref in enumerate(held):
        block = lax.rem(core + i, 2) * 4 + lax.rem(z + 4 - i // 2, 4)
        rows = pl.ds(pl.multiple_of(block * size, size), size)
        for j in range(3):
            sums_ref[j, rows, :] = decode(ref[j])
    top = top_ref[...]
    two = gram_ref[0] + sums_ref[0]
    two_ref[...] = two
    mixed = sums_ref[1]
    keep = jnp.concatenate(
        [
            jnp.full((top.shape[0] // 4, 1), keep_ref[i].astype(jnp.float32)) for i in range(4)
        ],
        axis=0,
    )
    top_cov = -keep * (product(two, top) - mixed.T)
    top_cov_ref[...] = top_cov
    one_ref[...] = gram_ref[1] + sums_ref[2] - product(top, top_cov, tdot) - product(mixed, top)


def small(at, held, gram, norm_top, bits_top):
    width = norm_top.shape[0]
    smem = pl.BlockSpec(memory_space=pltpu.SMEM)
    vmem = pl.BlockSpec(memory_space=pltpu.VMEM)
    return pl.pallas_call(
        small_kernel,
        out_shape=[jax.ShapeDtypeStruct((width, width), jnp.float32)] * 3,
        in_specs=[smem] * 2 + [vmem] * 10,
        out_specs=[vmem] * 3,
        scratch_shapes=[pltpu.VMEM((3, width, width), jnp.float32)],
        compiler_params=pltpu.CompilerParams(vmem_limit_bytes=ROOM),
        cost_estimate=LIGHT,
    )(at, bits_top, gram, norm_top, *held)


def early_kernel(keep_ref, top_rows_ref, inv_two_ref, inv_one_ref, gram_ref, top_ref):
    keep = jnp.concatenate(
        [
            jnp.full((top_rows_ref.shape[0] // 4, 1), keep_ref[i].astype(jnp.float32))
            for i in range(4)
        ],
        axis=0,
    )
    top_ref[...] = product(keep * top_rows_ref[...], inv_one_ref[...])
    gram_ref[0] = product(inv_two_ref[...], inv_two_ref[...], tdot)
    gram_ref[1] = product(inv_one_ref[...], inv_one_ref[...], tdot)


def early(bits_top, panel_top, inv_two, inv_one):
    width = inv_two.shape[0]
    smem = pl.BlockSpec(memory_space=pltpu.SMEM)
    vmem = pl.BlockSpec(memory_space=pltpu.VMEM)
    return pl.pallas_call(
        early_kernel,
        out_shape=[
            jax.ShapeDtypeStruct((2, width, width), jnp.float32),
            jax.ShapeDtypeStruct((width, width), jnp.float32),
        ],
        in_specs=[smem, vmem, vmem, vmem],
        out_specs=[vmem] * 2,
        compiler_params=pltpu.CompilerParams(vmem_limit_bytes=ROOM),
        cost_estimate=LIGHT,
    )(bits_top, panel_top, inv_two, inv_one)


def row_sums(value):
    ones = jnp.ones((8, value.shape[1]), jnp.bfloat16)
    head, tail = split(value)
    form = (((1,), (1,)), ((), ()))
    return lax.dot_general(
        ones, head, form, preferred_element_type=jnp.float32
    ) + lax.dot_general(ones, tail, form, preferred_element_type=jnp.float32)


def forms_kernel(units_ref, tile_ref, cross_ref, out_ref):
    bw = tile_ref.shape[0]
    front, back = units_ref[:, :bw], units_ref[:, bw:]
    middle = jnp.concatenate([*split(tile_ref[...]), *split(2.0 * cross_ref[...])], axis=1)
    both = dot(front, middle)
    value = (both[:, :bw] + both[:, bw : 2 * bw]) * front.astype(jnp.float32)
    value = value + (both[:, 2 * bw : 3 * bw] + both[:, 3 * bw :]) * back.astype(jnp.float32)
    out_ref[...] = row_sums(value)


def forms(units, tile, cross, step=1024):
    count, bw = units.shape[0], tile.shape[0]
    whole = pl.BlockSpec((bw, bw), lambda i: (0, 0))
    return pl.pallas_call(
        forms_kernel,
        out_shape=jax.ShapeDtypeStruct((8, count), jnp.float32),
        grid=(count // step,),
        in_specs=[pl.BlockSpec((step, 2 * bw), lambda i: (i, 0)), whole, whole],
        out_specs=pl.BlockSpec((8, step), lambda i: (0, i)),
        compiler_params=pltpu.CompilerParams(vmem_limit_bytes=ROOM),
        cost_estimate=LIGHT,
    )(units, tile, cross)


def inner_kernel(units_ref, panel_ref, diag_ref, out_ref):
    bw = units_ref.shape[1] // 2
    back = units_ref[:, bw:]
    count = diag_ref.shape[0] // bw
    value = jnp.zeros(back.shape, jnp.float32)
    for p in range(count):
        at = slice(p * bw, (p + 1) * bw)
        both = dot(back, jnp.concatenate(split(diag_ref[at, at]), axis=1))
        value = jnp.where(panel_ref[...] == p, both[:, :bw] + both[:, bw:], value)
    out_ref[...] = row_sums(value * back.astype(jnp.float32))


def inner(units, panel, diag, step=1024):
    count, width = units.shape
    return pl.pallas_call(
        inner_kernel,
        out_shape=jax.ShapeDtypeStruct((8, count), jnp.float32),
        grid=(count // step,),
        in_specs=[
            pl.BlockSpec((step, width), lambda i: (i, 0)),
            pl.BlockSpec((step, 1), lambda i: (i, 0)),
            pl.BlockSpec(diag.shape, lambda i: (0, 0)),
        ],
        out_specs=pl.BlockSpec((8, step), lambda i: (0, i)),
        compiler_params=pltpu.CompilerParams(vmem_limit_bytes=ROOM),
        cost_estimate=LIGHT,
    )(units, panel, diag)


class Ring:
    def __init__(self, axis, size, stride, count=4):
        self.axis, self.size, self.stride, self.count = axis, size, stride, count

    def move(self, value, step):
        pairs = []
        for i in range(self.size):
            at = i // self.stride % self.count
            pairs.append((i, i + ((at + step) % self.count - at) * self.stride))
        return lax.ppermute(value, self.axis, pairs)

    def others(self, parts):
        return [self.move(part, step + 1) for step, part in enumerate(parts)]


def spread_pairs(row_count, col_count):
    pairs = []
    for r in range(row_count):
        for c in range(col_count):
            first, x, y = 2 * r % 4, c % 4, c // 4
            side = 0 if x in (first, (first + 3) % 4) else 1
            j = 2 * y + (0 if x in (first, first + 1) else 1)
            pairs.append((r * col_count + c, j * col_count + 2 * r + side))
    return pairs


def local(
    trail_cov,
    panel_two_rows,
    diag_inv_two,
    panel_one_top,
    panel_one_rows,
    diag_inv_one,
    pattern_two,
    pattern_one,
    loadings,
    unit_block,
    block_panel,
    counts,
    shape_par,
    exposure,
):
    row_count = lax.axis_size("row")
    col_count = lax.axis_size("col")
    total_count = row_count * col_count
    row_index = lax.axis_index("row")
    col_index = lax.axis_index("col")
    width = diag_inv_two.shape[0]
    bw = loadings.shape[1] // 2
    top_blocks = width // bw
    core = Ring("row", row_count, 1, 2)
    ring_z = Ring("row", row_count, 2)
    ring_x = Ring("col", col_count, 1)
    ring_y = Ring("col", col_count, 4)

    at = jnp.stack([row_index, col_index]).astype(jnp.int32)
    bits_top = pattern_one[:top_blocks]

    part = share(
        at, pattern_two, pattern_one, panel_two_rows, panel_one_rows, diag_inv_two, diag_inv_one, bw
    )
    blocks = unit_block[:, 0]
    part, blocks = lax.optimization_barrier((part, blocks))
    part = lax.ppermute(part, BOTH, spread_pairs(row_count, col_count))

    capacity = 2 * loadings.shape[0] // total_count
    hits = (blocks[:, None] == jnp.arange(total_count, dtype=jnp.int32)[None, :]).astype(jnp.int32)
    rank = jnp.sum(jnp.cumsum(hits, axis=0) * hits, axis=1) - 1
    slot = blocks * capacity + rank
    packed = jnp.zeros((total_count * capacity, 2 * bw), jnp.bfloat16).at[slot].set(loadings)
    packed = packed.reshape(total_count, capacity, 2 * bw)
    part, packed = lax.optimization_barrier((part, packed))
    held = []
    for step in range(4):
        piece = ring_z.move(part, step) if step else part
        held += [piece, core.move(piece, 1)]

    part, turn, bits_top = lax.optimization_barrier((part, at, bits_top))
    tiles = tiles_of(turn, trail_cov, row_count, bw)
    gram, norm_top = early(bits_top, panel_one_top, diag_inv_two, diag_inv_one)
    packed, tiles, norm_top, held[2], held[4], held[6] = lax.optimization_barrier(
        (packed, tiles, norm_top, held[2], held[4], held[6])
    )
    units = lax.all_to_all(packed, BOTH, split_axis=0, concat_axis=0, tiled=True)
    units = units.reshape(total_count * capacity, 2 * bw)

    tiles, units = lax.optimization_barrier((tiles, units))
    tiles = lax.all_to_all(tiles, "col", split_axis=0, concat_axis=0, tiled=True)
    image_two, image_one, own_two, own_one, *codes = image(at, trail_cov, held, bw)
    far_x, far_y = codes[1], codes[4]
    near = [ring_x.move(codes[0], 1), ring_x.move(codes[2], 3)]
    near += [ring_y.move(codes[3], 1), ring_y.move(codes[5], 3)]
    image_two, image_one, near[0] = lax.optimization_barrier((image_two, image_one, near[0]))
    far = [ring_x.move(far_x, 2), ring_y.move(far_y, 2)]

    keep, give = sums(
        at, pattern_two, pattern_one, panel_two_rows, panel_one_rows, image_two, image_one,
        diag_inv_two, diag_inv_one, bw,
    )
    give, near, far, tiles = lax.optimization_barrier((give, near, far, tiles))
    got = core.move(give, 1)
    codes = [near[0], far[0], near[1], near[2], far[1], near[3]]
    mine, parts = fold_z(at, keep, got)
    parts = lax.all_to_all(
        parts, "row", split_axis=0, concat_axis=0, tiled=True,
        axis_index_groups=[[2 * z + c for z in range(4)] for c in range(2)],
    )
    own_two, *two, own_one, one_a, one_b, one_c = fold_image(at, own_two, own_one, codes)
    codes = ring_y.others(two) + ring_x.others([one_a, one_b, one_c])
    mine, *parts = fold_x(at, mine, parts)
    total = mine
    for part in ring_x.others(parts):
        total = total + part
    total = fold_y(at, [total, *ring_y.others([total] * 3)])
    cov_two, cov_one, cross, tile = rows(
        at, pattern_two, pattern_one, block_panel, own_two, own_one, codes, tiles, norm_top, bw
    )
    value = forms(units, tile, cross)[0].reshape(total_count, capacity)
    total, value = lax.optimization_barrier((total, value))
    parts = [total, *ring_x.others([total] * 3)]
    total = unfold(at, parts)
    whole = []
    for piece in [total, *ring_z.others([total] * 3)]:
        whole += [piece, core.move(piece, 1)]
    returned = lax.all_to_all(value, BOTH, split_axis=0, concat_axis=0, tiled=True)
    diag_two, top_cov, diag_one = small(at, whole, gram, norm_top, bits_top)
    own_panel = jnp.sum(hits * block_panel[None, :], axis=1, keepdims=True)
    within = inner(loadings, own_panel, diag_one)[0]
    within, returned = lax.optimization_barrier((within, returned))
    picked = jnp.dot(
        hits.astype(jnp.float32), returned, precision=lax.Precision.HIGHEST,
        preferred_element_type=jnp.float32,
    )
    at_rank = rank[:, None] == jnp.arange(capacity, dtype=jnp.int32)[None, :]
    variance = jnp.sum(jnp.where(at_rank, picked, 0.0), axis=1)
    variance = variance + within

    mean = exposure * jnp.exp(0.5 * variance)
    seen = counts.astype(jnp.float32)
    scale = shape_par + mean
    shape_grad = (
        lax.digamma(shape_par + seen)
        - lax.digamma(shape_par)
        + jnp.log(shape_par / scale)
        + (mean - seen) / scale
    )
    return (cov_two, top_cov, cov_one, diag_two, diag_one, shape_grad)


def solution(mesh):
    in_specs = (
        P("row", "col"),
        P("row", None),
        P(),
        P(),
        P("row", None),
        P(),
        P(),
        P(),
        P(("row", "col"), None),
        P(("row", "col"), None),
        P(),
        P(("row", "col")),
        P(("row", "col")),
        P(("row", "col")),
    )
    out_specs = (P(("row", "col"), None), P(), P(("row", "col"), None), P(), P(), P(("row", "col")))
    return jax.shard_map(local, mesh=mesh, in_specs=in_specs, out_specs=out_specs, check_vma=False)
```

```python
import functools
import jax
import jax.numpy as jnp
from jax import lax
from jax.experimental import pallas as pl
from jax.experimental.pallas import tpu as pltpu
from jax.sharding import PartitionSpec as P

BOTH = ("row", "col")

LEVELS = 32700.0
STEPS = 64.0
TINY = 1e-33
ROOM = 56 * 1024 * 1024
LIGHT = pl.CostEstimate(flops=1, bytes_accessed=1, transcendentals=0)


def split(value):
    head = value.astype(jnp.bfloat16)
    return head, (value - head.astype(jnp.float32)).astype(jnp.bfloat16)


def dot(left, right):
    return jnp.dot(left, right, preferred_element_type=jnp.float32)


def tdot(left, right):
    return lax.dot_general(
        left, right, (((0,), (0,)), ((), ())), preferred_element_type=jnp.float32
    )


def product(left, right, form=dot):
    left_head, left_tail = split(left)
    right_head, right_tail = split(right)
    return form(left_head, right_head) + (form(left_head, right_tail) + form(left_tail, right_head))


def pack(code):
    half = code.shape[-1] // 2
    return code[..., :half] * 65536 + code[..., half:]


def unpack(word):
    low = lax.shift_right_arithmetic(lax.shift_left(word, 16), 16)
    high = lax.shift_right_arithmetic(word - low, 16)
    return jnp.concatenate([high, low], axis=-1).astype(jnp.float32)


def encode(value, out_ref, *at, first=0):
    rows = value.shape[0]
    largest = jnp.max(jnp.abs(value), axis=0, keepdims=True)
    step = jnp.ceil(jnp.log2(jnp.maximum(largest, TINY)) * STEPS)
    code = jnp.round(value * (jnp.exp2(step * (-1.0 / STEPS)) * LEVELS))
    code = jnp.clip(code, -32767.0, 32767.0).astype(jnp.int32)
    out_ref[(*at, pl.ds(first, rows), slice(None))] = pack(code)
    head = pack(step.astype(jnp.int32))
    out_ref[(*at, pl.ds(first + rows, 8), slice(None))] = jnp.broadcast_to(head, (8, head.shape[1]))


def decode(word):
    rows = word.shape[0] - 8
    scale = jnp.exp2(unpack(word[rows : rows + 1]) * (1.0 / STEPS)) * (1.0 / LEVELS)
    return unpack(word[:rows]) * scale


def chosen(row, col):
    first = lax.rem(2 * row, 4)
    x, y = lax.rem(col, 4), col // 4
    here = (x == first) | (x == lax.rem(first + 3, 4))
    left = (x == first) | (x == first + 1)
    return jnp.where(here, 0, 8) + 2 * y + jnp.where(left, 0, 1)


def share_kernel(at_ref, bits_two_ref, bits_one_ref, two_ref, one_ref, inv_two_ref, inv_one_ref, out_ref):
    block = 16 * at_ref[0] + chosen(at_ref[0], at_ref[1])
    skip = bits_one_ref.shape[0] - bits_two_ref.shape[0]
    keep_two = bits_two_ref[block].astype(jnp.float32)
    keep_one = bits_one_ref[skip + block].astype(jnp.float32)
    encode(product(keep_two * two_ref[...], inv_two_ref[...]), out_ref, 0)
    encode(product(keep_one * one_ref[...], inv_one_ref[...]), out_ref, 1)


def share(at, bits_two, bits_one, panel_two, panel_one, inv_two, inv_one, bw):
    width = inv_two.shape[0]
    rows = pl.BlockSpec((bw, width), lambda i, at, *_: (chosen(at[0], at[1]), 0))
    whole = pl.BlockSpec((width, width), lambda i, *_: (0, 0))
    return pl.pallas_call(
        share_kernel,
        out_shape=jax.ShapeDtypeStruct((2, bw + 8, width // 2), jnp.int32),
        grid_spec=pltpu.PrefetchScalarGridSpec(
            num_scalar_prefetch=3,
            grid=(1,),
            in_specs=[rows, rows, whole, whole],
            out_specs=pl.BlockSpec((2, bw + 8, width // 2), lambda i, *_: (0, 0, 0)),
        ),
        compiler_params=pltpu.CompilerParams(vmem_limit_bytes=ROOM),
        cost_estimate=LIGHT,
    )(at, bits_two, bits_one, panel_two, panel_one, inv_two, inv_one)


def encode_tile(tile, out_ref, block, first):
    bw = tile.shape[0]
    largest = jnp.max(jnp.abs(tile), axis=0, keepdims=True)
    step = jnp.ceil(jnp.log2(jnp.maximum(largest, TINY)) * STEPS)
    code = jnp.round(tile * (jnp.exp2(step * (-1.0 / STEPS)) * LEVELS))
    code = pack(jnp.clip(code, -32767.0, 32767.0).astype(jnp.int32))
    tall, wide = bw // 4, bw // 2
    out_ref[block, pl.ds(first, tall), :] = jnp.concatenate(
        [code[i * tall : (i + 1) * tall] for i in range(4)], axis=1
    )
    head = jnp.broadcast_to(pack(step.astype(jnp.int32)), (8, wide))
    out_ref[block, pl.ds(first + tall, 8), :] = jnp.concatenate([head] * 4, axis=1)


def decode_tile(word, bw):
    tall, wide = bw // 4, bw // 2
    code = jnp.concatenate(
        [word[:tall, i * wide : (i + 1) * wide] for i in range(4)]
        + [word[tall : tall + 8, :wide]],
        axis=0,
    )
    return decode(code)


def tiles_kernel(at_ref, *refs):
    given, out_ref = refs[:-1], refs[-1]
    bw = given[0].shape[0]
    for i, ref in enumerate(given):
        for side in range(2):

            @pl.when(at_ref[1] == 2 * at_ref[0] + side)
            def _():
                encode_tile(ref[...], out_ref, side * len(given) + i, 0)


def tiles_of(at, trail_cov, count, bw):
    def block(j):
        return pl.BlockSpec((bw, bw), lambda i, at: (lax.rem(at[1], 2) * count + j, j))

    shape = (2 * count, bw // 4 + 8, 2 * bw)
    return pl.pallas_call(
        tiles_kernel,
        out_shape=jax.ShapeDtypeStruct(shape, jnp.int32),
        grid_spec=pltpu.PrefetchScalarGridSpec(
            num_scalar_prefetch=1,
            grid=(1,),
            in_specs=[block(j) for j in range(count)],
            out_specs=pl.BlockSpec(shape, lambda i, at: (0, 0, 0)),
        ),
        compiler_params=pltpu.CompilerParams(vmem_limit_bytes=ROOM),
        cost_estimate=LIGHT,
    )(at, *[trail_cov] * count)


def image_kernel(bw, pieces, at_ref, cov_ref, *refs):
    held, (two_ref, one_ref, own_two_ref, own_one_ref) = refs[:pieces], refs[pieces : pieces + 4]
    to_x, to_y = refs[pieces + 4 : pieces + 7], refs[pieces + 7 : pieces + 10]
    head_ref, tail_ref = refs[pieces + 10 :]
    width = two_ref.shape[1]
    step = pl.program_id(0)
    x, y = lax.rem(at_ref[1], 4), at_ref[1] // 4
    here = lax.rem(y + 1 + step, 4)

    @pl.when(step == 0)
    def _():
        z, core = at_ref[0] // 2, lax.rem(at_ref[0], 2)
        for i in range(8):
            block = lax.rem(z + 4 - i // 2, 4) * 2 + lax.rem(core + i, 2)
            rows = pl.ds(pl.multiple_of(block * bw, bw), bw)
            for panel in range(2):
                word = held[i % 2][panel] if i < 2 else held[2 + i % 2][i // 2 - 1, panel]
                head, tail = split(decode(word))
                head_ref[rows, panel * width : (panel + 1) * width] = head
                tail_ref[rows, panel * width : (panel + 1) * width] = tail

    cov_head, cov_tail = split(cov_ref[...])
    for panel, image_ref in enumerate((two_ref, one_ref)):
        at = slice(panel * width, (panel + 1) * width)
        image_ref[...] = dot(cov_head, head_ref[:, at]) + (
            dot(cov_head, tail_ref[:, at]) + dot(cov_tail, head_ref[:, at])
        )
    own_two_ref[here] = two_ref[part_of(x, 0, bw), :]
    for i, ref in enumerate(to_x):
        encode(two_ref[part_of(x, i + 1, bw), :], ref, here)
    for i, ref in enumerate(to_y):

        @pl.when(step == i)
        def _():
            for j in range(4):
                encode(one_ref[j * bw : (j + 1) * bw], ref, j)

    @pl.when(step == 3)
    def _():
        for j in range(4):
            own_one_ref[j] = one_ref[j * bw : (j + 1) * bw]


def image(at, trail_cov, held, bw):
    rows, span = trail_cov.shape
    width = 2 * held[0].shape[-1]
    tile = 4 * bw

    def turned(i, at):
        return (lax.rem(at[1] // 4 + 1 + i, 4), 0)

    def fixed(*shape):
        return pl.BlockSpec(shape, lambda i, at: (0,) * len(shape))

    code = (4, bw + 8, width // 2)
    return pl.pallas_call(
        functools.partial(image_kernel, bw, len(held)),
        out_shape=[jax.ShapeDtypeStruct((rows, width), jnp.float32)] * 2
        + [jax.ShapeDtypeStruct((4, bw, width), jnp.float32)] * 2
        + [jax.ShapeDtypeStruct(code, jnp.int32)] * 6,
        grid_spec=pltpu.PrefetchScalarGridSpec(
            num_scalar_prefetch=1,
            grid=(rows // tile,),
            in_specs=[pl.BlockSpec((tile, span), turned)] + [fixed(*ref.shape) for ref in held],
            out_specs=[pl.BlockSpec((tile, width), turned)] * 2
            + [fixed(4, bw, width)] * 2
            + [fixed(*code)] * 6,
            scratch_shapes=[pltpu.VMEM((span, 2 * width), jnp.bfloat16)] * 2,
        ),
        compiler_params=pltpu.CompilerParams(vmem_limit_bytes=ROOM),
        cost_estimate=LIGHT,
    )(at, trail_cov, *held)


def fold_image_kernel(at_ref, own_two_ref, own_one_ref, *refs):
    codes, outs = (refs[:3], refs[3:6]), (refs[6:10], refs[10:14])
    place = at_ref[1] // 4, lax.rem(at_ref[1], 4)
    for panel, own_ref in enumerate((own_two_ref, own_one_ref)):
        for step, out_ref in enumerate(outs[panel]):
            block = lax.rem(place[panel] + step, 4)
            value = own_ref[block]
            for ref in codes[panel]:
                value = value + decode(ref[block])
            if step:
                encode(value, out_ref)
            else:
                out_ref[...] = value


def fold_image(at, own_two, own_one, codes):
    _, bw, width = own_two.shape
    part, code = ((bw, width), jnp.float32), ((bw + 8, width // 2), jnp.int32)
    return call(fold_image_kernel, at, [own_two, own_one, *codes], ([part] + [code] * 3) * 2)


def sums_kernel(
    bw, at_ref, bits_two_ref, bits_one_ref, two_ref, one_ref, image_two_ref, image_one_ref,
    inv_two_ref, inv_one_ref, keep_ref, give_ref, sums_ref,
):
    step = pl.program_id(0)

    @pl.when(step == 0)
    def _():
        sums_ref[...] = jnp.zeros_like(sums_ref)

    count = two_ref.shape[0] // bw
    first = 16 * at_ref[0] + step * count
    skip = bits_one_ref.shape[0] - bits_two_ref.shape[0]

    def masked(ref, bits_ref, base):
        keep = [
            jnp.full((bw, 1), bits_ref[base + i].astype(jnp.float32)) for i in range(count)
        ]
        keep = jnp.concatenate(keep, axis=0)
        return ref[...] * keep, keep

    two, keep_two = masked(two_ref, bits_two_ref, first)
    one, _ = masked(one_ref, bits_one_ref, skip + first)
    image_two = split(image_two_ref[...] * keep_two)
    image_one = split(image_one_ref[...])
    two, one = split(two), split(one)
    for i, (left, right) in enumerate(((two, image_two), (one, image_two), (one, image_one))):
        sums_ref[i] += tdot(left[0], right[0]) + (tdot(left[0], right[1]) + tdot(left[1], right[0]))

    @pl.when(step == pl.num_programs(0) - 1)
    def _():
        half = keep_ref.shape[1]
        core = lax.rem(at_ref[0], 2)
        for i, inv in enumerate((inv_two_ref, inv_one_ref, inv_one_ref)):
            sums_ref[i] = product(inv[...], sums_ref[i], tdot)
            keep_ref[i] = sums_ref[i, pl.ds(pl.multiple_of(core * half, half), half), :]
            give_ref[i] = sums_ref[i, pl.ds(pl.multiple_of((1 - core) * half, half), half), :]


def sums(at, bits_two, bits_one, panel_two, panel_one, image_two, image_one, inv_two, inv_one, bw, tile=512):
    rows, width = panel_two.shape
    part = pl.BlockSpec((tile, width), lambda i, *_: (i, 0))
    whole = pl.BlockSpec((width, width), lambda i, *_: (0, 0))
    half = (3, width // 2, width)
    return pl.pallas_call(
        functools.partial(sums_kernel, bw),
        out_shape=[jax.ShapeDtypeStruct(half, jnp.float32)] * 2,
        grid_spec=pltpu.PrefetchScalarGridSpec(
            num_scalar_prefetch=3,
            grid=(rows // tile,),
            in_specs=[part] * 4 + [whole] * 2,
            out_specs=[pl.BlockSpec(half, lambda i, *_: (0, 0, 0))] * 2,
            scratch_shapes=[pltpu.VMEM((3, width, width), jnp.float32)],
        ),
        compiler_params=pltpu.CompilerParams(vmem_limit_bytes=ROOM),
        cost_estimate=LIGHT,
    )(at, bits_two, bits_one, panel_two, panel_one, image_two, image_one, inv_two, inv_one)


def call(kernel, at, inputs, shapes):
    vmem = pl.BlockSpec(memory_space=pltpu.VMEM)
    return pl.pallas_call(
        kernel,
        out_shape=[jax.ShapeDtypeStruct(*shape) for shape in shapes],
        in_specs=[pl.BlockSpec(memory_space=pltpu.SMEM)] + [vmem] * len(inputs),
        out_specs=[vmem] * len(shapes),
        compiler_params=pltpu.CompilerParams(vmem_limit_bytes=ROOM),
        cost_estimate=LIGHT,
    )(at, *inputs)


def part_of(place, step, size):
    return pl.ds(pl.multiple_of(lax.rem(place + step, 4) * size, size), size)


def fold_z_kernel(at_ref, own_ref, got_ref, mine_ref, codes_ref):
    size = mine_ref.shape[1]
    z = at_ref[0] // 2
    for step in range(4):
        at = part_of(z, step, size)
        for i in range(3):
            value = own_ref[i, at, :] + got_ref[i, at, :]
            if step:
                encode(value, codes_ref, lax.rem(z + step, 4), i)
            else:
                mine_ref[i] = value


def fold_z(at, own, got):
    count, size, width = own.shape[0], own.shape[1] // 4, own.shape[2]
    return call(
        fold_z_kernel, at, [own, got],
        [((count, size, width), jnp.float32), ((4, count, size + 8, width // 2), jnp.int32)],
    )


def fold_x_kernel(at_ref, own_ref, codes_ref, *refs):
    outs, total_ref = refs[:4], refs[4]
    size = outs[0].shape[1]
    z = at_ref[0] // 2
    for i in range(3):
        value = own_ref[i]
        for step in range(1, 4):
            value = value + decode(codes_ref[lax.rem(z + step, 4), i])
        total_ref[i] = value
    for step, ref in enumerate(outs):
        ref[...] = total_ref[:, part_of(lax.rem(at_ref[1], 4), step, size), :]


def fold_x(at, own, codes):
    count, size, width = own.shape
    part, whole = ((count, size // 4, width), jnp.float32), ((count, size, width), jnp.float32)
    return call(fold_x_kernel, at, [own, codes], [part] * 4 + [whole])[:4]


def fold_y_kernel(at_ref, *refs):
    parts, (out_ref, held_ref) = refs[:4], refs[4:]
    for dy, ref in enumerate(parts):
        held_ref[lax.rem(at_ref[1] // 4 + 4 - dy, 4)] = ref[...]
    out_ref[...] = (held_ref[0] + held_ref[1]) + (held_ref[2] + held_ref[3])


def fold_y(at, parts):
    shape = parts[0].shape
    return call(
        fold_y_kernel, at, parts, [(shape, jnp.float32), ((4, *shape), jnp.float32)]
    )[0]


def unfold_kernel(at_ref, *refs):
    parts, (code_ref, total_ref) = refs[:4], refs[4:]
    size = parts[0].shape[1]
    for dx, ref in enumerate(parts):
        total_ref[:, part_of(lax.rem(at_ref[1], 4) + 4, -dx, size), :] = ref[...]
    for i in range(3):
        encode(total_ref[i], code_ref, i)


def unfold(at, parts):
    count, size, width = parts[0].shape
    return call(
        unfold_kernel, at, parts,
        [
            ((count, 4 * size + 8, width // 2), jnp.int32),
            ((count, 4 * size, width), jnp.float32),
        ],
    )[0]


def rows_kernel(
    at_ref, bits_two_ref, bits_one_ref, panel_ref, own_two_ref, own_one_ref, tiles_ref, top_ref, *refs
):
    codes, (cov_two_ref, cov_one_ref, cross_ref, tile_ref) = refs[:6], refs[6:]
    bw = tile_ref.shape[0]
    tile_ref[...] = decode_tile(tiles_ref[2 * at_ref[0] + at_ref[1] // 8], bw)
    block = 16 * at_ref[0] + at_ref[1]
    skip = bits_one_ref.shape[0] - bits_two_ref.shape[0]
    keep_two = bits_two_ref[block].astype(jnp.float32)
    keep_one = bits_one_ref[skip + block].astype(jnp.float32)

    def total(own_ref, parts):
        value = own_ref[...]
        for ref in parts:
            value = value + decode(ref[...])
        return value

    cov_two = -keep_two * total(own_two_ref, codes[:3])
    cov_two_ref[...] = cov_two
    cov_one = -keep_one * (product(cov_two, top_ref[...]) + total(own_one_ref, codes[3:]))
    cov_one_ref[...] = cov_one
    cross_ref[...] = cov_one_ref[:, pl.ds(pl.multiple_of(panel_ref[block] * bw, bw), bw)]


def rows(at, bits_two, bits_one, panel, own_two, own_one, codes, tiles, norm_top, bw):
    width = norm_top.shape[0]
    smem = pl.BlockSpec(memory_space=pltpu.SMEM)
    vmem = pl.BlockSpec(memory_space=pltpu.VMEM)
    return pl.pallas_call(
        rows_kernel,
        out_shape=[jax.ShapeDtypeStruct((bw, n), jnp.float32) for n in (width, width, bw, bw)],
        in_specs=[smem] * 4 + [vmem] * 10,
        out_specs=[vmem] * 4,
        compiler_params=pltpu.CompilerParams(vmem_limit_bytes=ROOM),
        cost_estimate=LIGHT,
    )(at, bits_two, bits_one, panel, own_two, own_one, tiles, norm_top, *codes)


def small_kernel(at_ref, keep_ref, gram_ref, top_ref, *refs):
    held, (two_ref, top_cov_ref, one_ref, sums_ref) = refs[:2], refs[2:]
    size = held[0].shape[2] - 8
    z, core = at_ref[0] // 2, lax.rem(at_ref[0], 2)
    for i in range(8):
        block = lax.rem(core + i, 2) * 4 + lax.rem(z + 4 - i // 2, 4)
        rows = pl.ds(pl.multiple_of(block * size, size), size)
        for j in range(3):
            sums_ref[j, rows, :] = decode(held[i % 2][i // 2, j])
    top = top_ref[...]
    two = gram_ref[0] + sums_ref[0]
    two_ref[...] = two
    mixed = sums_ref[1]
    keep = jnp.concatenate(
        [
            jnp.full((top.shape[0] // 4, 1), keep_ref[i].astype(jnp.float32)) for i in range(4)
        ],
        axis=0,
    )
    top_cov = -keep * (product(two, top) - mixed.T)
    top_cov_ref[...] = top_cov
    one_ref[...] = gram_ref[1] + sums_ref[2] - product(top, top_cov, tdot) - product(mixed, top)


def small(at, held, gram, norm_top, bits_top):
    width = norm_top.shape[0]
    smem = pl.BlockSpec(memory_space=pltpu.SMEM)
    vmem = pl.BlockSpec(memory_space=pltpu.VMEM)
    return pl.pallas_call(
        small_kernel,
        out_shape=[jax.ShapeDtypeStruct((width, width), jnp.float32)] * 3,
        in_specs=[smem] * 2 + [vmem] * 4,
        out_specs=[vmem] * 3,
        scratch_shapes=[pltpu.VMEM((3, width, width), jnp.float32)],
        compiler_params=pltpu.CompilerParams(vmem_limit_bytes=ROOM),
        cost_estimate=LIGHT,
    )(at, bits_top, gram, norm_top, *held)


def early_kernel(keep_ref, top_rows_ref, inv_two_ref, inv_one_ref, gram_ref, top_ref):
    keep = jnp.concatenate(
        [
            jnp.full((top_rows_ref.shape[0] // 4, 1), keep_ref[i].astype(jnp.float32))
            for i in range(4)
        ],
        axis=0,
    )
    top_ref[...] = product(keep * top_rows_ref[...], inv_one_ref[...])
    gram_ref[0] = product(inv_two_ref[...], inv_two_ref[...], tdot)
    gram_ref[1] = product(inv_one_ref[...], inv_one_ref[...], tdot)


def early(bits_top, panel_top, inv_two, inv_one):
    width = inv_two.shape[0]
    smem = pl.BlockSpec(memory_space=pltpu.SMEM)
    vmem = pl.BlockSpec(memory_space=pltpu.VMEM)
    return pl.pallas_call(
        early_kernel,
        out_shape=[
            jax.ShapeDtypeStruct((2, width, width), jnp.float32),
            jax.ShapeDtypeStruct((width, width), jnp.float32),
        ],
        in_specs=[smem, vmem, vmem, vmem],
        out_specs=[vmem] * 2,
        compiler_params=pltpu.CompilerParams(vmem_limit_bytes=ROOM),
        cost_estimate=LIGHT,
    )(bits_top, panel_top, inv_two, inv_one)


def row_sums(value):
    ones = jnp.ones((8, value.shape[1]), jnp.bfloat16)
    head, tail = split(value)
    form = (((1,), (1,)), ((), ()))
    return lax.dot_general(
        ones, head, form, preferred_element_type=jnp.float32
    ) + lax.dot_general(ones, tail, form, preferred_element_type=jnp.float32)


def forms_kernel(units_ref, tile_ref, cross_ref, out_ref):
    bw = tile_ref.shape[0]
    front, back = units_ref[:, :bw], units_ref[:, bw:]
    middle = jnp.concatenate([*split(tile_ref[...]), *split(2.0 * cross_ref[...])], axis=1)
    both = dot(front, middle)
    value = (both[:, :bw] + both[:, bw : 2 * bw]) * front.astype(jnp.float32)
    value = value + (both[:, 2 * bw : 3 * bw] + both[:, 3 * bw :]) * back.astype(jnp.float32)
    out_ref[...] = row_sums(value)


def forms(units, tile, cross, step=1024):
    count, bw = units.shape[0], tile.shape[0]
    whole = pl.BlockSpec((bw, bw), lambda i: (0, 0))
    return pl.pallas_call(
        forms_kernel,
        out_shape=jax.ShapeDtypeStruct((8, count), jnp.float32),
        grid=(count // step,),
        in_specs=[pl.BlockSpec((step, 2 * bw), lambda i: (i, 0)), whole, whole],
        out_specs=pl.BlockSpec((8, step), lambda i: (0, i)),
        compiler_params=pltpu.CompilerParams(vmem_limit_bytes=ROOM),
        cost_estimate=LIGHT,
    )(units, tile, cross)


def inner_kernel(units_ref, panel_ref, diag_ref, out_ref):
    bw = units_ref.shape[1] // 2
    back = units_ref[:, bw:]
    count = diag_ref.shape[0] // bw
    value = jnp.zeros(back.shape, jnp.float32)
    for p in range(count):
        at = slice(p * bw, (p + 1) * bw)
        both = dot(back, jnp.concatenate(split(diag_ref[at, at]), axis=1))
        value = jnp.where(panel_ref[...] == p, both[:, :bw] + both[:, bw:], value)
    out_ref[...] = row_sums(value * back.astype(jnp.float32))


def inner(units, panel, diag, step=1024):
    count, width = units.shape
    return pl.pallas_call(
        inner_kernel,
        out_shape=jax.ShapeDtypeStruct((8, count), jnp.float32),
        grid=(count // step,),
        in_specs=[
            pl.BlockSpec((step, width), lambda i: (i, 0)),
            pl.BlockSpec((step, 1), lambda i: (i, 0)),
            pl.BlockSpec(diag.shape, lambda i: (0, 0)),
        ],
        out_specs=pl.BlockSpec((8, step), lambda i: (0, i)),
        compiler_params=pltpu.CompilerParams(vmem_limit_bytes=ROOM),
        cost_estimate=LIGHT,
    )(units, panel, diag)


class Ring:
    def __init__(self, axis, size, stride, count=4):
        self.axis, self.size, self.stride, self.count = axis, size, stride, count

    def move(self, value, step):
        pairs = []
        for i in range(self.size):
            at = i // self.stride % self.count
            pairs.append((i, i + ((at + step) % self.count - at) * self.stride))
        return lax.ppermute(value, self.axis, pairs)

    def others(self, parts):
        return [self.move(part, step + 1) for step, part in enumerate(parts)]


def spread_pairs(row_count, col_count):
    pairs = []
    for r in range(row_count):
        for c in range(col_count):
            first, x, y = 2 * r % 4, c % 4, c // 4
            side = 0 if x in (first, (first + 3) % 4) else 1
            j = 2 * y + (0 if x in (first, first + 1) else 1)
            pairs.append((r * col_count + c, j * col_count + 2 * r + side))
    return pairs


def local(
    trail_cov,
    panel_two_rows,
    diag_inv_two,
    panel_one_top,
    panel_one_rows,
    diag_inv_one,
    pattern_two,
    pattern_one,
    loadings,
    unit_block,
    block_panel,
    counts,
    shape_par,
    exposure,
):
    row_count = lax.axis_size("row")
    col_count = lax.axis_size("col")
    total_count = row_count * col_count
    row_index = lax.axis_index("row")
    col_index = lax.axis_index("col")
    width = diag_inv_two.shape[0]
    bw = loadings.shape[1] // 2
    top_blocks = width // bw
    core = Ring("row", row_count, 1, 2)
    ring_z = Ring("row", row_count, 2)
    ring_x = Ring("col", col_count, 1)
    ring_y = Ring("col", col_count, 4)

    at = jnp.stack([row_index, col_index]).astype(jnp.int32)
    bits_top = pattern_one[:top_blocks]

    part = share(
        at, pattern_two, pattern_one, panel_two_rows, panel_one_rows, diag_inv_two, diag_inv_one, bw
    )
    blocks = unit_block[:, 0]
    part, blocks = lax.optimization_barrier((part, blocks))
    part = lax.ppermute(part, BOTH, spread_pairs(row_count, col_count))

    capacity = 2 * loadings.shape[0] // total_count
    hits = (blocks[:, None] == jnp.arange(total_count, dtype=jnp.int32)[None, :]).astype(jnp.int32)
    rank = jnp.sum(jnp.cumsum(hits, axis=0) * hits, axis=1) - 1
    slot = blocks * capacity + rank
    packed = jnp.zeros((total_count * capacity, 2 * bw), jnp.bfloat16).at[slot].set(loadings)
    packed = packed.reshape(total_count, capacity, 2 * bw)
    part, packed = lax.optimization_barrier((part, packed))
    pieces = ring_z.others([part] * 3)
    part, turn, bits_top = lax.optimization_barrier((part, at, bits_top))
    tiles = tiles_of(turn, trail_cov, row_count, bw)
    gram, norm_top = early(bits_top, panel_one_top, diag_inv_two, diag_inv_one)
    packed, tiles, norm_top, pieces = lax.optimization_barrier((packed, tiles, norm_top, pieces))
    far = jnp.stack(pieces)
    held = [part, core.move(part, 1), far, core.move(far, 1)]
    units = lax.all_to_all(packed, BOTH, split_axis=0, concat_axis=0, tiled=True)
    units = units.reshape(total_count * capacity, 2 * bw)

    tiles, units = lax.optimization_barrier((tiles, units))
    tiles = lax.all_to_all(tiles, "col", split_axis=0, concat_axis=0, tiled=True)
    image_two, image_one, own_two, own_one, *codes = image(at, trail_cov, held, bw)
    far_x, far_y = codes[1], codes[4]
    near = [ring_x.move(codes[0], 1), ring_x.move(codes[2], 3)]
    near += [ring_y.move(codes[3], 1), ring_y.move(codes[5], 3)]
    image_two, image_one, near[0] = lax.optimization_barrier((image_two, image_one, near[0]))
    far = [ring_x.move(far_x, 2), ring_y.move(far_y, 2)]

    keep, give = sums(
        at, pattern_two, pattern_one, panel_two_rows, panel_one_rows, image_two, image_one,
        diag_inv_two, diag_inv_one, bw,
    )
    give, near, far, tiles = lax.optimization_barrier((give, near, far, tiles))
    got = core.move(give, 1)
    codes = [near[0], far[0], near[1], near[2], far[1], near[3]]
    mine, parts = fold_z(at, keep, got)
    parts = lax.all_to_all(
        parts, "row", split_axis=0, concat_axis=0, tiled=True,
        axis_index_groups=[[2 * z + c for z in range(4)] for c in range(2)],
    )
    own_two, *two, own_one, one_a, one_b, one_c = fold_image(at, own_two, own_one, codes)
    codes = ring_y.others(two) + ring_x.others([one_a, one_b, one_c])
    mine, *parts = fold_x(at, mine, parts)
    total = mine
    for part in ring_x.others(parts):
        total = total + part
    total = fold_y(at, [total, *ring_y.others([total] * 3)])
    cov_two, cov_one, cross, tile = rows(
        at, pattern_two, pattern_one, block_panel, own_two, own_one, codes, tiles, norm_top, bw
    )
    value = forms(units, tile, cross)[0].reshape(total_count, capacity)
    total, value = lax.optimization_barrier((total, value))
    parts = [total, *ring_x.others([total] * 3)]
    total = unfold(at, parts)
    whole = jnp.stack([total, *ring_z.others([total] * 3)])
    whole = [whole, core.move(whole, 1)]
    returned = lax.all_to_all(value, BOTH, split_axis=0, concat_axis=0, tiled=True)
    diag_two, top_cov, diag_one = small(at, whole, gram, norm_top, bits_top)
    own_panel = jnp.sum(hits * block_panel[None, :], axis=1, keepdims=True)
    within = inner(loadings, own_panel, diag_one)[0]
    within, returned = lax.optimization_barrier((within, returned))
    picked = jnp.dot(
        hits.astype(jnp.float32), returned, precision=lax.Precision.HIGHEST,
        preferred_element_type=jnp.float32,
    )
    at_rank = rank[:, None] == jnp.arange(capacity, dtype=jnp.int32)[None, :]
    variance = jnp.sum(jnp.where(at_rank, picked, 0.0), axis=1)
    variance = variance + within

    mean = exposure * jnp.exp(0.5 * variance)
    seen = counts.astype(jnp.float32)
    scale = shape_par + mean
    shape_grad = (
        lax.digamma(shape_par + seen)
        - lax.digamma(shape_par)
        + jnp.log(shape_par / scale)
        + (mean - seen) / scale
    )
    return (cov_two, top_cov, cov_one, diag_two, diag_one, shape_grad)


def solution(mesh):
    in_specs = (
        P("row", "col"),
        P("row", None),
        P(),
        P(),
        P("row", None),
        P(),
        P(),
        P(),
        P(("row", "col"), None),
        P(("row", "col"), None),
        P(),
        P(("row", "col")),
        P(("row", "col")),
        P(("row", "col")),
    )
    out_specs = (P(("row", "col"), None), P(), P(("row", "col"), None), P(), P(), P(("row", "col")))
    return jax.shard_map(local, mesh=mesh, in_specs=in_specs, out_specs=out_specs, check_vma=False)
```

```python
import functools
import jax
import jax.numpy as jnp
from jax import lax
from jax.experimental import pallas as pl
from jax.experimental.pallas import tpu as pltpu
from jax.sharding import PartitionSpec as P

BOTH = ("row", "col")

LEVELS = 32700.0
STEPS = 64.0
TINY = 1e-33
ROOM = 56 * 1024 * 1024
LIGHT = pl.CostEstimate(flops=1, bytes_accessed=1, transcendentals=0)


def split(value):
    head = value.astype(jnp.bfloat16)
    return head, (value - head.astype(jnp.float32)).astype(jnp.bfloat16)


def dot(left, right):
    return jnp.dot(left, right, preferred_element_type=jnp.float32)


def tdot(left, right):
    return lax.dot_general(
        left, right, (((0,), (0,)), ((), ())), preferred_element_type=jnp.float32
    )


def product(left, right, form=dot):
    left_head, left_tail = split(left)
    right_head, right_tail = split(right)
    return form(left_head, right_head) + (form(left_head, right_tail) + form(left_tail, right_head))


def pack(code):
    half = code.shape[-1] // 2
    return code[..., :half] * 65536 + code[..., half:]


def unpack(word):
    low = lax.shift_right_arithmetic(lax.shift_left(word, 16), 16)
    high = lax.shift_right_arithmetic(word - low, 16)
    return jnp.concatenate([high, low], axis=-1).astype(jnp.float32)


def encode(value, out_ref, *at, first=0):
    rows = value.shape[0]
    largest = jnp.max(jnp.abs(value), axis=0, keepdims=True)
    step = jnp.ceil(jnp.log2(jnp.maximum(largest, TINY)) * STEPS)
    code = jnp.round(value * (jnp.exp2(step * (-1.0 / STEPS)) * LEVELS))
    code = jnp.clip(code, -32767.0, 32767.0).astype(jnp.int32)
    out_ref[(*at, pl.ds(first, rows), slice(None))] = pack(code)
    head = pack(step.astype(jnp.int32))
    out_ref[(*at, pl.ds(first + rows, 8), slice(None))] = jnp.broadcast_to(head, (8, head.shape[1]))


def decode(word):
    rows = word.shape[0] - 8
    scale = jnp.exp2(unpack(word[rows : rows + 1]) * (1.0 / STEPS)) * (1.0 / LEVELS)
    return unpack(word[:rows]) * scale


def chosen(row, col):
    first = lax.rem(2 * row, 4)
    x, y = lax.rem(col, 4), col // 4
    here = (x == first) | (x == lax.rem(first + 3, 4))
    left = (x == first) | (x == first + 1)
    return jnp.where(here, 0, 8) + 2 * y + jnp.where(left, 0, 1)


def share_kernel(at_ref, bits_two_ref, bits_one_ref, two_ref, one_ref, inv_two_ref, inv_one_ref, out_ref):
    block = 16 * at_ref[0] + chosen(at_ref[0], at_ref[1])
    skip = bits_one_ref.shape[0] - bits_two_ref.shape[0]
    keep_two = bits_two_ref[block].astype(jnp.float32)
    keep_one = bits_one_ref[skip + block].astype(jnp.float32)
    encode(product(keep_two * two_ref[...], inv_two_ref[...]), out_ref, 0)
    encode(product(keep_one * one_ref[...], inv_one_ref[...]), out_ref, 1)


def share(at, bits_two, bits_one, panel_two, panel_one, inv_two, inv_one, bw):
    width = inv_two.shape[0]
    rows = pl.BlockSpec((bw, width), lambda i, at, *_: (chosen(at[0], at[1]), 0))
    whole = pl.BlockSpec((width, width), lambda i, *_: (0, 0))
    return pl.pallas_call(
        share_kernel,
        out_shape=jax.ShapeDtypeStruct((2, bw + 8, width // 2), jnp.int32),
        grid_spec=pltpu.PrefetchScalarGridSpec(
            num_scalar_prefetch=3,
            grid=(1,),
            in_specs=[rows, rows, whole, whole],
            out_specs=pl.BlockSpec((2, bw + 8, width // 2), lambda i, *_: (0, 0, 0)),
        ),
        compiler_params=pltpu.CompilerParams(vmem_limit_bytes=ROOM),
        cost_estimate=LIGHT,
    )(at, bits_two, bits_one, panel_two, panel_one, inv_two, inv_one)


def encode_tile(tile, out_ref, block, first):
    bw = tile.shape[0]
    largest = jnp.max(jnp.abs(tile), axis=0, keepdims=True)
    step = jnp.ceil(jnp.log2(jnp.maximum(largest, TINY)) * STEPS)
    code = jnp.round(tile * (jnp.exp2(step * (-1.0 / STEPS)) * LEVELS))
    code = pack(jnp.clip(code, -32767.0, 32767.0).astype(jnp.int32))
    tall, wide = bw // 4, bw // 2
    out_ref[block, pl.ds(first, tall), :] = jnp.concatenate(
        [code[i * tall : (i + 1) * tall] for i in range(4)], axis=1
    )
    head = jnp.broadcast_to(pack(step.astype(jnp.int32)), (8, wide))
    out_ref[block, pl.ds(first + tall, 8), :] = jnp.concatenate([head] * 4, axis=1)


def decode_tile(word, bw):
    tall, wide = bw // 4, bw // 2
    code = jnp.concatenate(
        [word[:tall, i * wide : (i + 1) * wide] for i in range(4)]
        + [word[tall : tall + 8, :wide]],
        axis=0,
    )
    return decode(code)


def tiles_kernel(at_ref, *refs):
    given, out_ref = refs[:-1], refs[-1]
    bw = given[0].shape[0]
    side = at_ref[1] - 2 * at_ref[0]

    @pl.when((side == 0) | (side == 1))
    def _():
        for i, ref in enumerate(given):
            encode_tile(ref[...], out_ref, side * len(given) + i, 0)


def tiles_of(at, trail_cov, count, bw):
    def block(j):
        return pl.BlockSpec((bw, bw), lambda i, at: (lax.rem(at[1], 2) * count + j, j))

    shape = (2 * count, bw // 4 + 8, 2 * bw)
    return pl.pallas_call(
        tiles_kernel,
        out_shape=jax.ShapeDtypeStruct(shape, jnp.int32),
        grid_spec=pltpu.PrefetchScalarGridSpec(
            num_scalar_prefetch=1,
            grid=(1,),
            in_specs=[block(j) for j in range(count)],
            out_specs=pl.BlockSpec(shape, lambda i, at: (0, 0, 0)),
        ),
        compiler_params=pltpu.CompilerParams(vmem_limit_bytes=ROOM),
        cost_estimate=LIGHT,
    )(at, *[trail_cov] * count)


def image_kernel(bw, pieces, at_ref, cov_ref, *refs):
    held, (two_ref, one_ref, own_two_ref, own_one_ref) = refs[:pieces], refs[pieces : pieces + 4]
    to_x, to_y = refs[pieces + 4 : pieces + 7], refs[pieces + 7 : pieces + 10]
    head_ref, tail_ref = refs[pieces + 10 :]
    width = two_ref.shape[1]
    step = pl.program_id(0)
    x, y = lax.rem(at_ref[1], 4), at_ref[1] // 4
    here = lax.rem(y + 1 + step, 4)

    @pl.when(step == 0)
    def _():
        z, core = at_ref[0] // 2, lax.rem(at_ref[0], 2)
        def place(word, flip, behind, panel):
            block = lax.rem(z + 4 - behind, 4) * 2 + lax.rem(core + flip, 2)
            rows = pl.ds(pl.multiple_of(block * bw, bw), bw)
            head, tail = split(decode(word))
            head_ref[rows, panel * width : (panel + 1) * width] = head
            tail_ref[rows, panel * width : (panel + 1) * width] = tail

        for flip in range(2):
            for panel in range(2):
                place(held[flip][panel], flip, 0, panel)

                @pl.loop(0, 3)
                def _(d, flip=flip, panel=panel):
                    place(held[2 + flip][d, panel], flip, d + 1, panel)

    cov_head, cov_tail = split(cov_ref[...])
    for panel, image_ref in enumerate((two_ref, one_ref)):
        at = slice(panel * width, (panel + 1) * width)
        image_ref[...] = dot(cov_head, head_ref[:, at]) + (
            dot(cov_head, tail_ref[:, at]) + dot(cov_tail, head_ref[:, at])
        )
    own_two_ref[here] = two_ref[part_of(x, 0, bw), :]
    for i, ref in enumerate(to_x):
        encode(two_ref[part_of(x, i + 1, bw), :], ref, here)
    for i, ref in enumerate(to_y):

        @pl.when(step == i)
        def _():
            @pl.loop(0, 4)
            def _(j):
                encode(one_ref[pl.ds(pl.multiple_of(j * bw, bw), bw), :], ref, j)

    @pl.when(step == 3)
    def _():
        for j in range(4):
            own_one_ref[j] = one_ref[j * bw : (j + 1) * bw]


def image(at, trail_cov, held, bw):
    rows, span = trail_cov.shape
    width = 2 * held[0].shape[-1]
    tile = 4 * bw

    def turned(i, at):
        return (lax.rem(at[1] // 4 + 1 + i, 4), 0)

    def fixed(*shape):
        return pl.BlockSpec(shape, lambda i, at: (0,) * len(shape))

    code = (4, bw + 8, width // 2)
    return pl.pallas_call(
        functools.partial(image_kernel, bw, len(held)),
        out_shape=[jax.ShapeDtypeStruct((rows, width), jnp.float32)] * 2
        + [jax.ShapeDtypeStruct((4, bw, width), jnp.float32)] * 2
        + [jax.ShapeDtypeStruct(code, jnp.int32)] * 6,
        grid_spec=pltpu.PrefetchScalarGridSpec(
            num_scalar_prefetch=1,
            grid=(rows // tile,),
            in_specs=[pl.BlockSpec((tile, span), turned)] + [fixed(*ref.shape) for ref in held],
            out_specs=[pl.BlockSpec((tile, width), turned)] * 2
            + [fixed(4, bw, width)] * 2
            + [fixed(*code)] * 6,
            scratch_shapes=[pltpu.VMEM((span, 2 * width), jnp.bfloat16)] * 2,
        ),
        compiler_params=pltpu.CompilerParams(vmem_limit_bytes=ROOM),
        cost_estimate=LIGHT,
    )(at, trail_cov, *held)


def fold_image_kernel(at_ref, own_two_ref, own_one_ref, *refs):
    codes, outs, total_ref = (refs[:3], refs[3:6]), (refs[6:10], refs[10:14]), refs[14]
    place = at_ref[1] // 4, lax.rem(at_ref[1], 4)
    for panel, own_ref in enumerate((own_two_ref, own_one_ref)):

        @pl.loop(0, 4)
        def _(block, own_ref=own_ref, panel=panel):
            value = own_ref[block]
            for ref in codes[panel]:
                value = value + decode(ref[block])
            total_ref[block] = value

        for step, out_ref in enumerate(outs[panel]):
            value = total_ref[lax.rem(place[panel] + step, 4)]
            if step:
                encode(value, out_ref)
            else:
                out_ref[...] = value


def fold_image(at, own_two, own_one, codes):
    _, bw, width = own_two.shape
    part, code = ((bw, width), jnp.float32), ((bw + 8, width // 2), jnp.int32)
    shapes = ([part] + [code] * 3) * 2 + [((4, bw, width), jnp.float32)]
    return call(fold_image_kernel, at, [own_two, own_one, *codes], shapes)[:8]


def sums_kernel(
    bw, at_ref, bits_two_ref, bits_one_ref, two_ref, one_ref, image_two_ref, image_one_ref,
    inv_two_ref, inv_one_ref, keep_ref, give_ref, sums_ref,
):
    step = pl.program_id(0)

    @pl.when(step == 0)
    def _():
        sums_ref[...] = jnp.zeros_like(sums_ref)

    count = two_ref.shape[0] // bw
    first = 16 * at_ref[0] + step * count
    skip = bits_one_ref.shape[0] - bits_two_ref.shape[0]

    def masked(ref, bits_ref, base):
        keep = [
            jnp.full((bw, 1), bits_ref[base + i].astype(jnp.float32)) for i in range(count)
        ]
        keep = jnp.concatenate(keep, axis=0)
        return ref[...] * keep, keep

    two, keep_two = masked(two_ref, bits_two_ref, first)
    one, _ = masked(one_ref, bits_one_ref, skip + first)
    image_two = split(image_two_ref[...] * keep_two)
    image_one = split(image_one_ref[...])
    two, one = split(two), split(one)
    for i, (left, right) in enumerate(((two, image_two), (one, image_two), (one, image_one))):
        sums_ref[i] += tdot(left[0], right[0]) + (tdot(left[0], right[1]) + tdot(left[1], right[0]))

    @pl.when(step == pl.num_programs(0) - 1)
    def _():
        half = keep_ref.shape[1]
        core = lax.rem(at_ref[0], 2)
        for i, inv in enumerate((inv_two_ref, inv_one_ref, inv_one_ref)):
            sums_ref[i] = product(inv[...], sums_ref[i], tdot)
            keep_ref[i] = sums_ref[i, pl.ds(pl.multiple_of(core * half, half), half), :]
            give_ref[i] = sums_ref[i, pl.ds(pl.multiple_of((1 - core) * half, half), half), :]


def sums(at, bits_two, bits_one, panel_two, panel_one, image_two, image_one, inv_two, inv_one, bw, tile=512):
    rows, width = panel_two.shape
    part = pl.BlockSpec((tile, width), lambda i, *_: (i, 0))
    whole = pl.BlockSpec((width, width), lambda i, *_: (0, 0))
    half = (3, width // 2, width)
    return pl.pallas_call(
        functools.partial(sums_kernel, bw),
        out_shape=[jax.ShapeDtypeStruct(half, jnp.float32)] * 2,
        grid_spec=pltpu.PrefetchScalarGridSpec(
            num_scalar_prefetch=3,
            grid=(rows // tile,),
            in_specs=[part] * 4 + [whole] * 2,
            out_specs=[pl.BlockSpec(half, lambda i, *_: (0, 0, 0))] * 2,
            scratch_shapes=[pltpu.VMEM((3, width, width), jnp.float32)],
        ),
        compiler_params=pltpu.CompilerParams(vmem_limit_bytes=ROOM),
        cost_estimate=LIGHT,
    )(at, bits_two, bits_one, panel_two, panel_one, image_two, image_one, inv_two, inv_one)


def call(kernel, at, inputs, shapes):
    vmem = pl.BlockSpec(memory_space=pltpu.VMEM)
    return pl.pallas_call(
        kernel,
        out_shape=[jax.ShapeDtypeStruct(*shape) for shape in shapes],
        in_specs=[pl.BlockSpec(memory_space=pltpu.SMEM)] + [vmem] * len(inputs),
        out_specs=[vmem] * len(shapes),
        compiler_params=pltpu.CompilerParams(vmem_limit_bytes=ROOM),
        cost_estimate=LIGHT,
    )(at, *inputs)


def part_of(place, step, size):
    return pl.ds(pl.multiple_of(lax.rem(place + step, 4) * size, size), size)


def fold_z_kernel(at_ref, own_ref, got_ref, mine_ref, codes_ref):
    size = mine_ref.shape[1]
    z = at_ref[0] // 2
    for step in range(4):
        at = part_of(z, step, size)

        @pl.loop(0, 3)
        def _(i, step=step, at=at):
            value = own_ref[i, at, :] + got_ref[i, at, :]
            if step:
                encode(value, codes_ref, lax.rem(z + step, 4), i)
            else:
                mine_ref[i] = value


def fold_z(at, own, got):
    count, size, width = own.shape[0], own.shape[1] // 4, own.shape[2]
    return call(
        fold_z_kernel, at, [own, got],
        [((count, size, width), jnp.float32), ((4, count, size + 8, width // 2), jnp.int32)],
    )


def fold_x_kernel(at_ref, own_ref, codes_ref, *refs):
    outs, total_ref = refs[:4], refs[4]
    size = outs[0].shape[1]
    z = at_ref[0] // 2

    @pl.loop(0, 3)
    def _(i):
        value = own_ref[i]
        for step in range(1, 4):
            value = value + decode(codes_ref[lax.rem(z + step, 4), i])
        total_ref[i] = value

    for step, ref in enumerate(outs):
        ref[...] = total_ref[:, part_of(lax.rem(at_ref[1], 4), step, size), :]


def fold_x(at, own, codes):
    count, size, width = own.shape
    part, whole = ((count, size // 4, width), jnp.float32), ((count, size, width), jnp.float32)
    return call(fold_x_kernel, at, [own, codes], [part] * 4 + [whole])[:4]


def fold_y_kernel(at_ref, *refs):
    parts, (out_ref, held_ref) = refs[:4], refs[4:]
    for dy, ref in enumerate(parts):
        held_ref[lax.rem(at_ref[1] // 4 + 4 - dy, 4)] = ref[...]
    out_ref[...] = (held_ref[0] + held_ref[1]) + (held_ref[2] + held_ref[3])


def fold_y(at, parts):
    shape = parts[0].shape
    return call(
        fold_y_kernel, at, parts, [(shape, jnp.float32), ((4, *shape), jnp.float32)]
    )[0]


def unfold_kernel(at_ref, *refs):
    parts, (code_ref, total_ref) = refs[:4], refs[4:]
    size = parts[0].shape[1]
    for dx, ref in enumerate(parts):
        total_ref[:, part_of(lax.rem(at_ref[1], 4) + 4, -dx, size), :] = ref[...]

    @pl.loop(0, 3)
    def _(i):
        encode(total_ref[i], code_ref, i)


def unfold(at, parts):
    count, size, width = parts[0].shape
    return call(
        unfold_kernel, at, parts,
        [
            ((count, 4 * size + 8, width // 2), jnp.int32),
            ((count, 4 * size, width), jnp.float32),
        ],
    )[0]


def rows_kernel(
    at_ref, bits_two_ref, bits_one_ref, panel_ref, own_two_ref, own_one_ref, tiles_ref, top_ref, *refs
):
    codes, (cov_two_ref, cov_one_ref, cross_ref, tile_ref) = refs[:6], refs[6:]
    bw = tile_ref.shape[0]
    tile_ref[...] = decode_tile(tiles_ref[2 * at_ref[0] + at_ref[1] // 8], bw)
    block = 16 * at_ref[0] + at_ref[1]
    skip = bits_one_ref.shape[0] - bits_two_ref.shape[0]
    keep_two = bits_two_ref[block].astype(jnp.float32)
    keep_one = bits_one_ref[skip + block].astype(jnp.float32)

    def total(own_ref, parts):
        value = own_ref[...]
        for ref in parts:
            value = value + decode(ref[...])
        return value

    cov_two = -keep_two * total(own_two_ref, codes[:3])
    cov_two_ref[...] = cov_two
    cov_one = -keep_one * (product(cov_two, top_ref[...]) + total(own_one_ref, codes[3:]))
    cov_one_ref[...] = cov_one
    cross_ref[...] = cov_one_ref[:, pl.ds(pl.multiple_of(panel_ref[block] * bw, bw), bw)]


def rows(at, bits_two, bits_one, panel, own_two, own_one, codes, tiles, norm_top, bw):
    width = norm_top.shape[0]
    smem = pl.BlockSpec(memory_space=pltpu.SMEM)
    vmem = pl.BlockSpec(memory_space=pltpu.VMEM)
    return pl.pallas_call(
        rows_kernel,
        out_shape=[jax.ShapeDtypeStruct((bw, n), jnp.float32) for n in (width, width, bw, bw)],
        in_specs=[smem] * 4 + [vmem] * 10,
        out_specs=[vmem] * 4,
        compiler_params=pltpu.CompilerParams(vmem_limit_bytes=ROOM),
        cost_estimate=LIGHT,
    )(at, bits_two, bits_one, panel, own_two, own_one, tiles, norm_top, *codes)


def small_kernel(at_ref, keep_ref, gram_ref, top_ref, *refs):
    held, (two_ref, top_cov_ref, one_ref, sums_ref) = refs[:2], refs[2:]
    size = held[0].shape[2] - 8
    z, core = at_ref[0] // 2, lax.rem(at_ref[0], 2)
    for flip in range(2):

        @pl.loop(0, 4)
        def _(d, flip=flip):
            block = lax.rem(core + flip, 2) * 4 + lax.rem(z + 4 - d, 4)
            rows = pl.ds(pl.multiple_of(block * size, size), size)
            for j in range(3):
                sums_ref[j, rows, :] = decode(held[flip][d, j])
    top = top_ref[...]
    two = gram_ref[0] + sums_ref[0]
    two_ref[...] = two
    mixed = sums_ref[1]
    keep = jnp.concatenate(
        [
            jnp.full((top.shape[0] // 4, 1), keep_ref[i].astype(jnp.float32)) for i in range(4)
        ],
        axis=0,
    )
    top_cov = -keep * (product(two, top) - mixed.T)
    top_cov_ref[...] = top_cov
    one_ref[...] = gram_ref[1] + sums_ref[2] - product(top, top_cov, tdot) - product(mixed, top)


def small(at, held, gram, norm_top, bits_top):
    width = norm_top.shape[0]
    smem = pl.BlockSpec(memory_space=pltpu.SMEM)
    vmem = pl.BlockSpec(memory_space=pltpu.VMEM)
    return pl.pallas_call(
        small_kernel,
        out_shape=[jax.ShapeDtypeStruct((width, width), jnp.float32)] * 3,
        in_specs=[smem] * 2 + [vmem] * 4,
        out_specs=[vmem] * 3,
        scratch_shapes=[pltpu.VMEM((3, width, width), jnp.float32)],
        compiler_params=pltpu.CompilerParams(vmem_limit_bytes=ROOM),
        cost_estimate=LIGHT,
    )(at, bits_top, gram, norm_top, *held)


def early_kernel(keep_ref, top_rows_ref, inv_two_ref, inv_one_ref, gram_ref, top_ref):
    keep = jnp.concatenate(
        [
            jnp.full((top_rows_ref.shape[0] // 4, 1), keep_ref[i].astype(jnp.float32))
            for i in range(4)
        ],
        axis=0,
    )
    top_ref[...] = product(keep * top_rows_ref[...], inv_one_ref[...])
    gram_ref[0] = product(inv_two_ref[...], inv_two_ref[...], tdot)
    gram_ref[1] = product(inv_one_ref[...], inv_one_ref[...], tdot)


def early(bits_top, panel_top, inv_two, inv_one):
    width = inv_two.shape[0]
    smem = pl.BlockSpec(memory_space=pltpu.SMEM)
    vmem = pl.BlockSpec(memory_space=pltpu.VMEM)
    return pl.pallas_call(
        early_kernel,
        out_shape=[
            jax.ShapeDtypeStruct((2, width, width), jnp.float32),
            jax.ShapeDtypeStruct((width, width), jnp.float32),
        ],
        in_specs=[smem, vmem, vmem, vmem],
        out_specs=[vmem] * 2,
        compiler_params=pltpu.CompilerParams(vmem_limit_bytes=ROOM),
        cost_estimate=LIGHT,
    )(bits_top, panel_top, inv_two, inv_one)


def row_sums(value):
    ones = jnp.ones((8, value.shape[1]), jnp.bfloat16)
    head, tail = split(value)
    form = (((1,), (1,)), ((), ()))
    return lax.dot_general(
        ones, head, form, preferred_element_type=jnp.float32
    ) + lax.dot_general(ones, tail, form, preferred_element_type=jnp.float32)


def forms_kernel(units_ref, tile_ref, cross_ref, out_ref):
    bw = tile_ref.shape[0]
    front, back = units_ref[:, :bw], units_ref[:, bw:]
    middle = jnp.concatenate([*split(tile_ref[...]), *split(2.0 * cross_ref[...])], axis=1)
    both = dot(front, middle)
    value = (both[:, :bw] + both[:, bw : 2 * bw]) * front.astype(jnp.float32)
    value = value + (both[:, 2 * bw : 3 * bw] + both[:, 3 * bw :]) * back.astype(jnp.float32)
    out_ref[...] = row_sums(value)


def forms(units, tile, cross, step=1024):
    count, bw = units.shape[0], tile.shape[0]
    whole = pl.BlockSpec((bw, bw), lambda i: (0, 0))
    return pl.pallas_call(
        forms_kernel,
        out_shape=jax.ShapeDtypeStruct((8, count), jnp.float32),
        grid=(count // step,),
        in_specs=[pl.BlockSpec((step, 2 * bw), lambda i: (i, 0)), whole, whole],
        out_specs=pl.BlockSpec((8, step), lambda i: (0, i)),
        compiler_params=pltpu.CompilerParams(vmem_limit_bytes=ROOM),
        cost_estimate=LIGHT,
    )(units, tile, cross)


def inner_kernel(units_ref, panel_ref, diag_ref, out_ref):
    bw = units_ref.shape[1] // 2
    back = units_ref[:, bw:]
    count = diag_ref.shape[0] // bw
    value = jnp.zeros(back.shape, jnp.float32)
    for p in range(count):
        at = slice(p * bw, (p + 1) * bw)
        both = dot(back, jnp.concatenate(split(diag_ref[at, at]), axis=1))
        value = jnp.where(panel_ref[...] == p, both[:, :bw] + both[:, bw:], value)
    out_ref[...] = row_sums(value * back.astype(jnp.float32))


def inner(units, panel, diag, step=1024):
    count, width = units.shape
    return pl.pallas_call(
        inner_kernel,
        out_shape=jax.ShapeDtypeStruct((8, count), jnp.float32),
        grid=(count // step,),
        in_specs=[
            pl.BlockSpec((step, width), lambda i: (i, 0)),
            pl.BlockSpec((step, 1), lambda i: (i, 0)),
            pl.BlockSpec(diag.shape, lambda i: (0, 0)),
        ],
        out_specs=pl.BlockSpec((8, step), lambda i: (0, i)),
        compiler_params=pltpu.CompilerParams(vmem_limit_bytes=ROOM),
        cost_estimate=LIGHT,
    )(units, panel, diag)


class Ring:
    def __init__(self, axis, size, stride, count=4):
        self.axis, self.size, self.stride, self.count = axis, size, stride, count

    def move(self, value, step):
        pairs = []
        for i in range(self.size):
            at = i // self.stride % self.count
            pairs.append((i, i + ((at + step) % self.count - at) * self.stride))
        return lax.ppermute(value, self.axis, pairs)

    def others(self, parts):
        return [self.move(part, step + 1) for step, part in enumerate(parts)]


def spread_pairs(row_count, col_count):
    pairs = []
    for r in range(row_count):
        for c in range(col_count):
            first, x, y = 2 * r % 4, c % 4, c // 4
            side = 0 if x in (first, (first + 3) % 4) else 1
            j = 2 * y + (0 if x in (first, first + 1) else 1)
            pairs.append((r * col_count + c, j * col_count + 2 * r + side))
    return pairs


def local(
    trail_cov,
    panel_two_rows,
    diag_inv_two,
    panel_one_top,
    panel_one_rows,
    diag_inv_one,
    pattern_two,
    pattern_one,
    loadings,
    unit_block,
    block_panel,
    counts,
    shape_par,
    exposure,
):
    row_count = lax.axis_size("row")
    col_count = lax.axis_size("col")
    total_count = row_count * col_count
    row_index = lax.axis_index("row")
    col_index = lax.axis_index("col")
    width = diag_inv_two.shape[0]
    bw = loadings.shape[1] // 2
    top_blocks = width // bw
    core = Ring("row", row_count, 1, 2)
    ring_z = Ring("row", row_count, 2)
    ring_x = Ring("col", col_count, 1)
    ring_y = Ring("col", col_count, 4)

    at = jnp.stack([row_index, col_index]).astype(jnp.int32)
    bits_top = pattern_one[:top_blocks]

    part = share(
        at, pattern_two, pattern_one, panel_two_rows, panel_one_rows, diag_inv_two, diag_inv_one, bw
    )
    blocks = unit_block[:, 0]
    part, blocks = lax.optimization_barrier((part, blocks))
    part = lax.ppermute(part, BOTH, spread_pairs(row_count, col_count))

    capacity = 2 * loadings.shape[0] // total_count
    hits = (blocks[:, None] == jnp.arange(total_count, dtype=jnp.int32)[None, :]).astype(jnp.int32)
    rank = jnp.sum(jnp.cumsum(hits, axis=0) * hits, axis=1) - 1
    slot = blocks * capacity + rank
    packed = jnp.zeros((total_count * capacity, 2 * bw), jnp.bfloat16).at[slot].set(loadings)
    packed = packed.reshape(total_count, capacity, 2 * bw)
    part, packed = lax.optimization_barrier((part, packed))
    pieces = ring_z.others([part] * 3)
    part, turn, bits_top = lax.optimization_barrier((part, at, bits_top))
    tiles = tiles_of(turn, trail_cov, row_count, bw)
    gram, norm_top = early(bits_top, panel_one_top, diag_inv_two, diag_inv_one)
    packed, tiles, norm_top, pieces = lax.optimization_barrier((packed, tiles, norm_top, pieces))
    far = jnp.stack(pieces)
    held = [part, core.move(part, 1), far, core.move(far, 1)]
    units = lax.all_to_all(packed, BOTH, split_axis=0, concat_axis=0, tiled=True)
    units = units.reshape(total_count * capacity, 2 * bw)

    tiles, units = lax.optimization_barrier((tiles, units))
    tiles = lax.all_to_all(tiles, "col", split_axis=0, concat_axis=0, tiled=True)
    image_two, image_one, own_two, own_one, *codes = image(at, trail_cov, held, bw)
    far_x, far_y = codes[1], codes[4]
    near = [ring_x.move(codes[0], 1), ring_x.move(codes[2], 3)]
    near += [ring_y.move(codes[3], 1), ring_y.move(codes[5], 3)]
    image_two, image_one, near[0] = lax.optimization_barrier((image_two, image_one, near[0]))
    far = [ring_x.move(far_x, 2), ring_y.move(far_y, 2)]

    keep, give = sums(
        at, pattern_two, pattern_one, panel_two_rows, panel_one_rows, image_two, image_one,
        diag_inv_two, diag_inv_one, bw,
    )
    give, near, far, tiles = lax.optimization_barrier((give, near, far, tiles))
    got = core.move(give, 1)
    codes = [near[0], far[0], near[1], near[2], far[1], near[3]]
    mine, parts = fold_z(at, keep, got)
    parts = lax.all_to_all(
        parts, "row", split_axis=0, concat_axis=0, tiled=True,
        axis_index_groups=[[2 * z + c for z in range(4)] for c in range(2)],
    )
    own_two, *two, own_one, one_a, one_b, one_c = fold_image(at, own_two, own_one, codes)
    codes = ring_y.others(two) + ring_x.others([one_a, one_b, one_c])
    mine, *parts = fold_x(at, mine, parts)
    total = mine
    for part in ring_x.others(parts):
        total = total + part
    total = fold_y(at, [total, *ring_y.others([total] * 3)])
    cov_two, cov_one, cross, tile = rows(
        at, pattern_two, pattern_one, block_panel, own_two, own_one, codes, tiles, norm_top, bw
    )
    value = forms(units, tile, cross)[0].reshape(total_count, capacity)
    total, value = lax.optimization_barrier((total, value))
    parts = [total, *ring_x.others([total] * 3)]
    total = unfold(at, parts)
    whole = jnp.stack([total, *ring_z.others([total] * 3)])
    whole = [whole, core.move(whole, 1)]
    returned = lax.all_to_all(value, BOTH, split_axis=0, concat_axis=0, tiled=True)
    diag_two, top_cov, diag_one = small(at, whole, gram, norm_top, bits_top)
    own_panel = jnp.sum(hits * block_panel[None, :], axis=1, keepdims=True)
    within = inner(loadings, own_panel, diag_one)[0]
    within, returned = lax.optimization_barrier((within, returned))
    picked = jnp.dot(
        hits.astype(jnp.float32), returned, precision=lax.Precision.HIGHEST,
        preferred_element_type=jnp.float32,
    )
    at_rank = rank[:, None] == jnp.arange(capacity, dtype=jnp.int32)[None, :]
    variance = jnp.sum(jnp.where(at_rank, picked, 0.0), axis=1)
    variance = variance + within

    mean = exposure * jnp.exp(0.5 * variance)
    seen = counts.astype(jnp.float32)
    scale = shape_par + mean
    shape_grad = (
        lax.digamma(shape_par + seen)
        - lax.digamma(shape_par)
        + jnp.log(shape_par / scale)
        + (mean - seen) / scale
    )
    return (cov_two, top_cov, cov_one, diag_two, diag_one, shape_grad)


def solution(mesh):
    in_specs = (
        P("row", "col"),
        P("row", None),
        P(),
        P(),
        P("row", None),
        P(),
        P(),
        P(),
        P(("row", "col"), None),
        P(("row", "col"), None),
        P(),
        P(("row", "col")),
        P(("row", "col")),
        P(("row", "col")),
    )
    out_specs = (P(("row", "col"), None), P(), P(("row", "col"), None), P(), P(), P(("row", "col")))
    return jax.shard_map(local, mesh=mesh, in_specs=in_specs, out_specs=out_specs, check_vma=False)
```
